128 devices in a mesh: pool: 32 (over x, z, core), tp: 4 (over y).
Axes of the slice: x: 4, y: 4, z: 4, core: 2. Of those that a mesh axis runs over, the one named last changes fastest.
Arguments:
- tokens: bfloat16 [4096, 7168], P('pool', 'tp'), may hold values from -6 to 6
- down_weight: bfloat16 [7168, 576], P('tp'), may hold values from -0.0625 to 0.0625
- kv_gain: float32 [512], replicated, may hold values from 0.4 to 1.6
- queries: bfloat16 [4096, 128, 576], P('pool', 'tp'), may hold values from -151 to 151
- value_weight: bfloat16 [128, 512, 128], P('tp'), may hold values from -1 to 1
- pool: bfloat16 [2048, 64, 576], P('pool', 'tp'), may hold values from -4 to 4
- block_holder: int32 [32, 32], replicated, may hold values from 0 to 31, as said below
- block_slot: int32 [32, 32], replicated, may hold values from 0 to 63, as said below
- prefix_blocks: int32 [32], replicated, may hold values from 1 to 30, as said below
- suffix_len: int32 [32], replicated, may hold values from 1 to 128, 3072 in all
Outputs:
- attn_out: bfloat16 [4096, 16384], P('pool', 'tp')
- new_pool: bfloat16 [2048, 64, 576], P('pool', 'tp')
The draws below stay inside these ranges and needn't reach their ends.
Inputs may be any that keep to these rules, and one draw needn't show every extreme that they name: `block_holder`: table entries 2 * k to 2 * k + 1 of a request name one holder, and different such groups of one request name different holders, so at most 2 blocks of one request sit on one holder. `block_slot`: no two table entries name the same holder and slot. `prefix_blocks`: some request has 30 prefix blocks.
All inputs are finite; a program needn't handle non-finite values.
Results may differ from the reference program's by a relative error of at most 0.0063.
Values may be sent and summed in bfloat16 or wider, within the bound.
A program may use at most 128 MiB of HBM per device.

```python
import math
from functools import partial
import jax
import jax.numpy as jnp
import numpy as np
from jax import lax

D = 7168
HEADS = 128
LATENT = 512
VALUE_DIM = 128
BLOCK = 64
SUFFIX = 128
TABLE = 32
LATENT_ROW_WIDTH = 576
PREFIX_SPAN = 30
REQUESTS = 32
TOKENS = 4096
CAP = 2
SLOTS = 64
POOL_BLOCKS = 2048


def permute_rows(key, rows, count):
    keys = jax.random.split(key, rows)
    return jax.vmap(partial(jax.random.permutation, x=count))(keys)


def prefix_counts(key):
    upper = jax.random.randint(jax.random.fold_in(key, 404), (REQUESTS,), 1, PREFIX_SPAN + 1)
    spread = jax.random.randint(jax.random.fold_in(key, 405), (REQUESTS,), 0, 1 << 20)
    counts = 1 + spread % upper
    fullest = jax.random.randint(jax.random.fold_in(key, 406), (), 0, REQUESTS)
    counts = jnp.where(jnp.arange(REQUESTS) == fullest, PREFIX_SPAN, counts)
    return counts.astype(jnp.int32)


def layout(key):
    counts = prefix_counts(key)
    orders = permute_rows(jax.random.fold_in(key, 101), REQUESTS, REQUESTS)
    request_ids = jnp.arange(REQUESTS)
    neighbour = (request_ids + 1) % REQUESTS
    flags = jax.random.randint(jax.random.fold_in(key, 407), (REQUESTS,), 0, 2)
    forced = (flags == 1) | (request_ids == 0)
    group_here = counts // CAP
    columns = jnp.arange(REQUESTS)[None, :]
    where_neighbour = jnp.sum(jnp.where(orders == neighbour[:, None], columns, 0), axis=1)
    current = jnp.sum(jnp.where(columns == group_here[:, None], orders, 0), axis=1)
    swapped = jnp.where(columns == group_here[:, None], neighbour[:, None], jnp.where(columns == where_neighbour[:, None], current[:, None], orders))
    orders = jnp.where(forced[:, None], swapped, orders)
    groups = jnp.arange(TABLE) // CAP
    holder = orders[:, groups]
    shuffles = permute_rows(jax.random.fold_in(key, 202), REQUESTS, SLOTS)
    local = jnp.arange(REQUESTS)[:, None] * CAP + (jnp.arange(TABLE) % CAP)[None, :]
    slot = shuffles[holder, local]
    return (holder.astype(jnp.int32), slot.astype(jnp.int32), counts)


def pool_values(key):
    value_rows = jax.random.normal(jax.random.fold_in(key, 303), (POOL_BLOCKS, BLOCK, LATENT_ROW_WIDTH), jnp.float32)
    return jnp.clip(value_rows, -4.0, 4.0)


def draw_block_holder(key, part):
    holder, slot, counts = layout(key)
    return holder


def draw_block_slot(key, part):
    holder, slot, counts = layout(key)
    return slot


def draw_prefix_blocks(key, part):
    holder, slot, counts = layout(key)
    return counts


def draw_pool(key, part):
    value_rows = pool_values(key)
    return value_rows.astype(jnp.bfloat16)


def draw_queries(key, part):
    key = jax.random.fold_in(key, 5)
    base = jax.random.normal(key, (TOKENS, HEADS, LATENT_ROW_WIDTH), jnp.float32) * 1.15
    return base.astype(jnp.bfloat16)


def steps_of(key, dims, shards, least, high):
    loudness, own = 1.0, jax.random.fold_in(key, 6)
    for dim, parts in shards:
        draws = jnp.exp(jax.random.uniform(jax.random.fold_in(own, dim), (parts,), jnp.float32, least / len(shards), high / len(shards)))
        loudness = loudness * jnp.repeat(draws, dims[dim] // parts).reshape([-1 if axis == dim else 1 for axis in range(len(dims))])
    return loudness


def length_profile(count, total, bound, slope):
    weights = [(1 << 20) // math.isqrt(rank ** slope) + 1 for rank in range(2, count + 1)]
    spare, given = total - bound - (count - 1), [1] * (count - 1)
    while spare > 0:
        movable = [i for i in range(count - 1) if given[i] < bound]
        whole, budget = sum([weights[i] for i in movable]), spare
        for i in movable:
            addition = min(bound - given[i], max(1, budget * weights[i] // whole), spare)
            given[i] = given[i] + addition
            spare = spare - addition
    return np.array([bound] + given)


def uneven_parts(stream_key, number_of, total, bound, skew):
    if number_of == 2:
        one = jax.random.randint(stream_key, (), max(1, total - bound), min(bound, total - 1) + 1)
        return jnp.stack([one, total - one])
    tallies = jnp.asarray(length_profile(number_of, total, bound, skew), jnp.int32)
    twos = (number_of - 1) // 2
    giver, sink = tallies[1:1 + 2 * twos:2], tallies[2:2 + 2 * twos:2]
    room = jnp.minimum(giver - 1, bound - sink)
    passed = jax.random.randint(jax.random.fold_in(stream_key, 1), (twos,), 0, 1 << 20) % (room + 1)
    tallies = tallies.at[1:1 + 2 * twos:2].set(giver - passed).at[2:2 + 2 * twos:2].set(sink + passed)
    return tallies[jax.random.permutation(jax.random.fold_in(stream_key, 2), number_of)]


def bell_draw(own_key, shape, scale, bound, cuts=(), held_as=jnp.bfloat16):
    values = scale * jax.random.normal(own_key, shape, jnp.float32)
    if cuts:
        values = values * steps_of(own_key, shape, cuts, -0.22, 0.18)
    return jnp.clip(values, -bound, bound).astype(held_as)


def setup_inputs(seed: int = 0) -> dict:
    key_list = jax.random.split(jax.random.key(seed), 11)
    return {
        "tokens": bell_draw(key_list[0], (TOKENS, D), 1.0, 6.0, ((0, 32), (1, 4))),
        "down_weight": bell_draw(key_list[1], (D, LATENT_ROW_WIDTH), D ** -0.5, 0.0625, ((0, 4),)),
        "kv_gain": jnp.clip(1.0 + 0.12 * jax.random.normal(key_list[2], (LATENT,), jnp.float32), 0.4, 1.6),
        "queries": draw_queries(jax.random.fold_in(key_list[10], 71), 0),
        "value_weight": bell_draw(key_list[4], (HEADS, LATENT, VALUE_DIM), (LATENT // 16) ** -0.5, 1.0, ((0, 4),)),
        "pool": draw_pool(jax.random.fold_in(key_list[10], 71), 0),
        "block_holder": draw_block_holder(jax.random.fold_in(key_list[10], 71), 0),
        "block_slot": draw_block_slot(jax.random.fold_in(key_list[10], 71), 0),
        "prefix_blocks": draw_prefix_blocks(jax.random.fold_in(key_list[10], 71), 0),
        "suffix_len": uneven_parts(key_list[9], REQUESTS, REQUESTS * SUFFIX * 3 // 4, SUFFIX, 1).astype(jnp.int32),
    }


logit_scale_factor = 192.0 ** (-0.5)
rope_base = 10000.0
epsilon = 1e-06

def make_keys(latent, positions, kv_gain, live):
    width = kv_gain.shape[0]
    content = latent[:, :width]
    rotary = latent[:, width:]
    inverse = lax.rsqrt(lax.optimization_barrier(jnp.mean(content * content, axis=1, keepdims=True)) + epsilon)
    normed = content * inverse * kv_gain[None, :]
    half_width = rotary.shape[1] // 2
    exponent = jnp.arange(half_width).astype(jnp.float32) * (2.0 / rotary.shape[1])
    angles = positions[:, None] * (rope_base ** (-exponent))[None, :]
    cosine_part = jnp.cos(angles)
    sine_part = jnp.sin(angles)
    first_half = rotary[:, :half_width]
    second_half = rotary[:, half_width:]
    turned = jnp.concatenate([first_half * cosine_part - second_half * sine_part, first_half * sine_part + second_half * cosine_part], axis=1)
    joined = jnp.concatenate([normed, turned], axis=1)
    return jnp.where(live[:, None], joined, 0.0).astype(jnp.bfloat16)

def reference(tokens, down_weight, kv_gain, queries, value_weight, pool, block_holder, block_slot, prefix_blocks, suffix_len):
    new_count = SUFFIX // BLOCK
    prefix_span = TABLE - new_count
    token_rows = tokens.reshape(REQUESTS, SUFFIX, D)
    query_rows = queries.reshape(REQUESTS, SUFFIX, HEADS, LATENT_ROW_WIDTH)
    steps_index = jnp.arange(SUFFIX).astype(jnp.int32)
    key_index = jnp.arange(prefix_span * BLOCK + SUFFIX).astype(jnp.int32)

    def one_request(inputs):
        token_part, query_part, holder_row, slot_row, prefix_count, length = inputs
        latent = jnp.dot(token_part, down_weight, preferred_element_type=jnp.float32)
        positions = (prefix_count * BLOCK + steps_index).astype(jnp.float32)
        new_keys = make_keys(latent, positions, kv_gain, steps_index < length)
        blocks = holder_row[:prefix_span] * SLOTS + slot_row[:prefix_span]
        prefix_keys = jnp.take(pool, blocks, axis=0).reshape(prefix_span * BLOCK, LATENT_ROW_WIDTH)
        keys = jnp.concatenate([prefix_keys, new_keys], axis=0)
        visible = jnp.where(key_index[None, :] < prefix_span * BLOCK, (key_index < prefix_count * BLOCK)[None, :], key_index[None, :] - prefix_span * BLOCK <= steps_index[:, None])
        scores = jnp.einsum('shk,tk->hst', query_part.astype(jnp.float32), keys.astype(jnp.float32)) * logit_scale_factor
        scores = jnp.where(visible[None], scores, -jnp.inf)
        highest = lax.optimization_barrier(jnp.max(scores, axis=2, keepdims=True))
        exponent = jnp.exp(scores - highest)
        weights = (exponent / lax.optimization_barrier(jnp.sum(exponent, axis=2, keepdims=True))).astype(jnp.bfloat16)
        mixed_output = jnp.einsum('hst,tk->hsk', weights.astype(jnp.float32), keys[:, :LATENT].astype(jnp.float32)).astype(jnp.bfloat16)
        value_rows = jnp.einsum('tnu,tux->ntx', mixed_output.astype(jnp.float32), value_weight.astype(jnp.float32))
        value_rows = jnp.where((steps_index < length)[:, None, None], value_rows, 0.0).astype(jnp.bfloat16)
        return (value_rows.reshape(SUFFIX, HEADS * VALUE_DIM), new_keys)
    outputs, fresh = lax.map(one_request, (token_rows, query_rows, block_holder, block_slot, prefix_blocks, suffix_len))
    attn_out = outputs.reshape(TOKENS, HEADS * VALUE_DIM)
    places = prefix_blocks[:, None] + jnp.arange(new_count).astype(jnp.int32)[None, :]
    targets = jnp.take_along_axis(block_holder, places, axis=1) * SLOTS + jnp.take_along_axis(block_slot, places, axis=1)
    new_pool = pool.at[targets.reshape(-1)].set(fresh.reshape(REQUESTS * new_count, BLOCK, LATENT_ROW_WIDTH))
    return (attn_out, new_pool)
```

```python
import functools
import math

import jax
import jax.numpy as jnp
import numpy as np
from jax import lax
from jax.experimental import pallas as pl
from jax.experimental.pallas import tpu as pltpu
from jax.sharding import PartitionSpec as P

LATENT = 512
VALUE_DIM = 128
BLOCK = 64
SUFFIX = 128
TABLE = 32
WIDTH = 576
WIDE = 640
ROPE = WIDTH - LATENT
HALF = 256
ROWS = 256
SCALE = 192.0 ** (-0.5) * math.log2(math.e)
HIDDEN = -1e30
EPSILON = 1e-06
MESH = pl.DeviceIdType.MESH


def kernel(
    pool_count,
    tp_count,
    holder,
    slot,
    prefix,
    length,
    gain,
    frequency,
    tokens_h,
    down_h,
    queries_h,
    value_h,
    pool_h,
    out_h,
    new_pool_h,
    tokens_v,
    down_v,
    queries_raw,
    queries,
    value_v,
    pool_v,
    leaving,
    arrived_even,
    arrived_odd,
    partial_v,
    partial_in,
    fresh,
    fresh_in,
    own,
    near,
    far,
    acc,
    high,
    norm,
    out_v,
    new_pool_v,
    index_v,
    index_s,
    load_sem,
    index_sem,
    block_send,
    block_recv,
    sum_send,
    sum_recv,
    fresh_send,
    fresh_recv,
    near_send,
    near_recv,
    far_send,
    far_recv,
):
    me = lax.axis_index("pool")
    tp = lax.axis_index("tp")
    core, z, x = me % 2, (me // 2) % 4, me // 8
    ahead, behind = (tp + 1) % tp_count, (tp + tp_count - 1) % tp_count
    across = (tp + 2) % tp_count
    heads = value_v.shape[0]
    slots = pool_v.shape[0]
    piece = pool_v.shape[1]
    groups = TABLE // 2
    total_rows = queries.shape[0]
    arrived = (arrived_even, arrived_odd)

    def peer(step):
        to_core = (core + step % 2) % 2
        to_z = (z + (step // 2) % 4) % 4
        to_x = (x + step // 8) % 4
        return (to_x * 4 + to_z) * 2 + to_core

    loads = [
        pltpu.make_async_copy(pool_h, pool_v, load_sem.at[0]),
        pltpu.make_async_copy(tokens_h, tokens_v, load_sem.at[1]),
        pltpu.make_async_copy(down_h, down_v, load_sem.at[2]),
        pltpu.make_async_copy(queries_h, queries_raw, load_sem.at[3]),
        pltpu.make_async_copy(value_h, value_v, load_sem.at[4]),
    ]
    for load in loads:
        load.start()

    barrier = pltpu.get_barrier_semaphore()

    @pl.loop(1, pool_count)
    def _(step):
        pl.semaphore_signal(barrier, inc=1, device_id=(peer(step), tp), device_id_type=MESH)

    for step in range(1, tp_count):
        pl.semaphore_signal(
            barrier, inc=1, device_id=(me, (tp + step) % tp_count), device_id_type=MESH
        )
    pl.semaphore_wait(barrier, pool_count - 1 + tp_count - 1)

    loads[0].wait()

    def wanted(request):
        at = jnp.int32(0)
        for k in range(groups - 1):
            at = jnp.where(holder[request, 2 * k] == me, 2 * k, at)
        return at

    def send_blocks(parity):
        @pl.loop(1, pool_count)
        def _(step):
            request = peer(step)
            leaving[parity, request] = pool_v[slot[request, wanted(request) + parity]]
            pltpu.make_async_remote_copy(
                src_ref=leaving.at[parity, request],
                dst_ref=arrived[parity].at[me],
                send_sem=block_send.at[parity],
                recv_sem=block_recv.at[parity],
                device_id=(request, tp),
                device_id_type=MESH,
            ).start()

        arrived[parity][me] = pool_v[slot[me, wanted(me) + parity]]

    send_blocks(0)

    loads[1].wait()
    loads[2].wait()
    partial = jnp.dot(tokens_v[...], down_v[...], preferred_element_type=jnp.float32)
    for owner in range(tp_count):
        for b in range(2):
            partial_v[owner, b * piece : (b + 1) * piece, :] = partial[
                b * BLOCK + owner * piece : b * BLOCK + (owner + 1) * piece, :
            ]
    sums = []
    for step in range(1, tp_count):
        to = (tp + step) % tp_count
        copy = pltpu.make_async_remote_copy(
            src_ref=partial_v.at[to],
            dst_ref=partial_in.at[step - 1],
            send_sem=sum_send.at[step - 1],
            recv_sem=sum_recv.at[step - 1],
            device_id=(me, to),
            device_id_type=MESH,
        )
        copy.start()
        sums.append(copy)

    send_blocks(1)

    loads[3].wait()
    lane64 = lax.broadcasted_iota(jnp.int32, (ROWS, WIDE - WIDTH), 1)
    one_mark = jnp.where(lane64 == 0, 1.0, 0.0).astype(jnp.bfloat16)

    @pl.loop(0, total_rows // ROWS)
    def _(i):
        rows = pl.ds(pl.multiple_of(i * ROWS, ROWS), ROWS)
        queries[rows, :LATENT] = queries_raw[rows, :LATENT]
        queries[rows, LATENT:] = jnp.concatenate([queries_raw[rows, LATENT:], one_mark], axis=1)

    for copy in sums:
        copy.wait_recv()
    latent = partial_v[tp] + partial_in[0] + partial_in[1] + partial_in[2]
    content = latent[:, :LATENT]
    rotary = latent[:, LATENT:]
    inverse = lax.rsqrt(jnp.mean(content * content, axis=1, keepdims=True) + EPSILON)
    normed = content * inverse * gain[...]
    row = lax.broadcasted_iota(jnp.int32, (2 * piece, ROPE), 0)
    lane = lax.broadcasted_iota(jnp.int32, (2 * piece, ROPE), 1)
    token = (row // piece) * BLOCK + tp * piece + row % piece
    angles = (prefix[me] * BLOCK + token).astype(jnp.float32) * frequency[...]
    turned_by = jnp.concatenate([rotary[:, ROPE // 2 :], rotary[:, : ROPE // 2]], axis=1)
    sine = jnp.where(lane < ROPE // 2, -1.0, 1.0) * jnp.sin(angles)
    turned = rotary * jnp.cos(angles) + turned_by * sine
    row512 = lax.broadcasted_iota(jnp.int32, (2 * piece, LATENT), 0)
    token512 = (row512 // piece) * BLOCK + tp * piece + row512 % piece
    normed = jnp.where(token512 < length[me], normed, 0.0).astype(jnp.bfloat16)
    turned = jnp.where(token < length[me], turned, 0.0)
    plain = jnp.zeros((piece, WIDE - WIDTH), jnp.float32)
    for b in range(2):
        rows = slice(b * piece, (b + 1) * piece)
        last = jnp.concatenate([turned[rows], plain], axis=1).astype(jnp.bfloat16)
        fresh[b, :, :LATENT] = normed[rows]
        fresh[b, :, LATENT:] = last[:, :ROPE]
        own[b, (groups - 1) * piece : groups * piece, :LATENT] = normed[rows]
        own[b, (groups - 1) * piece : groups * piece, LATENT:] = last

    @pl.loop(1, pool_count)
    def _(step):
        pltpu.make_async_remote_copy(
            src_ref=fresh,
            dst_ref=fresh_in.at[pl.ds(2 * me, 2)],
            send_sem=fresh_send,
            recv_sem=fresh_recv,
            device_id=(peer(step), tp),
            device_id_type=MESH,
        ).start()

    fresh_in[pl.ds(2 * me, 2)] = fresh[...]

    lane_mark = lax.broadcasted_iota(jnp.int32, (piece, WIDE - WIDTH), 1)

    def gather_blocks(parity):
        others = arrived[parity].at[pl.ds(0, pool_count - 1)]
        pltpu.make_async_copy(others, others, block_recv.at[parity]).wait()

        @pl.loop(0, groups - 1)
        def _(k):
            block = arrived[parity][holder[me, 2 * k + parity]]
            mark = jnp.where(2 * k + parity < prefix[me], 0.0, HIDDEN)
            marks = jnp.where(lane_mark == 0, mark, 0.0).astype(jnp.bfloat16)
            rows = pl.ds(pl.multiple_of(k * piece, piece), piece)
            own[parity, rows, :LATENT] = block[:, :LATENT]
            own[parity, rows, LATENT:] = jnp.concatenate([block[:, LATENT:], marks], axis=1)

        for side, to in enumerate((ahead, behind)):
            near_copy(parity, side, to).start()

    def near_copy(parity, side, to):
        return pltpu.make_async_remote_copy(
            src_ref=own.at[parity],
            dst_ref=near.at[parity, side],
            send_sem=near_send.at[parity, side],
            recv_sem=near_recv.at[parity, side],
            device_id=(me, to),
            device_id_type=MESH,
        )

    def far_copy(parity, side, to):
        rows = pl.ds(side * (HALF // 2), HALF // 2)
        return pltpu.make_async_remote_copy(
            src_ref=near.at[parity, side, rows],
            dst_ref=far.at[parity, rows],
            send_sem=far_send.at[parity, side],
            recv_sem=far_recv.at[parity, side],
            device_id=(me, to),
            device_id_type=MESH,
        )

    def forward(parity):
        for side, to in enumerate((ahead, behind)):
            near_copy(parity, side, to).wait_recv()
            far_copy(parity, side, to).start()

    row_token = lax.broadcasted_iota(jnp.int32, (ROWS, 128), 0) // heads
    lane128 = lax.broadcasted_iota(jnp.int32, (ROWS, 128), 1)

    def attend(halves, first=False, last=False):
        def scores_of(rows):
            query = queries[rows, :]
            return [
                lax.dot_general(
                    query, keys[...], (((1,), (1,)), ((), ())), preferred_element_type=jnp.float32
                )
                for keys, _ in halves
            ]

        def weigh(i, rows, scores):
            tiles = []
            for score, (_, base) in zip(scores, halves):
                tiles.append(score[:, :128])
                seen_from = jnp.where(lane128 >= 128 - piece, base + lane128 - (128 - piece), -1)
                hide = seen_from > row_token + i * (ROWS // heads)
                tiles.append(jnp.where(hide, HIDDEN, score[:, 128:]))
            top = functools.reduce(jnp.maximum, tiles)
            top = jnp.max(top, axis=1, keepdims=True) * SCALE
            if first:
                new_high = jnp.broadcast_to(top, (ROWS, 128))
            else:
                old_high = high[rows, :]
                new_high = jnp.maximum(old_high, top)
                decay = jnp.exp2(old_high - new_high)
            raised = [jnp.exp2(tile * SCALE - new_high) for tile in tiles]
            count = functools.reduce(jnp.add, raised)
            if not first:
                count = count + norm[rows, :] * decay
            mixed = None
            for j, (keys, _) in enumerate(halves):
                weights = jnp.concatenate(
                    [r.astype(jnp.bfloat16) for r in raised[2 * j : 2 * j + 2]], axis=1
                )
                term = jnp.dot(weights, keys[:, :LATENT], preferred_element_type=jnp.float32)
                mixed = term if mixed is None else mixed + term
            if last:
                share = 1.0 / jnp.sum(count, axis=1, keepdims=True)
            else:
                high[rows, :] = new_high
                norm[rows, :] = count
            for j in range(LATENT // 128):
                part = mixed[:, j * 128 : (j + 1) * 128]
                if not first:
                    part = part + acc[j, rows, :] * decay
                if last:
                    part = part * share
                acc[j, rows, :] = part

        @pl.loop(0, total_rows // ROWS // 2)
        def _(pair):
            tiles = [2 * pair, 2 * pair + 1]
            places = [pl.ds(pl.multiple_of(i * ROWS, ROWS), ROWS) for i in tiles]
            scores = [scores_of(rows) for rows in places]
            for i, rows, score in zip(tiles, places, scores):
                weigh(i, rows, score)

    gather_blocks(0)
    attend([(own.at[0], tp * piece)], first=True)
    gather_blocks(1)
    attend([(own.at[1], BLOCK + tp * piece)])
    for parity in range(2):
        forward(parity)
        attend(
            [
                (near.at[parity, 0], parity * BLOCK + behind * piece),
                (near.at[parity, 1], parity * BLOCK + ahead * piece),
            ]
        )

    lane_slot = lax.broadcasted_iota(jnp.int32, (8, 128), 1)

    def mark_slot(request, index):
        for b in range(2):
            entry = prefix[request] + b
            here = holder[request, entry] == me
            target = jnp.where(here, slot[request, entry], -1)
            index = jnp.where(lane_slot == target, 2 * request + b, index)
        return index

    index_v[...] = lax.fori_loop(0, pool_count, mark_slot, jnp.full((8, 128), -1, jnp.int32))
    to_scalars = pltpu.make_async_copy(index_v, index_s, index_sem)
    to_scalars.start()
    arrivals = fresh_in.at[pl.ds(0, 2 * (pool_count - 1))]
    pltpu.make_async_copy(arrivals, arrivals, fresh_recv).wait()
    to_scalars.wait()

    @pl.loop(0, slots)
    def _(place):
        at = index_s[0, place]
        replaced = jnp.where(at >= 0, 1.0, 0.0)
        kept = pool_v[place]
        taken = fresh_in[jnp.maximum(at, 0)]
        new_pool_v[place] = jnp.where(replaced > 0.5, taken, kept)

    store_pool = pltpu.make_async_copy(new_pool_v, new_pool_h, load_sem.at[0])
    store_pool.start()

    for parity in range(2):
        for side, to in enumerate((ahead, behind)):
            far_copy(parity, side, to).wait_recv()
    attend(
        [(far.at[parity], parity * BLOCK + across * piece) for parity in range(2)], last=True
    )

    loads[4].wait()
    live = lax.broadcasted_iota(jnp.int32, (SUFFIX, VALUE_DIM), 0) < length[me]

    @pl.loop(0, heads // 4)
    def _(quad):
        for inner in range(4):
            head = quad * 4 + inner
            mixed = jnp.concatenate(
                [
                    acc[j, pl.ds(head, SUFFIX, stride=heads), :].astype(jnp.bfloat16)
                    for j in range(LATENT // 128)
                ],
                axis=1,
            )
            value = jnp.dot(mixed, value_v[head], preferred_element_type=jnp.float32)
            columns = pl.ds(pl.multiple_of(head * VALUE_DIM, VALUE_DIM), VALUE_DIM)
            out_v[:, columns] = jnp.where(live, value, 0.0).astype(jnp.bfloat16)

    store_out = pltpu.make_async_copy(out_v, out_h, load_sem.at[1])
    store_out.start()

    for copy in sums:
        copy.wait_send()
    for parity in range(2):
        sent = leaving.at[parity, pl.ds(0, pool_count - 1)]
        pltpu.make_async_copy(sent, sent, block_send.at[parity]).wait()
        for side, to in enumerate((ahead, behind)):
            near_copy(parity, side, to).wait_send()
            far_copy(parity, side, to).wait_send()
    pltpu.make_async_copy(arrivals, arrivals, fresh_send).wait()
    store_pool.wait()
    store_out.wait()


def on_device(
    pool_count,
    tp_count,
    tokens,
    down_weight,
    kv_gain,
    queries,
    value_weight,
    pool,
    block_holder,
    block_slot,
    prefix_blocks,
    suffix_len,
):
    heads = queries.shape[1]
    rows = queries.shape[0] * heads
    slots, piece, width = pool.shape
    exponent = np.arange(ROPE // 2).astype(np.float32) * np.float32(2.0 / ROPE)
    inverse_frequency = np.power(np.float32(10000.0), -exponent).astype(np.float32)
    frequency = np.tile(inverse_frequency, 2)[None, :]
    bf16, f32 = jnp.bfloat16, jnp.float32
    smem = pl.BlockSpec(memory_space=pltpu.SMEM)
    vmem = pl.BlockSpec(memory_space=pltpu.VMEM)
    anywhere = pl.BlockSpec(memory_space=pl.ANY)
    dma = pltpu.SemaphoreType.DMA
    return pl.pallas_call(
        functools.partial(kernel, pool_count, tp_count),
        out_shape=(
            jax.ShapeDtypeStruct((SUFFIX, heads * VALUE_DIM), bf16),
            jax.ShapeDtypeStruct(pool.shape, bf16),
        ),
        in_specs=[smem] * 4 + [vmem] * 2 + [anywhere] * 5,
        out_specs=(anywhere, anywhere),
        scratch_shapes=[
            pltpu.VMEM(tokens.shape, bf16),
            pltpu.VMEM(down_weight.shape, bf16),
            pltpu.VMEM((rows, WIDTH), bf16),
            pltpu.VMEM((rows, WIDE), bf16),
            pltpu.VMEM(value_weight.shape, bf16),
            pltpu.VMEM(pool.shape, bf16),
            pltpu.VMEM((2, pool_count, piece, WIDTH), bf16),
            pltpu.VMEM((pool_count, piece, WIDTH), bf16),
            pltpu.VMEM((pool_count, piece, WIDTH), bf16),
            pltpu.VMEM((tp_count, 2 * piece, WIDTH), f32),
            pltpu.VMEM((tp_count - 1, 2 * piece, WIDTH), f32),
            pltpu.VMEM((2, piece, WIDTH), bf16),
            pltpu.VMEM((2 * pool_count, piece, WIDTH), bf16),
            pltpu.VMEM((2, HALF, WIDE), bf16),
            pltpu.VMEM((2, 2, HALF, WIDE), bf16),
            pltpu.VMEM((2, HALF, WIDE), bf16),
            pltpu.VMEM((LATENT // 128, rows, 128), f32),
            pltpu.VMEM((rows, 128), f32),
            pltpu.VMEM((rows, 128), f32),
            pltpu.VMEM((SUFFIX, heads * VALUE_DIM), bf16),
            pltpu.VMEM(pool.shape, bf16),
            pltpu.VMEM((8, 128), jnp.int32),
            pltpu.SMEM((8, 128), jnp.int32),
            dma((5,)),
            dma,
            dma((2,)),
            dma((2,)),
            dma((tp_count - 1,)),
            dma((tp_count - 1,)),
            dma,
            dma,
            dma((2, 2)),
            dma((2, 2)),
            dma((2, 2)),
            dma((2, 2)),
        ],
        compiler_params=pltpu.CompilerParams(
            collective_id=0, has_side_effects=True, vmem_limit_bytes=60 * 1024 * 1024
        ),
        name="latent_attention",
    )(
        block_holder,
        block_slot,
        prefix_blocks,
        suffix_len,
        kv_gain.reshape(1, LATENT),
        jnp.asarray(frequency),
        tokens,
        down_weight,
        queries.reshape(rows, WIDTH),
        value_weight,
        pool,
    )


def solution(mesh):
    in_specs = (
        P("pool", "tp"),
        P("tp", None),
        P(),
        P("pool", "tp", None),
        P("tp", None, None),
        P("pool", "tp", None),
        P(),
        P(),
        P(),
        P(),
    )
    out_specs = (P("pool", "tp"), P("pool", "tp", None))
    return jax.shard_map(
        functools.partial(on_device, mesh.shape["pool"], mesh.shape["tp"]),
        mesh=mesh,
        in_specs=in_specs,
        out_specs=out_specs,
        check_vma=False,
    )
```

```python
import functools
import math

import jax
import jax.numpy as jnp
import numpy as np
from jax import lax
from jax.experimental import pallas as pl
from jax.experimental.pallas import tpu as pltpu
from jax.sharding import PartitionSpec as P

LATENT = 512
VALUE_DIM = 128
BLOCK = 64
SUFFIX = 128
TABLE = 32
WIDTH = 576
WIDE = 640
ROPE = WIDTH - LATENT
HALF = 256
SCALE = 192.0 ** (-0.5) * math.log2(math.e)
HIDDEN = -1e30
EPSILON = 1e-06
MESH = pl.DeviceIdType.MESH


def kernel(
    pool_count,
    tp_count,
    holder,
    slot,
    prefix,
    length,
    gain,
    frequency,
    tokens_h,
    down_h,
    queries_h,
    value_h,
    pool_h,
    out_h,
    new_pool_h,
    tokens_v,
    down_v,
    queries,
    value_v,
    value_t,
    pool_v,
    leaving,
    arrived_even,
    arrived_odd,
    partial_v,
    partial_in,
    fresh,
    fresh_in,
    own,
    near,
    far,
    keys_t,
    acc,
    high,
    norm,
    out_v,
    new_pool_v,
    index_v,
    index_s,
    load_sem,
    index_sem,
    block_send,
    block_recv,
    sum_send,
    sum_recv,
    fresh_send,
    fresh_recv,
    near_send,
    near_recv,
    far_send,
    far_recv,
):
    me = lax.axis_index("pool")
    tp = lax.axis_index("tp")
    core, z, x = me % 2, (me // 2) % 4, me // 8
    ahead, behind = (tp + 1) % tp_count, (tp + tp_count - 1) % tp_count
    across = (tp + 2) % tp_count
    heads = queries.shape[0]
    slots = pool_v.shape[0]
    piece = pool_v.shape[1]
    groups = TABLE // 2
    arrived = (arrived_even, arrived_odd)

    def peer(step):
        to_core = (core + step % 2) % 2
        to_z = (z + (step // 2) % 4) % 4
        to_x = (x + step // 8) % 4
        return (to_x * 4 + to_z) * 2 + to_core

    loads = [
        pltpu.make_async_copy(pool_h, pool_v, load_sem.at[0]),
        pltpu.make_async_copy(tokens_h, tokens_v, load_sem.at[1]),
        pltpu.make_async_copy(down_h, down_v, load_sem.at[2]),
        pltpu.make_async_copy(queries_h, queries.at[:, pl.ds(0, WIDTH)], load_sem.at[3]),
        pltpu.make_async_copy(value_h, value_v, load_sem.at[4]),
    ]
    for load in loads:
        load.start()

    barrier = pltpu.get_barrier_semaphore()

    @pl.loop(1, pool_count)
    def _(step):
        pl.semaphore_signal(barrier, inc=1, device_id=(peer(step), tp), device_id_type=MESH)

    for step in range(1, tp_count):
        pl.semaphore_signal(
            barrier, inc=1, device_id=(me, (tp + step) % tp_count), device_id_type=MESH
        )
    pl.semaphore_wait(barrier, pool_count - 1 + tp_count - 1)

    loads[0].wait()

    def wanted(request):
        at = jnp.int32(0)
        for k in range(groups - 1):
            at = jnp.where(holder[request, 2 * k] == me, 2 * k, at)
        return at

    def send_blocks(parity):
        @pl.loop(1, pool_count)
        def _(step):
            request = peer(step)
            leaving[parity, request] = pool_v[slot[request, wanted(request) + parity]]
            pltpu.make_async_remote_copy(
                src_ref=leaving.at[parity, request],
                dst_ref=arrived[parity].at[me],
                send_sem=block_send.at[parity],
                recv_sem=block_recv.at[parity],
                device_id=(request, tp),
                device_id_type=MESH,
            ).start()

        arrived[parity][me] = pool_v[slot[me, wanted(me) + parity]]

    send_blocks(0)

    loads[1].wait()
    loads[2].wait()
    partial = lax.dot_general(
        tokens_v[...], down_v[...], (((1,), (1,)), ((), ())), preferred_element_type=jnp.float32
    )
    for owner in range(tp_count):
        for b in range(2):
            partial_v[owner, b * piece : (b + 1) * piece, :] = partial[
                b * BLOCK + owner * piece : b * BLOCK + (owner + 1) * piece, :
            ]
    sums = []
    for step in range(1, tp_count):
        to = (tp + step) % tp_count
        copy = pltpu.make_async_remote_copy(
            src_ref=partial_v.at[to],
            dst_ref=partial_in.at[step - 1],
            send_sem=sum_send.at[step - 1],
            recv_sem=sum_recv.at[step - 1],
            device_id=(me, to),
            device_id_type=MESH,
        )
        copy.start()
        sums.append(copy)

    send_blocks(1)

    mark_row = lax.broadcasted_iota(jnp.int32, (WIDE - WIDTH, SUFFIX), 0)
    one_mark = jnp.where(mark_row == 0, 1.0, 0.0).astype(jnp.bfloat16)

    @pl.loop(0, heads)
    def _(head):
        queries[head, WIDTH:, :] = one_mark

    for copy in sums:
        copy.wait_recv()
    latent = partial_v[tp] + partial_in[0] + partial_in[1] + partial_in[2]
    content = latent[:, :LATENT]
    rotary = latent[:, LATENT:]
    inverse = lax.rsqrt(jnp.mean(content * content, axis=1, keepdims=True) + EPSILON)
    normed = content * inverse * gain[...]
    row = lax.broadcasted_iota(jnp.int32, (2 * piece, ROPE), 0)
    lane = lax.broadcasted_iota(jnp.int32, (2 * piece, ROPE), 1)
    token = (row // piece) * BLOCK + tp * piece + row % piece
    angles = (prefix[me] * BLOCK + token).astype(jnp.float32) * frequency[...]
    turned_by = jnp.concatenate([rotary[:, ROPE // 2 :], rotary[:, : ROPE // 2]], axis=1)
    sine = jnp.where(lane < ROPE // 2, -1.0, 1.0) * jnp.sin(angles)
    turned = rotary * jnp.cos(angles) + turned_by * sine
    row512 = lax.broadcasted_iota(jnp.int32, (2 * piece, LATENT), 0)
    token512 = (row512 // piece) * BLOCK + tp * piece + row512 % piece
    normed = jnp.where(token512 < length[me], normed, 0.0).astype(jnp.bfloat16)
    turned = jnp.where(token < length[me], turned, 0.0)
    plain = jnp.zeros((piece, WIDE - WIDTH), jnp.float32)
    for b in range(2):
        rows = slice(b * piece, (b + 1) * piece)
        last = jnp.concatenate([turned[rows], plain], axis=1).astype(jnp.bfloat16)
        fresh[b, :, :LATENT] = normed[rows]
        fresh[b, :, LATENT:] = last[:, :ROPE]
        own[b, (groups - 1) * piece : groups * piece, :LATENT] = normed[rows]
        own[b, (groups - 1) * piece : groups * piece, LATENT:] = last

    @pl.loop(1, pool_count)
    def _(step):
        pltpu.make_async_remote_copy(
            src_ref=fresh,
            dst_ref=fresh_in.at[pl.ds(2 * me, 2)],
            send_sem=fresh_send,
            recv_sem=fresh_recv,
            device_id=(peer(step), tp),
            device_id_type=MESH,
        ).start()

    fresh_in[pl.ds(2 * me, 2)] = fresh[...]

    lane_mark = lax.broadcasted_iota(jnp.int32, (piece, WIDE - WIDTH), 1)

    def gather_blocks(parity):
        others = arrived[parity].at[pl.ds(0, pool_count - 1)]
        pltpu.make_async_copy(others, others, block_recv.at[parity]).wait()

        @pl.loop(0, groups - 1)
        def _(k):
            block = arrived[parity][holder[me, 2 * k + parity]]
            mark = jnp.where(2 * k + parity < prefix[me], 0.0, HIDDEN)
            marks = jnp.where(lane_mark == 0, mark, 0.0).astype(jnp.bfloat16)
            rows = pl.ds(pl.multiple_of(k * piece, piece), piece)
            own[parity, rows, :LATENT] = block[:, :LATENT]
            own[parity, rows, LATENT:] = jnp.concatenate([block[:, LATENT:], marks], axis=1)

        for side, to in enumerate((ahead, behind)):
            near_copy(parity, side, to).start()

    def near_copy(parity, side, to):
        return pltpu.make_async_remote_copy(
            src_ref=own.at[parity],
            dst_ref=near.at[parity, pl.ds(side * HALF, HALF)],
            send_sem=near_send.at[parity, side],
            recv_sem=near_recv.at[parity, side],
            device_id=(me, to),
            device_id_type=MESH,
        )

    def far_copy(parity, side, to):
        rows = HALF // 2
        return pltpu.make_async_remote_copy(
            src_ref=near.at[parity, pl.ds(side * (HALF + rows), rows)],
            dst_ref=far.at[pl.ds(parity * HALF + side * rows, rows)],
            send_sem=far_send.at[parity, side],
            recv_sem=far_recv.at[parity, side],
            device_id=(me, to),
            device_id_type=MESH,
        )

    def forward(parity):
        for side, to in enumerate((ahead, behind)):
            near_copy(parity, side, to).wait_recv()
            far_copy(parity, side, to).start()

    loads[3].wait()
    loads[4].wait()

    @pl.loop(0, heads)
    def _(head):
        value_t[head] = value_v[head].T

    new_row = lax.broadcasted_iota(jnp.int32, (piece, SUFFIX), 0)
    token_lane = lax.broadcasted_iota(jnp.int32, (piece, SUFFIX), 1)
    live = lax.broadcasted_iota(jnp.int32, (SUFFIX, VALUE_DIM), 0) < length[me]

    def attend(keys, bases, first=False, last=False):
        count = len(bases) * HALF
        for half in range(len(bases)):
            rows = slice(half * HALF, (half + 1) * HALF)
            keys_t[:, rows] = keys[rows, :LATENT].T
        hidden = [base + new_row > token_lane for base in bases]

        def scores_of(group):
            query = jnp.concatenate([queries[head] for head in group], axis=1)
            return jnp.dot(keys[...], query, preferred_element_type=jnp.float32)

        def weigh(group, scores):
            weights, decays, sums_of = [], [], []
            for j, head in enumerate(group):
                score = scores[:, j * SUFFIX : (j + 1) * SUFFIX]
                parts = []
                for half, hide in enumerate(hidden):
                    end = (half + 1) * HALF
                    parts.append(score[half * HALF : end - piece])
                    parts.append(jnp.where(hide, HIDDEN, score[end - piece : end]))
                score = jnp.concatenate(parts, axis=0).reshape(count // 8, 8, SUFFIX)
                top = jnp.max(jnp.max(score, axis=0), axis=0, keepdims=True) * SCALE
                top = jnp.broadcast_to(top, (8, SUFFIX))
                if not first:
                    old = high[head]
                    top = jnp.maximum(old, top)
                    decay = jnp.exp2(old - top)
                    decays.append(decay)
                raised = jnp.exp2(score * SCALE - top[None])
                total = jnp.sum(raised, axis=0)
                if not first:
                    total = total + norm[head] * decay
                if last:
                    total = 1.0 / jnp.sum(total, axis=0, keepdims=True)
                    sums_of.append(jnp.broadcast_to(total, (8, SUFFIX)))
                else:
                    high[head] = top
                    norm[head] = total
                weights.append(raised.reshape(count, SUFFIX).astype(jnp.bfloat16))
            mixed = jnp.dot(
                keys_t[:, :count],
                jnp.concatenate(weights, axis=1),
                preferred_element_type=jnp.float32,
            )
            for j, head in enumerate(group):
                part = mixed[:, j * SUFFIX : (j + 1) * SUFFIX].reshape(LATENT // 8, 8, SUFFIX)
                if not first:
                    part = part + acc[head].reshape(LATENT // 8, 8, SUFFIX) * decays[j][None]
                if last:
                    part = (part * sums_of[j][None]).reshape(LATENT, SUFFIX).astype(jnp.bfloat16)
                    value = jnp.dot(value_t[head], part, preferred_element_type=jnp.float32).T
                    columns = pl.ds(pl.multiple_of(head * VALUE_DIM, VALUE_DIM), VALUE_DIM)
                    out_v[:, columns] = jnp.where(live, value, 0.0).astype(jnp.bfloat16)
                else:
                    acc[head] = part.reshape(LATENT, SUFFIX)

        @pl.loop(0, heads // 4)
        def _(quad):
            groups_of = [[4 * quad + 2 * j, 4 * quad + 2 * j + 1] for j in range(2)]
            scores = [scores_of(group) for group in groups_of]
            for group, score in zip(groups_of, scores):
                weigh(group, score)

    gather_blocks(0)
    attend(own.at[0], [tp * piece], first=True)
    gather_blocks(1)
    attend(own.at[1], [BLOCK + tp * piece])
    for parity in range(2):
        forward(parity)
        attend(near.at[parity], [parity * BLOCK + side * piece for side in (behind, ahead)])

    lane_slot = lax.broadcasted_iota(jnp.int32, (8, 128), 1)

    def mark_slot(request, index):
        for b in range(2):
            entry = prefix[request] + b
            here = holder[request, entry] == me
            target = jnp.where(here, slot[request, entry], -1)
            index = jnp.where(lane_slot == target, 2 * request + b, index)
        return index

    index_v[...] = lax.fori_loop(0, pool_count, mark_slot, jnp.full((8, 128), -1, jnp.int32))
    to_scalars = pltpu.make_async_copy(index_v, index_s, index_sem)
    to_scalars.start()
    arrivals = fresh_in.at[pl.ds(0, 2 * (pool_count - 1))]
    pltpu.make_async_copy(arrivals, arrivals, fresh_recv).wait()
    to_scalars.wait()

    @pl.loop(0, slots)
    def _(place):
        at = index_s[0, place]
        replaced = jnp.where(at >= 0, 1.0, 0.0)
        kept = pool_v[place]
        taken = fresh_in[jnp.maximum(at, 0)]
        new_pool_v[place] = jnp.where(replaced > 0.5, taken, kept)

    store_pool = pltpu.make_async_copy(new_pool_v, new_pool_h, load_sem.at[0])
    store_pool.start()

    for parity in range(2):
        for side, to in enumerate((ahead, behind)):
            far_copy(parity, side, to).wait_recv()
    attend(far, [parity * BLOCK + across * piece for parity in range(2)], last=True)

    store_out = pltpu.make_async_copy(out_v, out_h, load_sem.at[1])
    store_out.start()

    for copy in sums:
        copy.wait_send()
    for parity in range(2):
        sent = leaving.at[parity, pl.ds(0, pool_count - 1)]
        pltpu.make_async_copy(sent, sent, block_send.at[parity]).wait()
        for side, to in enumerate((ahead, behind)):
            near_copy(parity, side, to).wait_send()
            far_copy(parity, side, to).wait_send()
    pltpu.make_async_copy(arrivals, arrivals, fresh_send).wait()
    store_pool.wait()
    store_out.wait()


def on_device(
    pool_count,
    tp_count,
    tokens,
    down_weight,
    kv_gain,
    queries,
    value_weight,
    pool,
    block_holder,
    block_slot,
    prefix_blocks,
    suffix_len,
):
    heads = queries.shape[1]
    piece = pool.shape[1]
    exponent = np.arange(ROPE // 2).astype(np.float32) * np.float32(2.0 / ROPE)
    inverse_frequency = np.power(np.float32(10000.0), -exponent).astype(np.float32)
    frequency = np.tile(inverse_frequency, 2)[None, :]
    bf16, f32 = jnp.bfloat16, jnp.float32
    smem = pl.BlockSpec(memory_space=pltpu.SMEM)
    vmem = pl.BlockSpec(memory_space=pltpu.VMEM)
    anywhere = pl.BlockSpec(memory_space=pl.ANY)
    dma = pltpu.SemaphoreType.DMA
    return pl.pallas_call(
        functools.partial(kernel, pool_count, tp_count),
        out_shape=(
            jax.ShapeDtypeStruct((SUFFIX, heads * VALUE_DIM), bf16),
            jax.ShapeDtypeStruct(pool.shape, bf16),
        ),
        in_specs=[smem] * 4 + [vmem] * 2 + [anywhere] * 5,
        out_specs=(anywhere, anywhere),
        scratch_shapes=[
            pltpu.VMEM(tokens.shape, bf16),
            pltpu.VMEM(down_weight.shape[::-1], bf16),
            pltpu.VMEM((heads, WIDE, SUFFIX), bf16),
            pltpu.VMEM(value_weight.shape, bf16),
            pltpu.VMEM((heads, VALUE_DIM, LATENT), bf16),
            pltpu.VMEM(pool.shape, bf16),
            pltpu.VMEM((2, pool_count, piece, WIDTH), bf16),
            pltpu.VMEM((pool_count, piece, WIDTH), bf16),
            pltpu.VMEM((pool_count, piece, WIDTH), bf16),
            pltpu.VMEM((tp_count, 2 * piece, WIDTH), f32),
            pltpu.VMEM((tp_count - 1, 2 * piece, WIDTH), f32),
            pltpu.VMEM((2, piece, WIDTH), bf16),
            pltpu.VMEM((2 * pool_count, piece, WIDTH), bf16),
            pltpu.VMEM((2, HALF, WIDE), bf16),
            pltpu.VMEM((2, 2 * HALF, WIDE), bf16),
            pltpu.VMEM((2 * HALF, WIDE), bf16),
            pltpu.VMEM((LATENT, 2 * HALF), bf16),
            pltpu.VMEM((heads, LATENT, SUFFIX), f32),
            pltpu.VMEM((heads, 8, SUFFIX), f32),
            pltpu.VMEM((heads, 8, SUFFIX), f32),
            pltpu.VMEM((SUFFIX, heads * VALUE_DIM), bf16),
            pltpu.VMEM(pool.shape, bf16),
            pltpu.VMEM((8, 128), jnp.int32),
            pltpu.SMEM((8, 128), jnp.int32),
            dma((5,)),
            dma,
            dma((2,)),
            dma((2,)),
            dma((tp_count - 1,)),
            dma((tp_count - 1,)),
            dma,
            dma,
            dma((2, 2)),
            dma((2, 2)),
            dma((2, 2)),
            dma((2, 2)),
        ],
        compiler_params=pltpu.CompilerParams(
            collective_id=0, has_side_effects=True, vmem_limit_bytes=60 * 1024 * 1024
        ),
        name="latent_attention",
    )(
        block_holder,
        block_slot,
        prefix_blocks,
        suffix_len,
        kv_gain.reshape(1, LATENT),
        jnp.asarray(frequency),
        tokens,
        down_weight.T,
        queries.transpose(1, 2, 0),
        value_weight,
        pool,
    )


def solution(mesh):
    in_specs = (
        P("pool", "tp"),
        P("tp", None),
        P(),
        P("pool", "tp", None),
        P("tp", None, None),
        P("pool", "tp", None),
        P(),
        P(),
        P(),
        P(),
    )
    out_specs = (P("pool", "tp"), P("pool", "tp", None))
    return jax.shard_map(
        functools.partial(on_device, mesh.shape["pool"], mesh.shape["tp"]),
        mesh=mesh,
        in_specs=in_specs,
        out_specs=out_specs,
        check_vma=False,
    )
```

```python
import functools
import math

import jax
import jax.numpy as jnp
import numpy as np
from jax import lax
from jax.experimental import pallas as pl
from jax.experimental.pallas import tpu as pltpu
from jax.sharding import PartitionSpec as P

LATENT = 512
VALUE_DIM = 128
BLOCK = 64
SUFFIX = 128
TABLE = 32
WIDTH = 576
WIDE = 640
ROPE = WIDTH - LATENT
HALF = 256
SCALE = 192.0 ** (-0.5) * math.log2(math.e)
HIDDEN = -1e30
EPSILON = 1e-06
MESH = pl.DeviceIdType.MESH


def kernel(
    pool_count,
    tp_count,
    holder,
    slot,
    prefix,
    length,
    gain,
    frequency,
    tokens_h,
    down_h,
    queries_h,
    value_h,
    pool_h,
    out_h,
    new_pool_h,
    tokens_v,
    down_v,
    queries,
    value_v,
    value_t,
    pool_v,
    leaving,
    arrived_even,
    arrived_odd,
    partial_v,
    partial_in,
    fresh_in,
    own,
    near,
    far,
    keys_t,
    acc,
    high,
    norm,
    out_v,
    new_pool_v,
    index_v,
    index_s,
    entry_s,
    load_sem,
    index_sem,
    block_send,
    block_recv,
    sum_send,
    sum_recv,
    fresh_send,
    fresh_recv,
    near_send,
    near_recv,
    far_send,
    far_recv,
):
    me = lax.axis_index("pool")
    tp = lax.axis_index("tp")
    core, z, x = me % 2, (me // 2) % 4, me // 8
    ahead, behind = (tp + 1) % tp_count, (tp + tp_count - 1) % tp_count
    across = (tp + 2) % tp_count
    heads = queries.shape[0]
    slots = pool_v.shape[0]
    piece = pool_v.shape[1]
    groups = TABLE // 2
    arrived = (arrived_even, arrived_odd)

    def peer(step):
        to_core = (core + step % 2) % 2
        to_z = (z + (step // 2) % 4) % 4
        to_x = (x + step // 8) % 4
        return (to_x * 4 + to_z) * 2 + to_core

    loads = [
        pltpu.make_async_copy(pool_h, pool_v, load_sem.at[0]),
        pltpu.make_async_copy(tokens_h, tokens_v, load_sem.at[1]),
        pltpu.make_async_copy(down_h, down_v, load_sem.at[2]),
        pltpu.make_async_copy(queries_h, queries.at[:, pl.ds(0, WIDTH)], load_sem.at[3]),
        pltpu.make_async_copy(value_h, value_v, load_sem.at[4]),
    ]
    for load in loads:
        load.start()

    barrier = pltpu.get_barrier_semaphore()

    @pl.loop(1, pool_count)
    def _(step):
        pl.semaphore_signal(barrier, inc=1, device_id=(peer(step), tp), device_id_type=MESH)

    for step in range(1, tp_count):
        pl.semaphore_signal(
            barrier, inc=1, device_id=(me, (tp + step) % tp_count), device_id_type=MESH
        )
    pl.semaphore_wait(barrier, pool_count - 1 + tp_count - 1)

    loads[0].wait()

    def wanted(request, parity):
        if parity == 0:
            at = jnp.int32(0)
            for k in range(groups - 1):
                at = jnp.where(holder[request, 2 * k] == me, 2 * k, at)
            entry_s[request] = at
        return slot[request, entry_s[request] + parity]

    def send_blocks(parity):
        @pl.loop(1, pool_count)
        def _(step):
            request = peer(step)
            leaving[parity, request] = pool_v[wanted(request, parity)]
            pltpu.make_async_remote_copy(
                src_ref=leaving.at[parity, request],
                dst_ref=arrived[parity].at[me],
                send_sem=block_send.at[parity],
                recv_sem=block_recv.at[parity],
                device_id=(request, tp),
                device_id_type=MESH,
            ).start()

        arrived[parity][me] = pool_v[wanted(me, parity)]

    send_blocks(0)

    loads[1].wait()
    loads[2].wait()
    partial = lax.dot_general(
        tokens_v[...], down_v[...], (((1,), (1,)), ((), ())), preferred_element_type=jnp.float32
    )
    for owner in range(tp_count):
        for b in range(2):
            partial_v[owner, b * piece : (b + 1) * piece, :] = partial[
                b * BLOCK + owner * piece : b * BLOCK + (owner + 1) * piece, :
            ]
    sums = []
    for step in range(1, tp_count):
        to = (tp + step) % tp_count
        copy = pltpu.make_async_remote_copy(
            src_ref=partial_v.at[to],
            dst_ref=partial_in.at[step - 1],
            send_sem=sum_send.at[step - 1],
            recv_sem=sum_recv.at[step - 1],
            device_id=(me, to),
            device_id_type=MESH,
        )
        copy.start()
        sums.append(copy)

    send_blocks(1)

    mark_row = lax.broadcasted_iota(jnp.int32, (WIDE - WIDTH, SUFFIX), 0)
    one_mark = jnp.where(mark_row == 0, 1.0, 0.0).astype(jnp.bfloat16)

    @pl.loop(0, heads)
    def _(head):
        queries[head, WIDTH:, :] = one_mark

    for copy in sums:
        copy.wait_recv()
    latent = partial_v[tp] + partial_in[0] + partial_in[1] + partial_in[2]
    content = latent[:, :LATENT]
    rotary = latent[:, LATENT:]
    inverse = lax.rsqrt(jnp.mean(content * content, axis=1, keepdims=True) + EPSILON)
    normed = content * inverse * gain[...]
    row = lax.broadcasted_iota(jnp.int32, (2 * piece, ROPE), 0)
    lane = lax.broadcasted_iota(jnp.int32, (2 * piece, ROPE), 1)
    token = (row // piece) * BLOCK + tp * piece + row % piece
    angles = (prefix[me] * BLOCK + token).astype(jnp.float32) * frequency[...]
    turned_by = jnp.concatenate([rotary[:, ROPE // 2 :], rotary[:, : ROPE // 2]], axis=1)
    sine = jnp.where(lane < ROPE // 2, -1.0, 1.0) * jnp.sin(angles)
    turned = rotary * jnp.cos(angles) + turned_by * sine
    row512 = lax.broadcasted_iota(jnp.int32, (2 * piece, LATENT), 0)
    token512 = (row512 // piece) * BLOCK + tp * piece + row512 % piece
    normed = jnp.where(token512 < length[me], normed, 0.0).astype(jnp.bfloat16)
    turned = jnp.where(token < length[me], turned, 0.0)
    fresh_at = 2 * ((core * 4 + z) * 4 + x)
    plain = jnp.zeros((piece, WIDE - WIDTH), jnp.float32)
    for b in range(2):
        rows = slice(b * piece, (b + 1) * piece)
        last = jnp.concatenate([turned[rows], plain], axis=1).astype(jnp.bfloat16)
        fresh_in[fresh_at + b, :, :LATENT] = normed[rows]
        fresh_in[fresh_at + b, :, LATENT:] = last[:, :ROPE]
        own[b, (groups - 1) * piece : groups * piece, :LATENT] = normed[rows]
        own[b, (groups - 1) * piece : groups * piece, LATENT:] = last

    def fresh_place(at_core, at_z, at_x):
        return 2 * ((at_core * 4 + at_z) * 4 + at_x)

    def along_x(step):
        here = fresh_in.at[pl.ds(fresh_place(core, z, x), 2)]
        to = (((x + step) % 4) * 4 + z) * 2 + core
        return pltpu.make_async_remote_copy(
            src_ref=here,
            dst_ref=here,
            send_sem=fresh_send.at[step - 1],
            recv_sem=fresh_recv.at[step - 1],
            device_id=(to, tp),
            device_id_type=MESH,
        )

    def along_z(step):
        here = fresh_in.at[pl.ds(fresh_place(core, z, 0), 8)]
        to = (x * 4 + (z + step) % 4) * 2 + core
        return pltpu.make_async_remote_copy(
            src_ref=here,
            dst_ref=here,
            send_sem=fresh_send.at[step + 2],
            recv_sem=fresh_recv.at[step + 2],
            device_id=(to, tp),
            device_id_type=MESH,
        )

    def to_other_core():
        here = fresh_in.at[pl.ds(fresh_place(core, 0, 0), 32)]
        return pltpu.make_async_remote_copy(
            src_ref=here,
            dst_ref=here,
            send_sem=fresh_send.at[6],
            recv_sem=fresh_recv.at[6],
            device_id=((x * 4 + z) * 2 + 1 - core, tp),
            device_id_type=MESH,
        )

    for step in range(1, 4):
        along_x(step).start()

    lane_mark = lax.broadcasted_iota(jnp.int32, (piece, WIDE - WIDTH), 1)

    def gather_blocks(parity):
        others = arrived[parity].at[pl.ds(0, pool_count - 1)]
        pltpu.make_async_copy(others, others, block_recv.at[parity]).wait()

        @pl.loop(0, groups - 1)
        def _(k):
            block = arrived[parity][holder[me, 2 * k + parity]]
            mark = jnp.where(2 * k + parity < prefix[me], 0.0, HIDDEN)
            marks = jnp.where(lane_mark == 0, mark, 0.0).astype(jnp.bfloat16)
            rows = pl.ds(pl.multiple_of(k * piece, piece), piece)
            own[parity, rows, :LATENT] = block[:, :LATENT]
            own[parity, rows, LATENT:] = jnp.concatenate([block[:, LATENT:], marks], axis=1)

        for side, to in enumerate((ahead, behind)):
            near_copy(parity, side, to).start()

    def near_copy(parity, side, to):
        return pltpu.make_async_remote_copy(
            src_ref=own.at[parity],
            dst_ref=near.at[parity, pl.ds(side * HALF, HALF)],
            send_sem=near_send.at[parity, side],
            recv_sem=near_recv.at[parity, side],
            device_id=(me, to),
            device_id_type=MESH,
        )

    def far_copy(parity, side, to):
        rows = HALF // 2
        return pltpu.make_async_remote_copy(
            src_ref=near.at[parity, pl.ds(side * (HALF + rows), rows)],
            dst_ref=far.at[pl.ds(parity * HALF + side * rows, rows)],
            send_sem=far_send.at[parity, side],
            recv_sem=far_recv.at[parity, side],
            device_id=(me, to),
            device_id_type=MESH,
        )

    def forward(parity):
        for side, to in enumerate((ahead, behind)):
            near_copy(parity, side, to).wait_recv()
            far_copy(parity, side, to).start()

    loads[3].wait()
    loads[4].wait()

    @pl.loop(0, heads)
    def _(head):
        value_t[head] = value_v[head].T

    new_row = lax.broadcasted_iota(jnp.int32, (piece, SUFFIX), 0)
    token_lane = lax.broadcasted_iota(jnp.int32, (piece, SUFFIX), 1)
    live = lax.broadcasted_iota(jnp.int32, (SUFFIX, VALUE_DIM), 0) < length[me]

    def attend(keys, bases, first=False, last=False):
        count = len(bases) * HALF
        for half in range(len(bases)):
            rows = slice(half * HALF, (half + 1) * HALF)
            keys_t[:, rows] = keys[rows, :LATENT].T
        hidden = [base + new_row > token_lane for base in bases]

        def scores_of(group):
            query = jnp.concatenate([queries[head] for head in group], axis=1)
            return jnp.dot(keys[...], query, preferred_element_type=jnp.float32)

        def weigh(group, scores):
            weights, decays, sums_of = [], [], []
            for j, head in enumerate(group):
                score = scores[:, j * SUFFIX : (j + 1) * SUFFIX]
                parts = []
                for half, hide in enumerate(hidden):
                    end = (half + 1) * HALF
                    parts.append(score[half * HALF : end - piece])
                    parts.append(jnp.where(hide, HIDDEN, score[end - piece : end]))
                score = jnp.concatenate(parts, axis=0).reshape(count // 8, 8, SUFFIX)
                top = jnp.max(jnp.max(score, axis=0), axis=0, keepdims=True) * SCALE
                top = jnp.broadcast_to(top, (8, SUFFIX))
                if not first:
                    old = high[head]
                    top = jnp.maximum(old, top)
                    decay = jnp.exp2(old - top)
                    decays.append(decay)
                raised = jnp.exp2(score * SCALE - top[None])
                total = jnp.sum(raised, axis=0)
                if not first:
                    total = total + norm[head] * decay
                if last:
                    total = 1.0 / jnp.sum(total, axis=0, keepdims=True)
                    sums_of.append(jnp.broadcast_to(total, (8, SUFFIX)))
                else:
                    high[head] = top
                    norm[head] = total
                weights.append(raised.reshape(count, SUFFIX).astype(jnp.bfloat16))
            mixed = jnp.dot(
                keys_t[:, :count],
                jnp.concatenate(weights, axis=1),
                preferred_element_type=jnp.float32,
            )
            for j, head in enumerate(group):
                part = mixed[:, j * SUFFIX : (j + 1) * SUFFIX].reshape(LATENT // 8, 8, SUFFIX)
                if not first:
                    part = part + acc[head].reshape(LATENT // 8, 8, SUFFIX) * decays[j][None]
                if last:
                    part = (part * sums_of[j][None]).reshape(LATENT, SUFFIX).astype(jnp.bfloat16)
                    value = jnp.dot(value_t[head], part, preferred_element_type=jnp.float32).T
                    columns = pl.ds(pl.multiple_of(head * VALUE_DIM, VALUE_DIM), VALUE_DIM)
                    out_v[:, columns] = jnp.where(live, value, 0.0).astype(jnp.bfloat16)
                else:
                    acc[head] = part.reshape(LATENT, SUFFIX)

        @pl.loop(0, heads // 4)
        def _(quad):
            groups_of = [[4 * quad + 2 * j, 4 * quad + 2 * j + 1] for j in range(2)]
            scores = [scores_of(group) for group in groups_of]
            for group, score in zip(groups_of, scores):
                weigh(group, score)

    gather_blocks(0)
    attend(own.at[0], [tp * piece], first=True)
    gather_blocks(1)
    attend(own.at[1], [BLOCK + tp * piece])
    for step in range(1, 4):
        along_x(step).wait_recv()
    for step in range(1, 4):
        along_z(step).start()
    for parity in range(2):
        forward(parity)
        attend(near.at[parity], [parity * BLOCK + side * piece for side in (behind, ahead)])

    for step in range(1, 4):
        along_z(step).wait_recv()
    to_other_core().start()

    for parity in range(2):
        for side, to in enumerate((ahead, behind)):
            far_copy(parity, side, to).wait_recv()
    attend(far, [parity * BLOCK + across * piece for parity in range(2)], last=True)

    store_out = pltpu.make_async_copy(out_v, out_h, load_sem.at[1])
    store_out.start()

    lane_slot = lax.broadcasted_iota(jnp.int32, (8, 128), 1)

    def mark_slot(request, index):
        for b in range(2):
            entry = prefix[request] + b
            here = holder[request, entry] == me
            target = jnp.where(here, slot[request, entry], -1)
            index = jnp.where(lane_slot == target, fresh_place(request % 2, (request // 2) % 4, request // 8) + b, index)
        return index

    index_v[...] = lax.fori_loop(0, pool_count, mark_slot, jnp.full((8, 128), -1, jnp.int32))
    to_scalars = pltpu.make_async_copy(index_v, index_s, index_sem)
    to_scalars.start()
    to_other_core().wait_recv()
    to_scalars.wait()

    @pl.loop(0, slots)
    def _(place):
        at = index_s[0, place]
        replaced = jnp.where(at >= 0, 1.0, 0.0)
        kept = pool_v[place]
        taken = fresh_in[jnp.maximum(at, 0)]
        new_pool_v[place] = jnp.where(replaced > 0.5, taken, kept)

    store_pool = pltpu.make_async_copy(new_pool_v, new_pool_h, load_sem.at[0])
    store_pool.start()


    for copy in sums:
        copy.wait_send()
    for parity in range(2):
        sent = leaving.at[parity, pl.ds(0, pool_count - 1)]
        pltpu.make_async_copy(sent, sent, block_send.at[parity]).wait()
        for side, to in enumerate((ahead, behind)):
            near_copy(parity, side, to).wait_send()
            far_copy(parity, side, to).wait_send()
    for step in range(1, 4):
        along_x(step).wait_send()
        along_z(step).wait_send()
    to_other_core().wait_send()
    store_pool.wait()
    store_out.wait()


def on_device(
    pool_count,
    tp_count,
    tokens,
    down_weight,
    kv_gain,
    queries,
    value_weight,
    pool,
    block_holder,
    block_slot,
    prefix_blocks,
    suffix_len,
):
    heads = queries.shape[1]
    piece = pool.shape[1]
    exponent = np.arange(ROPE // 2).astype(np.float32) * np.float32(2.0 / ROPE)
    inverse_frequency = np.power(np.float32(10000.0), -exponent).astype(np.float32)
    frequency = np.tile(inverse_frequency, 2)[None, :]
    bf16, f32 = jnp.bfloat16, jnp.float32
    smem = pl.BlockSpec(memory_space=pltpu.SMEM)
    vmem = pl.BlockSpec(memory_space=pltpu.VMEM)
    anywhere = pl.BlockSpec(memory_space=pl.ANY)
    dma = pltpu.SemaphoreType.DMA
    return pl.pallas_call(
        functools.partial(kernel, pool_count, tp_count),
        out_shape=(
            jax.ShapeDtypeStruct((SUFFIX, heads * VALUE_DIM), bf16),
            jax.ShapeDtypeStruct(pool.shape, bf16),
        ),
        in_specs=[smem] * 4 + [vmem] * 2 + [anywhere] * 5,
        out_specs=(anywhere, anywhere),
        scratch_shapes=[
            pltpu.VMEM(tokens.shape, bf16),
            pltpu.VMEM(down_weight.shape[::-1], bf16),
            pltpu.VMEM((heads, WIDE, SUFFIX), bf16),
            pltpu.VMEM(value_weight.shape, bf16),
            pltpu.VMEM((heads, VALUE_DIM, LATENT), bf16),
            pltpu.VMEM(pool.shape, bf16),
            pltpu.VMEM((2, pool_count, piece, WIDTH), bf16),
            pltpu.VMEM((pool_count, piece, WIDTH), bf16),
            pltpu.VMEM((pool_count, piece, WIDTH), bf16),
            pltpu.VMEM((tp_count, 2 * piece, WIDTH), f32),
            pltpu.VMEM((tp_count - 1, 2 * piece, WIDTH), f32),
            pltpu.VMEM((2 * pool_count, piece, WIDTH), bf16),
            pltpu.VMEM((2, HALF, WIDE), bf16),
            pltpu.VMEM((2, 2 * HALF, WIDE), bf16),
            pltpu.VMEM((2 * HALF, WIDE), bf16),
            pltpu.VMEM((LATENT, 2 * HALF), bf16),
            pltpu.VMEM((heads, LATENT, SUFFIX), f32),
            pltpu.VMEM((heads, 8, SUFFIX), f32),
            pltpu.VMEM((heads, 8, SUFFIX), f32),
            pltpu.VMEM((SUFFIX, heads * VALUE_DIM), bf16),
            pltpu.VMEM(pool.shape, bf16),
            pltpu.VMEM((8, 128), jnp.int32),
            pltpu.SMEM((8, 128), jnp.int32),
            pltpu.SMEM((pool_count,), jnp.int32),
            dma((5,)),
            dma,
            dma((2,)),
            dma((2,)),
            dma((tp_count - 1,)),
            dma((tp_count - 1,)),
            dma((7,)),
            dma((7,)),
            dma((2, 2)),
            dma((2, 2)),
            dma((2, 2)),
            dma((2, 2)),
        ],
        compiler_params=pltpu.CompilerParams(
            collective_id=0, has_side_effects=True, vmem_limit_bytes=60 * 1024 * 1024
        ),
        name="latent_attention",
    )(
        block_holder,
        block_slot,
        prefix_blocks,
        suffix_len,
        kv_gain.reshape(1, LATENT),
        jnp.asarray(frequency),
        tokens,
        down_weight.T,
        queries.transpose(1, 2, 0),
        value_weight,
        pool,
    )


def solution(mesh):
    in_specs = (
        P("pool", "tp"),
        P("tp", None),
        P(),
        P("pool", "tp", None),
        P("tp", None, None),
        P("pool", "tp", None),
        P(),
        P(),
        P(),
        P(),
    )
    out_specs = (P("pool", "tp"), P("pool", "tp", None))
    return jax.shard_map(
        functools.partial(on_device, mesh.shape["pool"], mesh.shape["tp"]),
        mesh=mesh,
        in_specs=in_specs,
        out_specs=out_specs,
        check_vma=False,
    )
```

```python
import functools
import math

import jax
import jax.numpy as jnp
import numpy as np
from jax import lax
from jax.experimental import pallas as pl
from jax.experimental.pallas import tpu as pltpu
from jax.sharding import PartitionSpec as P

LATENT = 512
VALUE_DIM = 128
BLOCK = 64
SUFFIX = 128
TABLE = 32
WIDTH = 576
WIDE = 640
ROPE = WIDTH - LATENT
HALF = 256
SCALE = 192.0 ** (-0.5) * math.log2(math.e)
HIDDEN = -1e30
EPSILON = 1e-06
MESH = pl.DeviceIdType.MESH


def kernel(
    pool_count,
    tp_count,
    holder,
    slot,
    prefix,
    length,
    gain,
    frequency,
    tokens_h,
    down_h,
    pool_h,
    keys_h,
    new_pool_h,
    tokens_v,
    down_v,
    pool_v,
    leaving,
    arrived_even,
    arrived_odd,
    partial_v,
    partial_in,
    fresh_in,
    own,
    near,
    far,
    new_pool_v,
    index_v,
    index_s,
    entry_s,
    load_sem,
    index_sem,
    block_send,
    block_recv,
    sum_send,
    sum_recv,
    fresh_send,
    fresh_recv,
    near_send,
    near_recv,
    far_send,
    far_recv,
):
    me = lax.axis_index("pool")
    tp = lax.axis_index("tp")
    core, z, x = me % 2, (me // 2) % 4, me // 8
    ahead, behind = (tp + 1) % tp_count, (tp + tp_count - 1) % tp_count
    across = (tp + 2) % tp_count
    slots = pool_v.shape[0]
    piece = pool_v.shape[1]
    groups = TABLE // 2
    arrived = (arrived_even, arrived_odd)

    def peer(step):
        to_core = (core + step % 2) % 2
        to_z = (z + (step // 2) % 4) % 4
        to_x = (x + step // 8) % 4
        return (to_x * 4 + to_z) * 2 + to_core

    loads = [
        pltpu.make_async_copy(pool_h, pool_v, load_sem.at[0]),
        pltpu.make_async_copy(tokens_h, tokens_v, load_sem.at[1]),
        pltpu.make_async_copy(down_h, down_v, load_sem.at[2]),
    ]
    for load in loads:
        load.start()

    barrier = pltpu.get_barrier_semaphore()

    @pl.loop(1, pool_count)
    def _(step):
        pl.semaphore_signal(barrier, inc=1, device_id=(peer(step), tp), device_id_type=MESH)

    for step in range(1, tp_count):
        pl.semaphore_signal(
            barrier, inc=1, device_id=(me, (tp + step) % tp_count), device_id_type=MESH
        )
    pl.semaphore_wait(barrier, pool_count - 1 + tp_count - 1)

    loads[0].wait()

    def wanted(request, parity):
        if parity == 0:
            at = jnp.int32(0)
            for k in range(groups - 1):
                at = jnp.where(holder[request, 2 * k] == me, 2 * k, at)
            entry_s[request] = at
        return slot[request, entry_s[request] + parity]

    def send_blocks(parity):
        @pl.loop(1, pool_count)
        def _(step):
            request = peer(step)
            leaving[parity, request] = pool_v[wanted(request, parity)]
            pltpu.make_async_remote_copy(
                src_ref=leaving.at[parity, request],
                dst_ref=arrived[parity].at[me],
                send_sem=block_send.at[parity],
                recv_sem=block_recv.at[parity],
                device_id=(request, tp),
                device_id_type=MESH,
            ).start()

        arrived[parity][me] = pool_v[wanted(me, parity)]

    send_blocks(0)

    loads[1].wait()
    loads[2].wait()
    partial = lax.dot_general(
        tokens_v[...], down_v[...], (((1,), (1,)), ((), ())), preferred_element_type=jnp.float32
    )
    for owner in range(tp_count):
        for b in range(2):
            partial_v[owner, b * piece : (b + 1) * piece, :] = partial[
                b * BLOCK + owner * piece : b * BLOCK + (owner + 1) * piece, :
            ]
    sums = []
    for step in range(1, tp_count):
        to = (tp + step) % tp_count
        copy = pltpu.make_async_remote_copy(
            src_ref=partial_v.at[to],
            dst_ref=partial_in.at[step - 1],
            send_sem=sum_send.at[step - 1],
            recv_sem=sum_recv.at[step - 1],
            device_id=(me, to),
            device_id_type=MESH,
        )
        copy.start()
        sums.append(copy)

    send_blocks(1)

    for copy in sums:
        copy.wait_recv()
    latent = partial_v[tp] + partial_in[0] + partial_in[1] + partial_in[2]
    content = latent[:, :LATENT]
    rotary = latent[:, LATENT:]
    inverse = lax.rsqrt(jnp.mean(content * content, axis=1, keepdims=True) + EPSILON)
    normed = content * inverse * gain[...]
    row = lax.broadcasted_iota(jnp.int32, (2 * piece, ROPE), 0)
    lane = lax.broadcasted_iota(jnp.int32, (2 * piece, ROPE), 1)
    token = (row // piece) * BLOCK + tp * piece + row % piece
    angles = (prefix[me] * BLOCK + token).astype(jnp.float32) * frequency[...]
    turned_by = jnp.concatenate([rotary[:, ROPE // 2 :], rotary[:, : ROPE // 2]], axis=1)
    sine = jnp.where(lane < ROPE // 2, -1.0, 1.0) * jnp.sin(angles)
    turned = rotary * jnp.cos(angles) + turned_by * sine
    row512 = lax.broadcasted_iota(jnp.int32, (2 * piece, LATENT), 0)
    token512 = (row512 // piece) * BLOCK + tp * piece + row512 % piece
    normed = jnp.where(token512 < length[me], normed, 0.0).astype(jnp.bfloat16)
    turned = jnp.where(token < length[me], turned, 0.0)
    fresh_at = 2 * ((core * 4 + z) * 4 + x)
    lane_plain = lax.broadcasted_iota(jnp.int32, (piece, WIDE - WIDTH), 1)
    plain = jnp.where(lane_plain == 0, HIDDEN, 0.0)
    for b in range(2):
        rows = slice(b * piece, (b + 1) * piece)
        last = jnp.concatenate([turned[rows], plain], axis=1).astype(jnp.bfloat16)
        fresh_in[fresh_at + b, :, :LATENT] = normed[rows]
        fresh_in[fresh_at + b, :, LATENT:] = last[:, :ROPE]
        own[b, (groups - 1) * piece : groups * piece, :LATENT] = normed[rows]
        own[b, (groups - 1) * piece : groups * piece, LATENT:] = last

    def fresh_place(at_core, at_z, at_x):
        return 2 * ((at_core * 4 + at_z) * 4 + at_x)

    def along_x(step):
        here = fresh_in.at[pl.ds(fresh_place(core, z, x), 2)]
        to = (((x + step) % 4) * 4 + z) * 2 + core
        return pltpu.make_async_remote_copy(
            src_ref=here,
            dst_ref=here,
            send_sem=fresh_send.at[step - 1],
            recv_sem=fresh_recv.at[step - 1],
            device_id=(to, tp),
            device_id_type=MESH,
        )

    def along_z(step):
        here = fresh_in.at[pl.ds(fresh_place(core, z, 0), 8)]
        to = (x * 4 + (z + step) % 4) * 2 + core
        return pltpu.make_async_remote_copy(
            src_ref=here,
            dst_ref=here,
            send_sem=fresh_send.at[step + 2],
            recv_sem=fresh_recv.at[step + 2],
            device_id=(to, tp),
            device_id_type=MESH,
        )

    def to_other_core():
        here = fresh_in.at[pl.ds(fresh_place(core, 0, 0), 32)]
        return pltpu.make_async_remote_copy(
            src_ref=here,
            dst_ref=here,
            send_sem=fresh_send.at[6],
            recv_sem=fresh_recv.at[6],
            device_id=((x * 4 + z) * 2 + 1 - core, tp),
            device_id_type=MESH,
        )

    for step in range(1, 4):
        along_x(step).start()

    lane_mark = lax.broadcasted_iota(jnp.int32, (piece, WIDE - WIDTH), 1)

    def gather_blocks(parity):
        others = arrived[parity].at[pl.ds(0, pool_count - 1)]
        pltpu.make_async_copy(others, others, block_recv.at[parity]).wait()

        @pl.loop(0, groups - 1)
        def _(k):
            block = arrived[parity][holder[me, 2 * k + parity]]
            mark = jnp.where(2 * k + parity < prefix[me], 0.0, HIDDEN)
            marks = jnp.where(lane_mark == 0, mark, 0.0).astype(jnp.bfloat16)
            rows = pl.ds(pl.multiple_of(k * piece, piece), piece)
            own[parity, rows, :LATENT] = block[:, :LATENT]
            own[parity, rows, LATENT:] = jnp.concatenate([block[:, LATENT:], marks], axis=1)

        for side, to in enumerate((ahead, behind)):
            near_copy(parity, side, to).start()

    def near_copy(parity, side, to):
        return pltpu.make_async_remote_copy(
            src_ref=own.at[parity],
            dst_ref=near.at[parity, pl.ds(side * HALF, HALF)],
            send_sem=near_send.at[parity, side],
            recv_sem=near_recv.at[parity, side],
            device_id=(me, to),
            device_id_type=MESH,
        )

    def far_copy(parity, side, to):
        rows = HALF // 2
        return pltpu.make_async_remote_copy(
            src_ref=near.at[parity, pl.ds(side * (HALF + rows), rows)],
            dst_ref=far.at[parity, pl.ds(side * rows, rows)],
            send_sem=far_send.at[parity, side],
            recv_sem=far_recv.at[parity, side],
            device_id=(me, to),
            device_id_type=MESH,
        )

    def forward(parity):
        for side, to in enumerate((ahead, behind)):
            near_copy(parity, side, to).wait_recv()
            far_copy(parity, side, to).start()

    gather_blocks(0)
    gather_blocks(1)
    for step in range(1, 4):
        along_x(step).wait_recv()
    for step in range(1, 4):
        along_z(step).start()
    for parity in range(2):
        forward(parity)
    for step in range(1, 4):
        along_z(step).wait_recv()
    to_other_core().start()

    lane_slot = lax.broadcasted_iota(jnp.int32, (8, 128), 1)

    def mark_slot(request, index):
        for b in range(2):
            entry = prefix[request] + b
            here = holder[request, entry] == me
            target = jnp.where(here, slot[request, entry], -1)
            index = jnp.where(lane_slot == target, fresh_place(request % 2, (request // 2) % 4, request // 8) + b, index)
        return index

    index_v[...] = lax.fori_loop(0, pool_count, mark_slot, jnp.full((8, 128), -1, jnp.int32))
    to_scalars = pltpu.make_async_copy(index_v, index_s, index_sem)
    to_scalars.start()
    to_other_core().wait_recv()
    to_scalars.wait()

    @pl.loop(0, slots)
    def _(place):
        at = index_s[0, place]
        replaced = jnp.where(at >= 0, 1.0, 0.0)
        kept = pool_v[place]
        taken = fresh_in[jnp.maximum(at, 0)]
        new_pool_v[place] = jnp.where(replaced > 0.5, taken, kept)

    store_pool = pltpu.make_async_copy(new_pool_v, new_pool_h, load_sem.at[0])
    store_pool.start()

    store_keys = [pltpu.make_async_copy(own, keys_h.at[tp], load_sem.at[1])]
    for side, (to, source) in enumerate(((ahead, behind), (behind, ahead))):
        store_keys.append(
            pltpu.make_async_copy(
                near.at[:, pl.ds(side * HALF, HALF)], keys_h.at[source], load_sem.at[2 + side]
            )
        )
    for parity in range(2):
        for side, to in enumerate((ahead, behind)):
            far_copy(parity, side, to).wait_recv()
    store_keys.append(pltpu.make_async_copy(far, keys_h.at[across], load_sem.at[4]))
    for store in store_keys:
        store.start()


    for copy in sums:
        copy.wait_send()
    for parity in range(2):
        sent = leaving.at[parity, pl.ds(0, pool_count - 1)]
        pltpu.make_async_copy(sent, sent, block_send.at[parity]).wait()
        for side, to in enumerate((ahead, behind)):
            near_copy(parity, side, to).wait_send()
            far_copy(parity, side, to).wait_send()
    for step in range(1, 4):
        along_x(step).wait_send()
        along_z(step).wait_send()
    to_other_core().wait_send()
    store_pool.wait()
    for store in store_keys:
        store.wait()


def attention(prefix, length, keys, queries, values, out, keys_t, scores_v, acc):
    heads = queries.shape[0]
    pieces = keys.shape[0]
    piece = BLOCK // pieces
    span = 4 * piece
    chunk = 2 * pieces * span
    me = lax.axis_index("pool")
    fresh_count = 2 * BLOCK

    @pl.when(pl.program_id(0) == 0)
    def _():
        for c in range(HALF // span):
            rows = keys[:, :, c * span : (c + 1) * span, :LATENT].reshape(chunk, LATENT)
            keys_t[c] = rows.T
        rows = keys[:, :, HALF - piece :, :LATENT].reshape(fresh_count, LATENT)
        keys_t[HALF // span, :, :fresh_count] = rows.T

    mark_row = lax.broadcasted_iota(jnp.int32, (WIDE - WIDTH, 2 * SUFFIX), 0)
    one_mark = jnp.where(mark_row == 0, 1.0, 0.0).astype(jnp.bfloat16)
    pairs = [(j, j + 1) for j in range(0, heads, 2)]
    query = [jnp.concatenate([queries[a], queries[b]], axis=1) for a, b in pairs]

    def weigh(score, high, norm):
        count = score.shape[0]
        score = score.reshape(count // 8, 8, 2 * SUFFIX)
        top = jnp.max(jnp.max(score, axis=0), axis=0, keepdims=True) * SCALE
        top = jnp.broadcast_to(top, (8, 2 * SUFFIX))
        decay = None
        if high is not None:
            top = jnp.maximum(high, top)
            decay = jnp.exp2(high - top)
        raised = jnp.exp2(score * SCALE - top[None])
        total = jnp.sum(raised, axis=0)
        if norm is not None:
            total = total + norm * decay
        return raised.reshape(count, 2 * SUFFIX).astype(jnp.bfloat16), top, total, decay

    fresh_keys = keys[:, :, HALF - piece :, :].reshape(fresh_count, WIDE)[:, :WIDTH]
    row = lax.broadcasted_iota(jnp.int32, (fresh_count, 2 * SUFFIX), 0)
    lane = lax.broadcasted_iota(jnp.int32, (fresh_count, 2 * SUFFIX), 1) % SUFFIX
    token = (row // piece % 2) * BLOCK + (row // (2 * piece)) * piece + row % piece
    state = []
    for j in range(len(pairs)):
        score = jnp.dot(fresh_keys, query[j], preferred_element_type=jnp.float32)
        score = jnp.where(token > lane, HIDDEN, score)
        weights, top, total, _ = weigh(score, None, None)
        acc[j] = jnp.dot(
            keys_t[HALF // span, :, :fresh_count], weights, preferred_element_type=jnp.float32
        )
        state += [top, total]

    chunks = ((prefix[me] + 1) // 2 * piece + span - 1) // span
    wide = [jnp.concatenate([q, one_mark], axis=0) for q in query]

    def step(c, state):
        rows = pl.ds(pl.multiple_of(c * span, span), span)
        here = keys[:, :, rows, :].reshape(chunk, WIDE)
        for j in range(len(pairs)):
            scores_v[j] = jnp.dot(here, wide[j], preferred_element_type=jnp.float32)
        after = []
        for j in range(len(pairs)):
            weights, top, total, decay = weigh(scores_v[j], state[2 * j], state[2 * j + 1])
            mixed = jnp.dot(keys_t[c], weights, preferred_element_type=jnp.float32)
            old = acc[j].reshape(LATENT // 8, 8, 2 * SUFFIX) * decay[None]
            acc[j] = old.reshape(LATENT, 2 * SUFFIX) + mixed
            after += [top, total]
        return tuple(after)

    state = lax.fori_loop(0, chunks, step, tuple(state))

    live = lax.broadcasted_iota(jnp.int32, (SUFFIX, VALUE_DIM), 0) < length[me]
    for j, pair in enumerate(pairs):
        share = 1.0 / jnp.sum(state[2 * j + 1], axis=0, keepdims=True)
        mixed = (acc[j] * share).astype(jnp.bfloat16)
        for side, head in enumerate(pair):
            value = lax.dot_general(
                mixed[:, side * SUFFIX : (side + 1) * SUFFIX],
                values[head],
                (((0,), (0,)), ((), ())),
                preferred_element_type=jnp.float32,
            )
            out[:, head * VALUE_DIM : (head + 1) * VALUE_DIM] = jnp.where(live, value, 0.0).astype(
                jnp.bfloat16
            )


def on_device(
    pool_count,
    tp_count,
    tokens,
    down_weight,
    kv_gain,
    queries,
    value_weight,
    pool,
    block_holder,
    block_slot,
    prefix_blocks,
    suffix_len,
):
    heads = queries.shape[1]
    piece = pool.shape[1]
    exponent = np.arange(ROPE // 2).astype(np.float32) * np.float32(2.0 / ROPE)
    inverse_frequency = np.power(np.float32(10000.0), -exponent).astype(np.float32)
    frequency = np.tile(inverse_frequency, 2)[None, :]
    bf16, f32 = jnp.bfloat16, jnp.float32
    smem = pl.BlockSpec(memory_space=pltpu.SMEM)
    vmem = pl.BlockSpec(memory_space=pltpu.VMEM)
    anywhere = pl.BlockSpec(memory_space=pl.ANY)
    dma = pltpu.SemaphoreType.DMA
    keys, new_pool = pl.pallas_call(
        functools.partial(kernel, pool_count, tp_count),
        out_shape=(
            jax.ShapeDtypeStruct((tp_count, 2, HALF, WIDE), bf16),
            jax.ShapeDtypeStruct(pool.shape, bf16),
        ),
        in_specs=[smem] * 4 + [vmem] * 2 + [anywhere] * 3,
        out_specs=(anywhere, anywhere),
        scratch_shapes=[
            pltpu.VMEM(tokens.shape, bf16),
            pltpu.VMEM(down_weight.shape[::-1], bf16),
            pltpu.VMEM(pool.shape, bf16),
            pltpu.VMEM((2, pool_count, piece, WIDTH), bf16),
            pltpu.VMEM((pool_count, piece, WIDTH), bf16),
            pltpu.VMEM((pool_count, piece, WIDTH), bf16),
            pltpu.VMEM((tp_count, 2 * piece, WIDTH), f32),
            pltpu.VMEM((tp_count - 1, 2 * piece, WIDTH), f32),
            pltpu.VMEM((2 * pool_count, piece, WIDTH), bf16),
            pltpu.VMEM((2, HALF, WIDE), bf16),
            pltpu.VMEM((2, 2 * HALF, WIDE), bf16),
            pltpu.VMEM((2, HALF, WIDE), bf16),
            pltpu.VMEM(pool.shape, bf16),
            pltpu.VMEM((8, 128), jnp.int32),
            pltpu.SMEM((8, 128), jnp.int32),
            pltpu.SMEM((pool_count,), jnp.int32),
            dma((5,)),
            dma,
            dma((2,)),
            dma((2,)),
            dma((tp_count - 1,)),
            dma((tp_count - 1,)),
            dma((7,)),
            dma((7,)),
            dma((2, 2)),
            dma((2, 2)),
            dma((2, 2)),
            dma((2, 2)),
        ],
        compiler_params=pltpu.CompilerParams(
            collective_id=0, has_side_effects=True, vmem_limit_bytes=60 * 1024 * 1024
        ),
        name="move_blocks",
    )(
        block_holder,
        block_slot,
        prefix_blocks,
        suffix_len,
        kv_gain.reshape(1, LATENT),
        jnp.asarray(frequency),
        tokens,
        down_weight.T,
        pool,
    )
    group = 4
    spec = pltpu.PrefetchScalarGridSpec(
        num_scalar_prefetch=2,
        grid=(heads // group,),
        in_specs=[
            pl.BlockSpec((tp_count, 2, HALF, WIDE), lambda i, *_: (0, 0, 0, 0)),
            pl.BlockSpec((group, WIDTH, SUFFIX), lambda i, *_: (i, 0, 0)),
            pl.BlockSpec((group, LATENT, VALUE_DIM), lambda i, *_: (i, 0, 0)),
        ],
        out_specs=pl.BlockSpec((SUFFIX, group * VALUE_DIM), lambda i, *_: (0, i)),
        scratch_shapes=[
            pltpu.VMEM((5, LATENT, 2 * HALF), bf16),
            pltpu.VMEM((group // 2, 2 * HALF, 2 * SUFFIX), f32),
            pltpu.VMEM((group // 2, LATENT, 2 * SUFFIX), f32),
        ],
    )
    attn_out = pl.pallas_call(
        attention,
        out_shape=jax.ShapeDtypeStruct((SUFFIX, heads * VALUE_DIM), bf16),
        grid_spec=spec,
        compiler_params=pltpu.CompilerParams(vmem_limit_bytes=48 * 1024 * 1024),
        name="attend",
    )(prefix_blocks, suffix_len, keys, queries.transpose(1, 2, 0), value_weight)
    return attn_out, new_pool


def solution(mesh):
    in_specs = (
        P("pool", "tp"),
        P("tp", None),
        P(),
        P("pool", "tp", None),
        P("tp", None, None),
        P("pool", "tp", None),
        P(),
        P(),
        P(),
        P(),
    )
    out_specs = (P("pool", "tp"), P("pool", "tp", None))
    return jax.shard_map(
        functools.partial(on_device, mesh.shape["pool"], mesh.shape["tp"]),
        mesh=mesh,
        in_specs=in_specs,
        out_specs=out_specs,
        check_vma=False,
    )
```

```python
import functools

import jax
import jax.numpy as jnp
import numpy as np
from jax import lax
from jax.experimental import pallas as pl
from jax.experimental.pallas import tpu as pltpu
from jax.sharding import PartitionSpec as P

LATENT = 512
VALUE_DIM = 128
BLOCK = 64
SUFFIX = 128
TABLE = 32
WIDTH = 576
WIDE = 640
ROPE = WIDTH - LATENT
HALF = 256
SCALE = 192.0 ** (-0.5)
HIDDEN = -1e30
EPSILON = 1e-06
GROUP = 4
MESH = pl.DeviceIdType.MESH


def kernel(
    pool_count,
    tp_count,
    holder,
    slot,
    prefix,
    length,
    gain,
    frequency,
    tokens_h,
    down_h,
    queries_h,
    value_h,
    pool_h,
    out_h,
    new_pool_h,
    tokens_v,
    down_v,
    queries,
    value_v,
    value_t,
    pool_v,
    leaving,
    arrived_even,
    arrived_odd,
    partial_v,
    partial_in,
    fresh_in,
    own,
    near,
    far,
    keys_t,
    scores,
    weights,
    acc,
    high,
    norm,
    out_v,
    new_pool_v,
    index_v,
    index_s,
    entry_s,
    load_sem,
    index_sem,
    block_send,
    block_recv,
    sum_send,
    sum_recv,
    fresh_send,
    fresh_recv,
    near_send,
    near_recv,
    far_send,
    far_recv,
):
    me = lax.axis_index("pool")
    tp = lax.axis_index("tp")
    core, z, x = me % 2, (me // 2) % 4, me // 8
    ahead, behind = (tp + 1) % tp_count, (tp + tp_count - 1) % tp_count
    across = (tp + 2) % tp_count
    heads = queries.shape[0]
    slots = pool_v.shape[0]
    piece = pool_v.shape[1]
    groups = TABLE // 2
    arrived = (arrived_even, arrived_odd)

    def peer(step):
        to_core = (core + step % 2) % 2
        to_z = (z + (step // 2) % 4) % 4
        to_x = (x + step // 8) % 4
        return (to_x * 4 + to_z) * 2 + to_core

    loads = [
        pltpu.make_async_copy(pool_h, pool_v, load_sem.at[0]),
        pltpu.make_async_copy(tokens_h, tokens_v, load_sem.at[1]),
        pltpu.make_async_copy(down_h, down_v, load_sem.at[2]),
        pltpu.make_async_copy(queries_h, queries.at[:, pl.ds(0, WIDTH)], load_sem.at[3]),
        pltpu.make_async_copy(value_h, value_v, load_sem.at[4]),
    ]
    for load in loads:
        load.start()

    barrier = pltpu.get_barrier_semaphore()

    @pl.loop(1, pool_count)
    def _(step):
        pl.semaphore_signal(barrier, inc=1, device_id=(peer(step), tp), device_id_type=MESH)

    for step in range(1, tp_count):
        pl.semaphore_signal(
            barrier, inc=1, device_id=(me, (tp + step) % tp_count), device_id_type=MESH
        )
    pl.semaphore_wait(barrier, pool_count - 1 + tp_count - 1)

    loads[0].wait()

    def wanted(request, parity):
        if parity == 0:
            at = jnp.int32(0)
            for k in range(groups - 1):
                at = jnp.where(holder[request, 2 * k] == me, 2 * k, at)
            entry_s[request] = at
        return slot[request, entry_s[request] + parity]

    def send_blocks(parity):
        @pl.loop(1, pool_count)
        def _(step):
            request = peer(step)
            leaving[parity, request] = pool_v[wanted(request, parity)]
            pltpu.make_async_remote_copy(
                src_ref=leaving.at[parity, request],
                dst_ref=arrived[parity].at[me],
                send_sem=block_send.at[parity],
                recv_sem=block_recv.at[parity],
                device_id=(request, tp),
                device_id_type=MESH,
            ).start()

        arrived[parity][me] = pool_v[wanted(me, parity)]

    send_blocks(0)

    loads[1].wait()
    loads[2].wait()
    partial = lax.dot_general(
        tokens_v[...], down_v[...], (((1,), (1,)), ((), ())), preferred_element_type=jnp.float32
    )
    for owner in range(tp_count):
        for b in range(2):
            partial_v[owner, b * piece : (b + 1) * piece, :] = partial[
                b * BLOCK + owner * piece : b * BLOCK + (owner + 1) * piece, :
            ]
    sums = []
    for step in range(1, tp_count):
        to = (tp + step) % tp_count
        copy = pltpu.make_async_remote_copy(
            src_ref=partial_v.at[to],
            dst_ref=partial_in.at[step - 1],
            send_sem=sum_send.at[step - 1],
            recv_sem=sum_recv.at[step - 1],
            device_id=(me, to),
            device_id_type=MESH,
        )
        copy.start()
        sums.append(copy)

    mark_row = lax.broadcasted_iota(jnp.int32, (WIDE - WIDTH, SUFFIX), 0)
    one_mark = jnp.where(mark_row == 0, 1.0, 0.0).astype(jnp.bfloat16)

    @pl.loop(0, heads)
    def _(head):
        queries[head, WIDTH:, :] = one_mark

    for copy in sums:
        copy.wait_recv()
    latent = partial_v[tp] + partial_in[0] + partial_in[1] + partial_in[2]
    content = latent[:, :LATENT]
    rotary = latent[:, LATENT:]
    inverse = lax.rsqrt(jnp.mean(content * content, axis=1, keepdims=True) + EPSILON)
    normed = content * inverse * gain[...]
    row = lax.broadcasted_iota(jnp.int32, (2 * piece, ROPE), 0)
    lane = lax.broadcasted_iota(jnp.int32, (2 * piece, ROPE), 1)
    token = (row // piece) * BLOCK + tp * piece + row % piece
    angles = (prefix[me] * BLOCK + token).astype(jnp.float32) * frequency[...]
    turned_by = jnp.concatenate([rotary[:, ROPE // 2 :], rotary[:, : ROPE // 2]], axis=1)
    sine = jnp.where(lane < ROPE // 2, -1.0, 1.0) * jnp.sin(angles)
    turned = rotary * jnp.cos(angles) + turned_by * sine
    row512 = lax.broadcasted_iota(jnp.int32, (2 * piece, LATENT), 0)
    token512 = (row512 // piece) * BLOCK + tp * piece + row512 % piece
    normed = jnp.where(token512 < length[me], normed, 0.0).astype(jnp.bfloat16)
    turned = jnp.where(token < length[me], turned, 0.0)
    fresh_at = 2 * ((core * 4 + z) * 4 + x)
    plain = jnp.zeros((piece, WIDE - WIDTH), jnp.float32)
    for b in range(2):
        rows = slice(b * piece, (b + 1) * piece)
        last = jnp.concatenate([turned[rows], plain], axis=1).astype(jnp.bfloat16)
        fresh_in[fresh_at + b, :, :LATENT] = normed[rows]
        fresh_in[fresh_at + b, :, LATENT:] = last[:, :ROPE]
        own[b, (groups - 1) * piece : groups * piece, :LATENT] = normed[rows]
        own[b, (groups - 1) * piece : groups * piece, LATENT:] = last

    def fresh_place(at_core, at_z, at_x):
        return 2 * ((at_core * 4 + at_z) * 4 + at_x)

    def along_x(step):
        here = fresh_in.at[pl.ds(fresh_place(core, z, x), 2)]
        to = (((x + step) % 4) * 4 + z) * 2 + core
        return pltpu.make_async_remote_copy(
            src_ref=here,
            dst_ref=here,
            send_sem=fresh_send.at[step - 1],
            recv_sem=fresh_recv.at[step - 1],
            device_id=(to, tp),
            device_id_type=MESH,
        )

    def along_z(step):
        here = fresh_in.at[pl.ds(fresh_place(core, z, 0), 8)]
        to = (x * 4 + (z + step) % 4) * 2 + core
        return pltpu.make_async_remote_copy(
            src_ref=here,
            dst_ref=here,
            send_sem=fresh_send.at[step + 2],
            recv_sem=fresh_recv.at[step + 2],
            device_id=(to, tp),
            device_id_type=MESH,
        )

    def to_other_core():
        here = fresh_in.at[pl.ds(fresh_place(core, 0, 0), 32)]
        return pltpu.make_async_remote_copy(
            src_ref=here,
            dst_ref=here,
            send_sem=fresh_send.at[6],
            recv_sem=fresh_recv.at[6],
            device_id=((x * 4 + z) * 2 + 1 - core, tp),
            device_id_type=MESH,
        )

    for step in range(1, 4):
        along_x(step).start()

    lane_mark = lax.broadcasted_iota(jnp.int32, (piece, WIDE - WIDTH), 1)

    def gather_blocks(parity):
        others = arrived[parity].at[pl.ds(0, pool_count - 1)]
        pltpu.make_async_copy(others, others, block_recv.at[parity]).wait()
        if parity == 0:
            send_blocks(1)

        @pl.loop(0, groups - 1)
        def _(k):
            block = arrived[parity][holder[me, 2 * k + parity]]
            mark = jnp.where(2 * k + parity < prefix[me], 0.0, HIDDEN)
            marks = jnp.where(lane_mark == 0, mark, 0.0).astype(jnp.bfloat16)
            rows = pl.ds(pl.multiple_of(k * piece, piece), piece)
            own[parity, rows, :LATENT] = block[:, :LATENT]
            own[parity, rows, LATENT:] = jnp.concatenate([block[:, LATENT:], marks], axis=1)

        for side, to in enumerate((ahead, behind)):
            near_copy(parity, side, to).start()

    def near_copy(parity, side, to):
        return pltpu.make_async_remote_copy(
            src_ref=own.at[parity],
            dst_ref=near.at[parity, pl.ds(side * HALF, HALF)],
            send_sem=near_send.at[parity, side],
            recv_sem=near_recv.at[parity, side],
            device_id=(me, to),
            device_id_type=MESH,
        )

    def far_copy(parity, side, to):
        rows = HALF // 2
        return pltpu.make_async_remote_copy(
            src_ref=near.at[parity, pl.ds(side * (HALF + rows), rows)],
            dst_ref=far.at[pl.ds(parity * HALF + side * rows, rows)],
            send_sem=far_send.at[parity, side],
            recv_sem=far_recv.at[parity, side],
            device_id=(me, to),
            device_id_type=MESH,
        )

    def forward(parity):
        for side, to in enumerate((ahead, behind)):
            near_copy(parity, side, to).wait_recv()
            far_copy(parity, side, to).start()

    loads[3].wait()
    loads[4].wait()

    @pl.loop(0, heads)
    def _(head):
        value_t[head] = value_v[head].T

    new_row = lax.broadcasted_iota(jnp.int32, (piece, SUFFIX), 0)
    token_lane = lax.broadcasted_iota(jnp.int32, (piece, SUFFIX), 1)
    live = lax.broadcasted_iota(jnp.int32, (SUFFIX, VALUE_DIM), 0) < length[me]

    def attend(keys, bases, first=False, last=False):
        count = len(bases) * HALF
        for half in range(len(bases)):
            rows = slice(half * HALF, (half + 1) * HALF)
            keys_t[:, rows] = keys[rows, :LATENT].T
        hidden = [base + new_row > token_lane for base in bases]

        def score(group, place):
            query = jnp.concatenate([queries[GROUP * group + j] for j in range(GROUP)], axis=1)
            scores[place, :count] = jnp.dot(
                keys[...], query, preferred_element_type=jnp.float32
            )
            for half, hide in enumerate(hidden):
                rows = slice((half + 1) * HALF - piece, (half + 1) * HALF)
                for j in range(GROUP):
                    lanes = slice(j * SUFFIX, (j + 1) * SUFFIX)
                    scores[place, rows, lanes] = jnp.where(hide, HIDDEN, scores[place, rows, lanes])

        def weigh(group, place):
            decays, shares = [], []
            for j in range(GROUP):
                head = GROUP * group + j
                lanes = slice(j * SUFFIX, (j + 1) * SUFFIX)
                top = jnp.max(scores[place, :count, lanes].reshape(count // 8, 8, SUFFIX), axis=0)
                top = jnp.broadcast_to(jnp.max(top, axis=0, keepdims=True), (8, SUFFIX))
                if not first:
                    old = high[head]
                    top = jnp.maximum(old, top)
                    decay = jnp.exp((old - top) * SCALE)
                    decays.append(decay)
                total = None
                for row in range(0, count, 64):
                    part = scores[place, row : row + 64, lanes].reshape(8, 8, SUFFIX)
                    raised = jnp.exp((part - top[None]) * SCALE)
                    weights[place, row : row + 64, lanes] = raised.reshape(64, SUFFIX).astype(
                        jnp.bfloat16
                    )
                    raised = jnp.sum(raised, axis=0)
                    total = raised if total is None else total + raised
                if not first:
                    total = total + norm[head] * decay
                if last:
                    total = 1.0 / jnp.sum(total, axis=0, keepdims=True)
                    shares.append(jnp.broadcast_to(total, (8, SUFFIX)))
                else:
                    high[head] = top
                    norm[head] = total
            return decays, shares

        def mix(group, place, decays, shares):
            mixed = jnp.dot(
                keys_t[:, :count], weights[place, :count], preferred_element_type=jnp.float32
            )
            for j in range(GROUP):
                head = GROUP * group + j
                part = mixed[:, j * SUFFIX : (j + 1) * SUFFIX].reshape(LATENT // 8, 8, SUFFIX)
                if not first:
                    part = part + acc[head].reshape(LATENT // 8, 8, SUFFIX) * decays[j][None]
                if last:
                    part = (part * shares[j][None]).reshape(LATENT, SUFFIX).astype(jnp.bfloat16)
                    value = jnp.dot(value_t[head], part, preferred_element_type=jnp.float32).T
                    columns = pl.ds(pl.multiple_of(head * VALUE_DIM, VALUE_DIM), VALUE_DIM)
                    out_v[:, columns] = jnp.where(live, value, 0.0).astype(jnp.bfloat16)
                else:
                    acc[head] = part.reshape(LATENT, SUFFIX)

        def two_groups(group, more):
            score(group + 1, 1)
            mix(group, 0, *weigh(group, 0))
            if more:
                score(group + 2, 0)
            mix(group + 1, 1, *weigh(group + 1, 1))

        score(0, 0)

        @pl.loop(0, heads // GROUP // 2 - 1)
        def _(pair):
            two_groups(2 * pair, True)

        two_groups(heads // GROUP - 2, False)

    gather_blocks(0)
    attend(own.at[0], [tp * piece], first=True)
    gather_blocks(1)
    attend(own.at[1], [BLOCK + tp * piece])
    for step in range(1, 4):
        along_x(step).wait_recv()
    for step in range(1, 4):
        along_z(step).start()
    for parity in range(2):
        forward(parity)
        attend(near.at[parity], [parity * BLOCK + side * piece for side in (behind, ahead)])

    for step in range(1, 4):
        along_z(step).wait_recv()
    to_other_core().start()

    for parity in range(2):
        for side, to in enumerate((ahead, behind)):
            far_copy(parity, side, to).wait_recv()
    attend(far, [parity * BLOCK + across * piece for parity in range(2)], last=True)

    store_out = pltpu.make_async_copy(out_v, out_h, load_sem.at[1])
    store_out.start()

    lane_slot = lax.broadcasted_iota(jnp.int32, (8, 128), 1)

    def mark_slot(request, index):
        for b in range(2):
            entry = prefix[request] + b
            here = holder[request, entry] == me
            target = jnp.where(here, slot[request, entry], -1)
            index = jnp.where(lane_slot == target, fresh_place(request % 2, (request // 2) % 4, request // 8) + b, index)
        return index

    index_v[...] = lax.fori_loop(0, pool_count, mark_slot, jnp.full((8, 128), -1, jnp.int32))
    to_scalars = pltpu.make_async_copy(index_v, index_s, index_sem)
    to_scalars.start()
    to_other_core().wait_recv()
    to_scalars.wait()

    @pl.loop(0, slots)
    def _(place):
        at = index_s[0, place]
        replaced = jnp.where(at >= 0, 1.0, 0.0)
        kept = pool_v[place]
        taken = fresh_in[jnp.maximum(at, 0)]
        new_pool_v[place] = jnp.where(replaced > 0.5, taken, kept)

    store_pool = pltpu.make_async_copy(new_pool_v, new_pool_h, load_sem.at[0])
    store_pool.start()


    for copy in sums:
        copy.wait_send()
    for parity in range(2):
        sent = leaving.at[parity, pl.ds(0, pool_count - 1)]
        pltpu.make_async_copy(sent, sent, block_send.at[parity]).wait()
        for side, to in enumerate((ahead, behind)):
            near_copy(parity, side, to).wait_send()
            far_copy(parity, side, to).wait_send()
    for step in range(1, 4):
        along_x(step).wait_send()
        along_z(step).wait_send()
    to_other_core().wait_send()
    store_pool.wait()
    store_out.wait()


def on_device(
    pool_count,
    tp_count,
    tokens,
    down_weight,
    kv_gain,
    queries,
    value_weight,
    pool,
    block_holder,
    block_slot,
    prefix_blocks,
    suffix_len,
):
    heads = queries.shape[1]
    piece = pool.shape[1]
    exponent = np.arange(ROPE // 2).astype(np.float32) * np.float32(2.0 / ROPE)
    inverse_frequency = np.power(np.float32(10000.0), -exponent).astype(np.float32)
    frequency = np.tile(inverse_frequency, 2)[None, :]
    bf16, f32 = jnp.bfloat16, jnp.float32
    smem = pl.BlockSpec(memory_space=pltpu.SMEM)
    vmem = pl.BlockSpec(memory_space=pltpu.VMEM)
    anywhere = pl.BlockSpec(memory_space=pl.ANY)
    dma = pltpu.SemaphoreType.DMA
    return pl.pallas_call(
        functools.partial(kernel, pool_count, tp_count),
        out_shape=(
            jax.ShapeDtypeStruct((SUFFIX, heads * VALUE_DIM), bf16),
            jax.ShapeDtypeStruct(pool.shape, bf16),
        ),
        in_specs=[smem] * 4 + [vmem] * 2 + [anywhere] * 5,
        out_specs=(anywhere, anywhere),
        scratch_shapes=[
            pltpu.VMEM(tokens.shape, bf16),
            pltpu.VMEM(down_weight.shape[::-1], bf16),
            pltpu.VMEM((heads, WIDE, SUFFIX), bf16),
            pltpu.VMEM(value_weight.shape, bf16),
            pltpu.VMEM((heads, VALUE_DIM, LATENT), bf16),
            pltpu.VMEM(pool.shape, bf16),
            pltpu.VMEM((2, pool_count, piece, WIDTH), bf16),
            pltpu.VMEM((pool_count, piece, WIDTH), bf16),
            pltpu.VMEM((pool_count, piece, WIDTH), bf16),
            pltpu.VMEM((tp_count, 2 * piece, WIDTH), f32),
            pltpu.VMEM((tp_count - 1, 2 * piece, WIDTH), f32),
            pltpu.VMEM((2 * pool_count, piece, WIDTH), bf16),
            pltpu.VMEM((2, HALF, WIDE), bf16),
            pltpu.VMEM((2, 2 * HALF, WIDE), bf16),
            pltpu.VMEM((2 * HALF, WIDE), bf16),
            pltpu.VMEM((LATENT, 2 * HALF), bf16),
            pltpu.VMEM((2, 2 * HALF, GROUP * SUFFIX), f32),
            pltpu.VMEM((2, 2 * HALF, GROUP * SUFFIX), bf16),
            pltpu.VMEM((heads, LATENT, SUFFIX), f32),
            pltpu.VMEM((heads, 8, SUFFIX), f32),
            pltpu.VMEM((heads, 8, SUFFIX), f32),
            pltpu.VMEM((SUFFIX, heads * VALUE_DIM), bf16),
            pltpu.VMEM(pool.shape, bf16),
            pltpu.VMEM((8, 128), jnp.int32),
            pltpu.SMEM((8, 128), jnp.int32),
            pltpu.SMEM((pool_count,), jnp.int32),
            dma((5,)),
            dma,
            dma((2,)),
            dma((2,)),
            dma((tp_count - 1,)),
            dma((tp_count - 1,)),
            dma((7,)),
            dma((7,)),
            dma((2, 2)),
            dma((2, 2)),
            dma((2, 2)),
            dma((2, 2)),
        ],
        compiler_params=pltpu.CompilerParams(
            collective_id=0, has_side_effects=True, vmem_limit_bytes=60 * 1024 * 1024
        ),
        name="latent_attention",
    )(
        block_holder,
        block_slot,
        prefix_blocks,
        suffix_len,
        kv_gain.reshape(1, LATENT),
        jnp.asarray(frequency),
        tokens,
        down_weight.T,
        queries.transpose(1, 2, 0),
        value_weight,
        pool,
    )


def solution(mesh):
    in_specs = (
        P("pool", "tp"),
        P("tp", None),
        P(),
        P("pool", "tp", None),
        P("tp", None, None),
        P("pool", "tp", None),
        P(),
        P(),
        P(),
        P(),
    )
    out_specs = (P("pool", "tp"), P("pool", "tp", None))
    return jax.shard_map(
        functools.partial(on_device, mesh.shape["pool"], mesh.shape["tp"]),
        mesh=mesh,
        in_specs=in_specs,
        out_specs=out_specs,
        check_vma=False,
    )
```

```python
import functools

import jax
import jax.numpy as jnp
import numpy as np
from jax import lax
from jax.experimental import pallas as pl
from jax.experimental.pallas import tpu as pltpu
from jax.sharding import PartitionSpec as P

LATENT = 512
VALUE_DIM = 128
BLOCK = 64
SUFFIX = 128
TABLE = 32
WIDTH = 576
WIDE = 640
ROPE = WIDTH - LATENT
HALF = 256
SCALE = 192.0 ** (-0.5)
HIDDEN = -1e30
EPSILON = 1e-06
GROUP = 4
MESH = pl.DeviceIdType.MESH


def kernel(
    pool_count,
    tp_count,
    holder,
    slot,
    prefix,
    length,
    gain,
    frequency,
    tokens_h,
    down_h,
    queries_h,
    value_h,
    pool_h,
    out_h,
    fresh_h,
    tokens_v,
    down_v,
    queries,
    value_v,
    value_t,
    pool_v,
    leaving,
    relay,
    arrived_even,
    arrived_odd,
    partial_v,
    partial_in,
    fresh_in,
    own,
    near,
    far,
    keys_t,
    scores,
    weights,
    acc,
    high,
    norm,
    out_v,
    entry_s,
    load_sem,
    relay_send,
    relay_recv,
    block_send,
    block_recv,
    sum_send,
    sum_recv,
    fresh_send,
    fresh_recv,
    near_send,
    near_recv,
    far_send,
    far_recv,
):
    me = lax.axis_index("pool")
    tp = lax.axis_index("tp")
    core, z, x = me % 2, (me // 2) % 4, me // 8
    ahead, behind = (tp + 1) % tp_count, (tp + tp_count - 1) % tp_count
    across = (tp + 2) % tp_count
    heads = queries.shape[0]
    slots = pool_v.shape[0]
    piece = pool_v.shape[1]
    groups = TABLE // 2
    arrived = (arrived_even, arrived_odd)

    def peer(step):
        to_core = (core + step % 2) % 2
        to_z = (z + (step // 2) % 4) % 4
        to_x = (x + step // 8) % 4
        return (to_x * 4 + to_z) * 2 + to_core

    loads = [
        pltpu.make_async_copy(pool_h, pool_v, load_sem.at[0]),
        pltpu.make_async_copy(tokens_h, tokens_v, load_sem.at[1]),
        pltpu.make_async_copy(down_h, down_v, load_sem.at[2]),
        pltpu.make_async_copy(queries_h, queries.at[:, pl.ds(0, WIDTH)], load_sem.at[3]),
        pltpu.make_async_copy(value_h, value_v, load_sem.at[4]),
    ]
    for load in loads:
        load.start()

    barrier = pltpu.get_barrier_semaphore()

    @pl.loop(1, pool_count)
    def _(step):
        pl.semaphore_signal(barrier, inc=1, device_id=(peer(step), tp), device_id_type=MESH)

    for step in range(1, tp_count):
        pl.semaphore_signal(
            barrier, inc=1, device_id=(me, (tp + step) % tp_count), device_id_type=MESH
        )
    pl.semaphore_wait(barrier, pool_count - 1 + tp_count - 1)

    loads[0].wait()

    def wanted(request, parity):
        if parity == 0:
            at = jnp.int32(0)
            for k in range(groups - 1):
                at = jnp.where(holder[request, 2 * k] == me, 2 * k, at)
            entry_s[request] = at
        return slot[request, entry_s[request] + parity]

    def stage(parity, to_core, to_x, to_z):
        request = (to_x * 4 + to_z) * 2 + to_core
        leaving[parity, to_core, to_x, to_z] = pool_v[wanted(request, parity)]
        return request

    def bundles(parity):
        return (
            pltpu.make_async_remote_copy(
                src_ref=leaving.at[parity, core, (x + 2) % 4],
                dst_ref=relay.at[parity, 0],
                send_sem=relay_send.at[parity, 0],
                recv_sem=relay_recv.at[parity, 0],
                device_id=(((x + 3) % 4 * 4 + z) * 2 + core, tp),
                device_id_type=MESH,
            ),
            pltpu.make_async_remote_copy(
                src_ref=leaving.at[parity, 1 - core, :, (z + 2) % 4],
                dst_ref=relay.at[parity, 1],
                send_sem=relay_send.at[parity, 1],
                recv_sem=relay_recv.at[parity, 1],
                device_id=((x * 4 + (z + 3) % 4) * 2 + core, tp),
                device_id_type=MESH,
            ),
        )

    def send_block(parity, source, origin, to):
        pltpu.make_async_remote_copy(
            src_ref=source,
            dst_ref=arrived[parity].at[origin],
            send_sem=block_send.at[parity],
            recv_sem=block_recv.at[parity],
            device_id=(to, tp),
            device_id_type=MESH,
        ).start()

    def send_blocks(parity):
        @pl.loop(0, 4)
        def _(k):
            stage(parity, core, (x + 2) % 4, k)
            stage(parity, 1 - core, k, (z + 2) % 4)

        for bundle in bundles(parity):
            bundle.start()

        @pl.loop(1, pool_count)
        def _(step):
            by_core, by_z, by_x = step % 2, (step // 2) % 4, step // 8
            relayed = ((by_core == 0) & (by_x == 2)) | ((by_core == 1) & (by_z == 2))

            @pl.when(jnp.logical_not(relayed))
            def _():
                to_core, to_x, to_z = (core + by_core) % 2, (x + by_x) % 4, (z + by_z) % 4
                request = stage(parity, to_core, to_x, to_z)
                send_block(parity, leaving.at[parity, to_core, to_x, to_z], me, request)

        arrived[parity][me] = pool_v[wanted(me, parity)]

    def pass_on(parity):
        for bundle in bundles(parity):
            bundle.wait_recv()

        @pl.loop(0, 4)
        def _(k):
            send_block(
                parity,
                relay.at[parity, 0, k],
                ((x + 1) % 4 * 4 + z) * 2 + core,
                ((x + 3) % 4 * 4 + k) * 2 + core,
            )
            send_block(
                parity,
                relay.at[parity, 1, k],
                (x * 4 + (z + 1) % 4) * 2 + core,
                (k * 4 + (z + 3) % 4) * 2 + 1 - core,
            )

    send_blocks(0)

    loads[1].wait()
    loads[2].wait()
    partial = lax.dot_general(
        tokens_v[...], down_v[...], (((1,), (1,)), ((), ())), preferred_element_type=jnp.float32
    )
    for owner in range(tp_count):
        for b in range(2):
            partial_v[owner, b * piece : (b + 1) * piece, :] = partial[
                b * BLOCK + owner * piece : b * BLOCK + (owner + 1) * piece, :
            ]
    sums = []
    for step in range(1, tp_count):
        to = (tp + step) % tp_count
        copy = pltpu.make_async_remote_copy(
            src_ref=partial_v.at[to],
            dst_ref=partial_in.at[step - 1],
            send_sem=sum_send.at[step - 1],
            recv_sem=sum_recv.at[step - 1],
            device_id=(me, to),
            device_id_type=MESH,
        )
        copy.start()
        sums.append(copy)

    mark_row = lax.broadcasted_iota(jnp.int32, (WIDE - WIDTH, SUFFIX), 0)
    one_mark = jnp.where(mark_row == 0, 1.0, 0.0).astype(jnp.bfloat16)

    @pl.loop(0, heads)
    def _(head):
        queries[head, WIDTH:, :] = one_mark

    pass_on(0)

    for copy in sums:
        copy.wait_recv()
    latent = partial_v[tp] + partial_in[0] + partial_in[1] + partial_in[2]
    content = latent[:, :LATENT]
    rotary = latent[:, LATENT:]
    inverse = lax.rsqrt(jnp.mean(content * content, axis=1, keepdims=True) + EPSILON)
    normed = content * inverse * gain[...]
    row = lax.broadcasted_iota(jnp.int32, (2 * piece, ROPE), 0)
    lane = lax.broadcasted_iota(jnp.int32, (2 * piece, ROPE), 1)
    token = (row // piece) * BLOCK + tp * piece + row % piece
    angles = (prefix[me] * BLOCK + token).astype(jnp.float32) * frequency[...]
    turned_by = jnp.concatenate([rotary[:, ROPE // 2 :], rotary[:, : ROPE // 2]], axis=1)
    sine = jnp.where(lane < ROPE // 2, -1.0, 1.0) * jnp.sin(angles)
    turned = rotary * jnp.cos(angles) + turned_by * sine
    row512 = lax.broadcasted_iota(jnp.int32, (2 * piece, LATENT), 0)
    token512 = (row512 // piece) * BLOCK + tp * piece + row512 % piece
    normed = jnp.where(token512 < length[me], normed, 0.0).astype(jnp.bfloat16)
    turned = jnp.where(token < length[me], turned, 0.0)
    fresh_at = 2 * ((core * 4 + z) * 4 + x)
    plain = jnp.zeros((piece, WIDE - WIDTH), jnp.float32)
    for b in range(2):
        rows = slice(b * piece, (b + 1) * piece)
        last = jnp.concatenate([turned[rows], plain], axis=1).astype(jnp.bfloat16)
        fresh_in[fresh_at + b, :, :LATENT] = normed[rows]
        fresh_in[fresh_at + b, :, LATENT:] = last[:, :ROPE]
        own[b, (groups - 1) * piece : groups * piece, :LATENT] = normed[rows]
        own[b, (groups - 1) * piece : groups * piece, LATENT:] = last

    def along_x(step):
        here = fresh_in.at[pl.ds(fresh_place(core, z, x), 2)]
        to = (((x + step) % 4) * 4 + z) * 2 + core
        return pltpu.make_async_remote_copy(
            src_ref=here,
            dst_ref=here,
            send_sem=fresh_send.at[step - 1],
            recv_sem=fresh_recv.at[step - 1],
            device_id=(to, tp),
            device_id_type=MESH,
        )

    def along_z(step):
        here = fresh_in.at[pl.ds(fresh_place(core, z, 0), 8)]
        to = (x * 4 + (z + step) % 4) * 2 + core
        return pltpu.make_async_remote_copy(
            src_ref=here,
            dst_ref=here,
            send_sem=fresh_send.at[step + 2],
            recv_sem=fresh_recv.at[step + 2],
            device_id=(to, tp),
            device_id_type=MESH,
        )

    def to_other_core():
        here = fresh_in.at[pl.ds(fresh_place(core, 0, 0), 32)]
        return pltpu.make_async_remote_copy(
            src_ref=here,
            dst_ref=here,
            send_sem=fresh_send.at[6],
            recv_sem=fresh_recv.at[6],
            device_id=((x * 4 + z) * 2 + 1 - core, tp),
            device_id_type=MESH,
        )

    for step in range(1, 4):
        along_x(step).start()

    lane_mark = lax.broadcasted_iota(jnp.int32, (piece, WIDE - WIDTH), 1)

    def gather_blocks(parity):
        others = arrived[parity].at[pl.ds(0, pool_count - 1)]
        pltpu.make_async_copy(others, others, block_recv.at[parity]).wait()
        if parity == 0:
            send_blocks(1)

        @pl.loop(0, groups - 1)
        def _(k):
            block = arrived[parity][holder[me, 2 * k + parity]]
            mark = jnp.where(2 * k + parity < prefix[me], 0.0, HIDDEN)
            marks = jnp.where(lane_mark == 0, mark, 0.0).astype(jnp.bfloat16)
            rows = pl.ds(pl.multiple_of(k * piece, piece), piece)
            own[parity, rows, :LATENT] = block[:, :LATENT]
            own[parity, rows, LATENT:] = jnp.concatenate([block[:, LATENT:], marks], axis=1)

        for side, to in enumerate((ahead, behind)):
            near_copy(parity, side, to).start()

    def near_copy(parity, side, to):
        return pltpu.make_async_remote_copy(
            src_ref=own.at[parity],
            dst_ref=near.at[parity, pl.ds(side * HALF, HALF)],
            send_sem=near_send.at[parity, side],
            recv_sem=near_recv.at[parity, side],
            device_id=(me, to),
            device_id_type=MESH,
        )

    def far_copy(parity, side, to):
        rows = HALF // 2
        return pltpu.make_async_remote_copy(
            src_ref=near.at[parity, pl.ds(side * (HALF + rows), rows)],
            dst_ref=far.at[pl.ds(parity * HALF + side * rows, rows)],
            send_sem=far_send.at[parity, side],
            recv_sem=far_recv.at[parity, side],
            device_id=(me, to),
            device_id_type=MESH,
        )

    def forward(parity):
        for side, to in enumerate((ahead, behind)):
            near_copy(parity, side, to).wait_recv()
            far_copy(parity, side, to).start()

    loads[3].wait()
    loads[4].wait()

    @pl.loop(0, heads)
    def _(head):
        value_t[head] = value_v[head].T

    new_row = lax.broadcasted_iota(jnp.int32, (piece, SUFFIX), 0)
    token_lane = lax.broadcasted_iota(jnp.int32, (piece, SUFFIX), 1)
    live = lax.broadcasted_iota(jnp.int32, (SUFFIX, VALUE_DIM), 0) < length[me]

    def attend(keys, bases, first=False, last=False):
        count = len(bases) * HALF
        for half in range(len(bases)):
            rows = slice(half * HALF, (half + 1) * HALF)
            keys_t[:, rows] = keys[rows, :LATENT].T
        hidden = [base + new_row > token_lane for base in bases]

        def score(group, place):
            query = jnp.concatenate([queries[GROUP * group + j] for j in range(GROUP)], axis=1)
            scores[place, :count] = jnp.dot(
                keys[...], query, preferred_element_type=jnp.float32
            )
            for half, hide in enumerate(hidden):
                rows = slice((half + 1) * HALF - piece, (half + 1) * HALF)
                for j in range(GROUP):
                    lanes = slice(j * SUFFIX, (j + 1) * SUFFIX)
                    scores[place, rows, lanes] = jnp.where(hide, HIDDEN, scores[place, rows, lanes])

        def weigh(group, place):
            decays, shares = [], []
            for j in range(GROUP):
                head = GROUP * group + j
                lanes = slice(j * SUFFIX, (j + 1) * SUFFIX)
                top = jnp.max(scores[place, :count, lanes].reshape(count // 8, 8, SUFFIX), axis=0)
                top = jnp.broadcast_to(jnp.max(top, axis=0, keepdims=True), (8, SUFFIX))
                if not first:
                    old = high[head]
                    top = jnp.maximum(old, top)
                    decay = jnp.exp((old - top) * SCALE)
                    decays.append(decay)
                total = None
                for row in range(0, count, 64):
                    part = scores[place, row : row + 64, lanes].reshape(8, 8, SUFFIX)
                    raised = jnp.exp((part - top[None]) * SCALE)
                    weights[place, row : row + 64, lanes] = raised.reshape(64, SUFFIX).astype(
                        jnp.bfloat16
                    )
                    raised = jnp.sum(raised, axis=0)
                    total = raised if total is None else total + raised
                if not first:
                    total = total + norm[head] * decay
                if last:
                    total = 1.0 / jnp.sum(total, axis=0, keepdims=True)
                    shares.append(jnp.broadcast_to(total, (8, SUFFIX)))
                else:
                    high[head] = top
                    norm[head] = total
            return decays, shares

        def mix(group, place, decays, shares):
            mixed = jnp.dot(
                keys_t[:, :count], weights[place, :count], preferred_element_type=jnp.float32
            )
            for j in range(GROUP):
                head = GROUP * group + j
                part = mixed[:, j * SUFFIX : (j + 1) * SUFFIX].reshape(LATENT // 8, 8, SUFFIX)
                if not first:
                    part = part + acc[head].reshape(LATENT // 8, 8, SUFFIX) * decays[j][None]
                if last:
                    part = (part * shares[j][None]).reshape(LATENT, SUFFIX).astype(jnp.bfloat16)
                    value = jnp.dot(value_t[head], part, preferred_element_type=jnp.float32).T
                    columns = pl.ds(pl.multiple_of(head * VALUE_DIM, VALUE_DIM), VALUE_DIM)
                    out_v[:, columns] = jnp.where(live, value, 0.0).astype(jnp.bfloat16)
                else:
                    acc[head] = part.reshape(LATENT, SUFFIX)

        def two_groups(group, more):
            score(group + 1, 1)
            mix(group, 0, *weigh(group, 0))
            if more:
                score(group + 2, 0)
            mix(group + 1, 1, *weigh(group + 1, 1))

        score(0, 0)

        @pl.loop(0, heads // GROUP // 2 - 1)
        def _(pair):
            two_groups(2 * pair, True)

        two_groups(heads // GROUP - 2, False)

    gather_blocks(0)
    pass_on(1)
    attend(own.at[0], [tp * piece], first=True)
    gather_blocks(1)
    attend(own.at[1], [BLOCK + tp * piece])
    for step in range(1, 4):
        along_x(step).wait_recv()
    for step in range(1, 4):
        along_z(step).start()
    for parity in range(2):
        forward(parity)
        attend(near.at[parity], [parity * BLOCK + side * piece for side in (behind, ahead)])

    for step in range(1, 4):
        along_z(step).wait_recv()
    to_other_core().start()

    for parity in range(2):
        for side, to in enumerate((ahead, behind)):
            far_copy(parity, side, to).wait_recv()
    attend(far, [parity * BLOCK + across * piece for parity in range(2)], last=True)

    store_out = pltpu.make_async_copy(out_v, out_h, load_sem.at[1])
    store_out.start()

    to_other_core().wait_recv()
    store_fresh = pltpu.make_async_copy(fresh_in, fresh_h, load_sem.at[0])
    store_fresh.start()

    for copy in sums:
        copy.wait_send()
    for parity in range(2):
        sent = arrived[parity].at[pl.ds(0, pool_count - 1)]
        pltpu.make_async_copy(sent, sent, block_send.at[parity]).wait()
        for bundle in bundles(parity):
            bundle.wait_send()
        for side, to in enumerate((ahead, behind)):
            near_copy(parity, side, to).wait_send()
            far_copy(parity, side, to).wait_send()
    for step in range(1, 4):
        along_x(step).wait_send()
        along_z(step).wait_send()
    to_other_core().wait_send()
    store_fresh.wait()
    store_out.wait()


def fresh_place(at_core, at_z, at_x):
    return 2 * ((at_core * 4 + at_z) * 4 + at_x)


def finish(holder, slot, prefix, result, fresh, pool, out, new_pool, sems, block_sems):
    me = lax.axis_index("pool")
    copies = [
        pltpu.make_async_copy(pool, new_pool, sems.at[0]),
        pltpu.make_async_copy(result, out, sems.at[1]),
    ]
    for copy in copies:
        copy.start()
    copies[0].wait()

    def place(request, b, act):
        entry = prefix[request] + b

        @pl.when(holder[request, entry] == me)
        def _():
            source = fresh_place(request % 2, (request // 2) % 4, request // 8) + b
            copy = pltpu.make_async_copy(
                fresh.at[source], new_pool.at[slot[request, entry]], block_sems.at[request, b]
            )
            act(copy)

    @pl.loop(0, holder.shape[0])
    def _(request):
        for b in range(2):
            place(request, b, lambda copy: copy.start())

    @pl.loop(0, holder.shape[0])
    def _(request):
        for b in range(2):
            place(request, b, lambda copy: copy.wait())

    copies[1].wait()


def on_device(
    pool_count,
    tp_count,
    tokens,
    down_weight,
    kv_gain,
    queries,
    value_weight,
    pool,
    block_holder,
    block_slot,
    prefix_blocks,
    suffix_len,
):
    heads = queries.shape[1]
    piece = pool.shape[1]
    exponent = np.arange(ROPE // 2).astype(np.float32) * np.float32(2.0 / ROPE)
    inverse_frequency = np.power(np.float32(10000.0), -exponent).astype(np.float32)
    frequency = np.tile(inverse_frequency, 2)[None, :]
    bf16, f32 = jnp.bfloat16, jnp.float32
    smem = pl.BlockSpec(memory_space=pltpu.SMEM)
    vmem = pl.BlockSpec(memory_space=pltpu.VMEM)
    anywhere = pl.BlockSpec(memory_space=pl.ANY)
    dma = pltpu.SemaphoreType.DMA
    result, fresh = pl.pallas_call(
        functools.partial(kernel, pool_count, tp_count),
        out_shape=(
            jax.ShapeDtypeStruct((SUFFIX, heads * VALUE_DIM), bf16),
            jax.ShapeDtypeStruct((2 * pool_count, piece, WIDTH), bf16),
        ),
        in_specs=[smem] * 4 + [vmem] * 2 + [anywhere] * 5,
        out_specs=(anywhere, anywhere),
        scratch_shapes=[
            pltpu.VMEM(tokens.shape, bf16),
            pltpu.VMEM(down_weight.shape[::-1], bf16),
            pltpu.VMEM((heads, WIDE, SUFFIX), bf16),
            pltpu.VMEM(value_weight.shape, bf16),
            pltpu.VMEM((heads, VALUE_DIM, LATENT), bf16),
            pltpu.VMEM(pool.shape, bf16),
            pltpu.VMEM((2, 2, 4, 4, piece, WIDTH), bf16),
            pltpu.VMEM((2, 2, 4, piece, WIDTH), bf16),
            pltpu.VMEM((pool_count, piece, WIDTH), bf16),
            pltpu.VMEM((pool_count, piece, WIDTH), bf16),
            pltpu.VMEM((tp_count, 2 * piece, WIDTH), f32),
            pltpu.VMEM((tp_count - 1, 2 * piece, WIDTH), f32),
            pltpu.VMEM((2 * pool_count, piece, WIDTH), bf16),
            pltpu.VMEM((2, HALF, WIDE), bf16),
            pltpu.VMEM((2, 2 * HALF, WIDE), bf16),
            pltpu.VMEM((2 * HALF, WIDE), bf16),
            pltpu.VMEM((LATENT, 2 * HALF), bf16),
            pltpu.VMEM((2, 2 * HALF, GROUP * SUFFIX), f32),
            pltpu.VMEM((2, 2 * HALF, GROUP * SUFFIX), bf16),
            pltpu.VMEM((heads, LATENT, SUFFIX), f32),
            pltpu.VMEM((heads, 8, SUFFIX), f32),
            pltpu.VMEM((heads, 8, SUFFIX), f32),
            pltpu.VMEM((SUFFIX, heads * VALUE_DIM), bf16),
            pltpu.SMEM((pool_count,), jnp.int32),
            dma((5,)),
            dma((2, 2)),
            dma((2, 2)),
            dma((2,)),
            dma((2,)),
            dma((tp_count - 1,)),
            dma((tp_count - 1,)),
            dma((7,)),
            dma((7,)),
            dma((2, 2)),
            dma((2, 2)),
            dma((2, 2)),
            dma((2, 2)),
        ],
        compiler_params=pltpu.CompilerParams(
            collective_id=0, has_side_effects=True, vmem_limit_bytes=60 * 1024 * 1024
        ),
        name="latent_attention",
    )(
        block_holder,
        block_slot,
        prefix_blocks,
        suffix_len,
        kv_gain.reshape(1, LATENT),
        jnp.asarray(frequency),
        tokens,
        down_weight.T,
        queries.transpose(1, 2, 0),
        value_weight,
        pool,
    )
    return pl.pallas_call(
        finish,
        out_shape=(
            jax.ShapeDtypeStruct(result.shape, bf16),
            jax.ShapeDtypeStruct(pool.shape, bf16),
        ),
        in_specs=[smem] * 3 + [anywhere] * 3,
        out_specs=(anywhere, anywhere),
        scratch_shapes=[dma((2,)), dma((pool_count, 2))],
        name="finish",
    )(block_holder, block_slot, prefix_blocks, result, fresh, pool)


def solution(mesh):
    in_specs = (
        P("pool", "tp"),
        P("tp", None),
        P(),
        P("pool", "tp", None),
        P("tp", None, None),
        P("pool", "tp", None),
        P(),
        P(),
        P(),
        P(),
    )
    out_specs = (P("pool", "tp"), P("pool", "tp", None))
    return jax.shard_map(
        functools.partial(on_device, mesh.shape["pool"], mesh.shape["tp"]),
        mesh=mesh,
        in_specs=in_specs,
        out_specs=out_specs,
        check_vma=False,
    )
```

```python
import functools
import math

import jax
import jax.numpy as jnp
import numpy as np
from jax import lax
from jax.experimental import pallas as pl
from jax.experimental.pallas import tpu as pltpu
from jax.sharding import PartitionSpec as P

LATENT = 512
VALUE_DIM = 128
BLOCK = 64
SUFFIX = 128
TABLE = 32
WIDTH = 576
WIDE = 640
ROPE = WIDTH - LATENT
HALF = 256
SCALE = 192.0 ** (-0.5) * math.log2(math.e)
HIDDEN = -1e30
EPSILON = 1e-06
GROUP = 4
MESH = pl.DeviceIdType.MESH


def kernel(
    pool_count,
    tp_count,
    holder,
    slot,
    prefix,
    length,
    gain,
    frequency,
    tokens_h,
    down_h,
    queries_h,
    value_h,
    pool_h,
    out_h,
    fresh_h,
    tokens_v,
    down_v,
    queries,
    value_v,
    pool_v,
    leaving,
    arrived_even,
    arrived_odd,
    partial_v,
    partial_in,
    fresh_in,
    own,
    near,
    far,
    keys_t,
    scores,
    weights,
    acc,
    high,
    norm,
    out_v,
    entry_s,
    load_sem,
    block_send,
    block_recv,
    sum_send,
    sum_recv,
    fresh_send,
    fresh_recv,
    near_send,
    near_recv,
    far_send,
    far_recv,
):
    me = lax.axis_index("pool")
    tp = lax.axis_index("tp")
    core, z, x = me % 2, (me // 2) % 4, me // 8
    ahead, behind = (tp + 1) % tp_count, (tp + tp_count - 1) % tp_count
    across = (tp + 2) % tp_count
    heads = queries.shape[0]
    slots = pool_v.shape[0]
    piece = pool_v.shape[1]
    groups = TABLE // 2
    arrived = (arrived_even, arrived_odd)

    def peer(step):
        to_core = (core + step % 2) % 2
        to_z = (z + (step // 2) % 4) % 4
        to_x = (x + step // 8) % 4
        return (to_x * 4 + to_z) * 2 + to_core

    loads = [
        pltpu.make_async_copy(pool_h, pool_v, load_sem.at[0]),
        pltpu.make_async_copy(tokens_h, tokens_v, load_sem.at[1]),
        pltpu.make_async_copy(down_h, down_v, load_sem.at[2]),
        pltpu.make_async_copy(queries_h, queries.at[:, pl.ds(0, WIDTH)], load_sem.at[3]),
        pltpu.make_async_copy(value_h, value_v, load_sem.at[4]),
    ]
    for load in loads:
        load.start()

    barrier = pltpu.get_barrier_semaphore()

    @pl.loop(1, pool_count)
    def _(step):
        pl.semaphore_signal(barrier, inc=1, device_id=(peer(step), tp), device_id_type=MESH)

    for step in range(1, tp_count):
        pl.semaphore_signal(
            barrier, inc=1, device_id=(me, (tp + step) % tp_count), device_id_type=MESH
        )

    loads[0].wait()

    @pl.loop(0, pool_count)
    def _(request):
        at = jnp.int32(0)
        for k in range(groups - 1):
            at = jnp.where(holder[request, 2 * k] == me, 2 * k, at)
        entry_s[request] = at
        leaving[0, request] = pool_v[slot[request, at]]

    arrived[0][me] = pool_v[slot[me, entry_s[me]]]

    pl.semaphore_wait(barrier, pool_count - 1 + tp_count - 1)

    def send_blocks(parity):
        @pl.loop(1, pool_count)
        def _(step):
            request = peer(step)
            pltpu.make_async_remote_copy(
                src_ref=leaving.at[parity, request],
                dst_ref=arrived[parity].at[me],
                send_sem=block_send.at[parity],
                recv_sem=block_recv.at[parity],
                device_id=(request, tp),
                device_id_type=MESH,
            ).start()

    send_blocks(0)

    @pl.loop(0, pool_count)
    def _(request):
        leaving[1, request] = pool_v[slot[request, entry_s[request] + 1]]

    arrived[1][me] = pool_v[slot[me, entry_s[me] + 1]]

    loads[1].wait()
    loads[2].wait()
    partial = lax.dot_general(
        tokens_v[...], down_v[...], (((1,), (1,)), ((), ())), preferred_element_type=jnp.float32
    )
    for owner in range(tp_count):
        for b in range(2):
            partial_v[owner, b * piece : (b + 1) * piece, :] = partial[
                b * BLOCK + owner * piece : b * BLOCK + (owner + 1) * piece, :
            ]
    sums = []
    for step in range(1, tp_count):
        to = (tp + step) % tp_count
        copy = pltpu.make_async_remote_copy(
            src_ref=partial_v.at[to],
            dst_ref=partial_in.at[step - 1],
            send_sem=sum_send.at[step - 1],
            recv_sem=sum_recv.at[step - 1],
            device_id=(me, to),
            device_id_type=MESH,
        )
        copy.start()
        sums.append(copy)

    mark_row = lax.broadcasted_iota(jnp.int32, (WIDE - WIDTH, SUFFIX), 0)
    one_mark = jnp.where(mark_row == 0, 1.0, 0.0).astype(jnp.bfloat16)

    @pl.loop(0, heads)
    def _(head):
        queries[head, WIDTH:, :] = one_mark

    for copy in sums:
        copy.wait_recv()
    latent = partial_v[tp] + partial_in[0] + partial_in[1] + partial_in[2]
    content = latent[:, :LATENT]
    rotary = latent[:, LATENT:]
    inverse = lax.rsqrt(jnp.mean(content * content, axis=1, keepdims=True) + EPSILON)
    normed = content * inverse * gain[...]
    row = lax.broadcasted_iota(jnp.int32, (2 * piece, ROPE), 0)
    lane = lax.broadcasted_iota(jnp.int32, (2 * piece, ROPE), 1)
    token = (row // piece) * BLOCK + tp * piece + row % piece
    angles = (prefix[me] * BLOCK + token).astype(jnp.float32) * frequency[...]
    turned_by = jnp.concatenate([rotary[:, ROPE // 2 :], rotary[:, : ROPE // 2]], axis=1)
    sine = jnp.where(lane < ROPE // 2, -1.0, 1.0) * jnp.sin(angles)
    turned = rotary * jnp.cos(angles) + turned_by * sine
    row512 = lax.broadcasted_iota(jnp.int32, (2 * piece, LATENT), 0)
    token512 = (row512 // piece) * BLOCK + tp * piece + row512 % piece
    normed = jnp.where(token512 < length[me], normed, 0.0).astype(jnp.bfloat16)
    turned = jnp.where(token < length[me], turned, 0.0)
    fresh_at = 2 * ((core * 4 + z) * 4 + x)
    plain = jnp.zeros((piece, WIDE - WIDTH), jnp.float32)
    for b in range(2):
        rows = slice(b * piece, (b + 1) * piece)
        last = jnp.concatenate([turned[rows], plain], axis=1).astype(jnp.bfloat16)
        fresh_in[fresh_at + b, :, :LATENT] = normed[rows]
        fresh_in[fresh_at + b, :, LATENT:] = last[:, :ROPE]
        own[b, (groups - 1) * piece : groups * piece, :LATENT] = normed[rows]
        own[b, (groups - 1) * piece : groups * piece, LATENT:] = last

    def along_x(step):
        here = fresh_in.at[pl.ds(fresh_place(core, z, x), 2)]
        to = (((x + step) % 4) * 4 + z) * 2 + core
        return pltpu.make_async_remote_copy(
            src_ref=here,
            dst_ref=here,
            send_sem=fresh_send.at[step - 1],
            recv_sem=fresh_recv.at[step - 1],
            device_id=(to, tp),
            device_id_type=MESH,
        )

    def along_z(step):
        here = fresh_in.at[pl.ds(fresh_place(core, z, 0), 8)]
        to = (x * 4 + (z + step) % 4) * 2 + core
        return pltpu.make_async_remote_copy(
            src_ref=here,
            dst_ref=here,
            send_sem=fresh_send.at[step + 2],
            recv_sem=fresh_recv.at[step + 2],
            device_id=(to, tp),
            device_id_type=MESH,
        )

    def to_other_core():
        here = fresh_in.at[pl.ds(fresh_place(core, 0, 0), 32)]
        return pltpu.make_async_remote_copy(
            src_ref=here,
            dst_ref=here,
            send_sem=fresh_send.at[6],
            recv_sem=fresh_recv.at[6],
            device_id=((x * 4 + z) * 2 + 1 - core, tp),
            device_id_type=MESH,
        )

    for step in range(1, 4):
        along_x(step).start()

    lane_mark = lax.broadcasted_iota(jnp.int32, (piece, WIDE - WIDTH), 1)

    def gather_blocks(parity):
        others = arrived[parity].at[pl.ds(0, pool_count - 1)]
        pltpu.make_async_copy(others, others, block_recv.at[parity]).wait()
        if parity == 0:
            send_blocks(1)

        @pl.loop(0, groups - 1)
        def _(k):
            block = arrived[parity][holder[me, 2 * k + parity]]
            mark = jnp.where(2 * k + parity < prefix[me], 0.0, HIDDEN)
            marks = jnp.where(lane_mark == 0, mark, 0.0).astype(jnp.bfloat16)
            rows = pl.ds(pl.multiple_of(k * piece, piece), piece)
            own[parity, rows, :LATENT] = block[:, :LATENT]
            own[parity, rows, LATENT:] = jnp.concatenate([block[:, LATENT:], marks], axis=1)

        for part in range(2):
            for side in range(2):
                near_copy(parity, part, side).start()

    neighbours = (ahead, behind)
    third = HALF // 2

    def near_copy(parity, part, side):
        return pltpu.make_async_remote_copy(
            src_ref=own.at[parity, pl.ds(part * third, third)],
            dst_ref=near.at[parity, part, pl.ds(side * third, third)],
            send_sem=near_send.at[parity, part, side],
            recv_sem=near_recv.at[parity, part, side],
            device_id=(me, neighbours[side]),
            device_id_type=MESH,
        )

    def far_copy(parity, side):
        rows = pl.ds(side * third, third)
        return pltpu.make_async_remote_copy(
            src_ref=near.at[parity, side, rows],
            dst_ref=far.at[parity, rows],
            send_sem=far_send.at[parity, side],
            recv_sem=far_recv.at[parity, side],
            device_id=(me, neighbours[side]),
            device_id_type=MESH,
        )

    def take(parity, part):
        for side in range(2):
            near_copy(parity, part, side).wait_recv()
        far_copy(parity, part).start()

    def take_far(parity):
        for side in range(2):
            far_copy(parity, side).wait_recv()

    loads[3].wait()

    new_row = lax.broadcasted_iota(jnp.int32, (piece, SUFFIX), 0)
    token_lane = lax.broadcasted_iota(jnp.int32, (piece, SUFFIX), 1)
    live = lax.broadcasted_iota(jnp.int32, (SUFFIX, VALUE_DIM), 0) < length[me]

    def attend(pieces, fresh_rows, first=False, last=False):
        count = sum(piece_of.shape[0] for piece_of in pieces)
        starts = [sum(p.shape[0] for p in pieces[:n]) for n in range(len(pieces))]
        for start, keys in zip(starts, pieces):
            for row in range(0, keys.shape[0], HALF):
                keys_t[:, start + row : start + row + HALF] = keys[row : row + HALF, :LATENT].T
        hidden = [(row, base + new_row > token_lane) for row, base in fresh_rows]

        def score(group, place):
            query = jnp.concatenate([queries[GROUP * group + j] for j in range(GROUP)], axis=1)
            for start, keys in zip(starts, pieces):
                scores[place, start : start + keys.shape[0]] = jnp.dot(
                    keys[...], query, preferred_element_type=jnp.float32
                )
            for row, hide in hidden:
                rows = slice(row, row + piece)
                for j in range(GROUP):
                    lanes = slice(j * SUFFIX, (j + 1) * SUFFIX)
                    scores[place, rows, lanes] = jnp.where(hide, HIDDEN, scores[place, rows, lanes])

        def weigh(group, place):
            decays, shares = [], []
            for j in range(GROUP):
                head = GROUP * group + j
                lanes = slice(j * SUFFIX, (j + 1) * SUFFIX)
                top = jnp.max(scores[place, :count, lanes].reshape(count // 8, 8, SUFFIX), axis=0)
                top = jnp.max(top, axis=0, keepdims=True) * SCALE
                top = jnp.broadcast_to(top, (8, SUFFIX))
                if not first:
                    old = high[head]
                    top = jnp.maximum(old, top)
                    decay = jnp.exp2(old - top)
                    decays.append(decay)
                total = None
                for row in range(0, count, 64):
                    part = scores[place, row : row + 64, lanes].reshape(8, 8, SUFFIX)
                    raised = jnp.exp2(part * SCALE - top[None])
                    weights[place, row : row + 64, lanes] = raised.reshape(64, SUFFIX).astype(
                        jnp.bfloat16
                    )
                    raised = jnp.sum(raised, axis=0)
                    total = raised if total is None else total + raised
                if not first:
                    total = total + norm[head] * decay
                if last:
                    total = 1.0 / jnp.sum(total, axis=0, keepdims=True)
                    shares.append(jnp.broadcast_to(total, (8, SUFFIX)))
                else:
                    high[head] = top
                    norm[head] = total
            return decays, shares

        def mix(group, place, decays, shares):
            mixed = jnp.dot(
                keys_t[:, :count], weights[place, :count], preferred_element_type=jnp.float32
            )
            for j in range(GROUP):
                head = GROUP * group + j
                part = mixed[:, j * SUFFIX : (j + 1) * SUFFIX].reshape(LATENT // 8, 8, SUFFIX)
                if not first:
                    part = part + acc[head].reshape(LATENT // 8, 8, SUFFIX) * decays[j][None]
                if last:
                    part = (part * shares[j][None]).reshape(LATENT, SUFFIX).astype(jnp.bfloat16)
                    value = jnp.dot(value_v[head].T, part, preferred_element_type=jnp.float32).T
                    columns = pl.ds(pl.multiple_of(head * VALUE_DIM, VALUE_DIM), VALUE_DIM)
                    out_v[:, columns] = jnp.where(live, value, 0.0).astype(jnp.bfloat16)
                else:
                    acc[head] = part.reshape(LATENT, SUFFIX)

        def two_groups(group, more):
            score(group + 1, 1)
            mix(group, 0, *weigh(group, 0))
            if more:
                score(group + 2, 0)
            mix(group + 1, 1, *weigh(group + 1, 1))

        score(0, 0)

        @pl.loop(0, heads // GROUP // 2 - 1)
        def _(pair):
            two_groups(2 * pair, True)

        two_groups(heads // GROUP - 2, False)

    def first_new(parity, owner):
        return parity * BLOCK + owner * piece

    gather_blocks(0)
    attend([own.at[0]], [(HALF - piece, first_new(0, tp))], first=True)
    take(0, 0)
    attend([near.at[0, 0]], [])
    gather_blocks(1)
    take(0, 1)
    for step in range(1, 4):
        along_x(step).wait_recv()
    for step in range(1, 4):
        along_z(step).start()
    attend(
        [near.at[0, 1]],
        [(third - piece, first_new(0, behind)), (HALF - piece, first_new(0, ahead))],
    )
    take_far(0)
    attend(
        [far.at[0], own.at[1]],
        [(HALF - piece, first_new(0, across)), (2 * HALF - piece, first_new(1, tp))],
    )
    for part in range(2):
        take(1, part)
    for step in range(1, 4):
        along_z(step).wait_recv()
    to_other_core().start()
    attend(
        [near.at[1, 0], near.at[1, 1]],
        [
            (HALF + third - piece, first_new(1, behind)),
            (2 * HALF - piece, first_new(1, ahead)),
        ],
    )
    to_other_core().wait_recv()
    store_fresh = pltpu.make_async_copy(fresh_in, fresh_h, load_sem.at[0])
    store_fresh.start()
    take_far(1)
    loads[4].wait()
    attend([far.at[1]], [(HALF - piece, first_new(1, across))], last=True)

    store_out = pltpu.make_async_copy(out_v, out_h, load_sem.at[1])
    store_out.start()

    for copy in sums:
        copy.wait_send()
    for parity in range(2):
        sent = arrived[parity].at[pl.ds(0, pool_count - 1)]
        pltpu.make_async_copy(sent, sent, block_send.at[parity]).wait()
        for side in range(2):
            for part in range(2):
                near_copy(parity, part, side).wait_send()
            far_copy(parity, side).wait_send()
    for step in range(1, 4):
        along_x(step).wait_send()
        along_z(step).wait_send()
    to_other_core().wait_send()
    store_fresh.wait()
    store_out.wait()


def fresh_place(at_core, at_z, at_x):
    return 2 * ((at_core * 4 + at_z) * 4 + at_x)


def finish(
    holder, slot, prefix, result_h, fresh_h, pool_h, out_h, new_pool_h, result, fresh, pool, sems
):
    me = lax.axis_index("pool")
    loads = [
        pltpu.make_async_copy(pool_h, pool, sems.at[0]),
        pltpu.make_async_copy(fresh_h, fresh, sems.at[1]),
        pltpu.make_async_copy(result_h, result, sems.at[2]),
    ]
    for load in loads:
        load.start()
    for load in loads:
        load.wait()
    store_out = pltpu.make_async_copy(result, out_h, sems.at[2])
    store_out.start()

    @pl.loop(0, holder.shape[0])
    def _(request):
        for b in range(2):
            entry = prefix[request] + b

            @pl.when(holder[request, entry] == me)
            def _():
                source = fresh_place(request % 2, (request // 2) % 4, request // 8) + b
                pool[slot[request, entry]] = fresh[source]

    store_pool = pltpu.make_async_copy(pool, new_pool_h, sems.at[0])
    store_pool.start()
    store_out.wait()
    store_pool.wait()


def on_device(
    pool_count,
    tp_count,
    tokens,
    down_weight,
    kv_gain,
    queries,
    value_weight,
    pool,
    block_holder,
    block_slot,
    prefix_blocks,
    suffix_len,
):
    heads = queries.shape[1]
    piece = pool.shape[1]
    exponent = np.arange(ROPE // 2).astype(np.float32) * np.float32(2.0 / ROPE)
    inverse_frequency = np.power(np.float32(10000.0), -exponent).astype(np.float32)
    frequency = np.tile(inverse_frequency, 2)[None, :]
    bf16, f32 = jnp.bfloat16, jnp.float32
    smem = pl.BlockSpec(memory_space=pltpu.SMEM)
    vmem = pl.BlockSpec(memory_space=pltpu.VMEM)
    anywhere = pl.BlockSpec(memory_space=pl.ANY)
    dma = pltpu.SemaphoreType.DMA
    result, fresh = pl.pallas_call(
        functools.partial(kernel, pool_count, tp_count),
        out_shape=(
            jax.ShapeDtypeStruct((SUFFIX, heads * VALUE_DIM), bf16),
            jax.ShapeDtypeStruct((2 * pool_count, piece, WIDTH), bf16),
        ),
        in_specs=[smem] * 4 + [vmem] * 2 + [anywhere] * 5,
        out_specs=(anywhere, anywhere),
        scratch_shapes=[
            pltpu.VMEM(tokens.shape, bf16),
            pltpu.VMEM(down_weight.shape[::-1], bf16),
            pltpu.VMEM((heads, WIDE, SUFFIX), bf16),
            pltpu.VMEM(value_weight.shape, bf16),
            pltpu.VMEM(pool.shape, bf16),
            pltpu.VMEM((2, pool_count, piece, WIDTH), bf16),
            pltpu.VMEM((pool_count, piece, WIDTH), bf16),
            pltpu.VMEM((pool_count, piece, WIDTH), bf16),
            pltpu.VMEM((tp_count, 2 * piece, WIDTH), f32),
            pltpu.VMEM((tp_count - 1, 2 * piece, WIDTH), f32),
            pltpu.VMEM((2 * pool_count, piece, WIDTH), bf16),
            pltpu.VMEM((2, HALF, WIDE), bf16),
            pltpu.VMEM((2, 2, HALF, WIDE), bf16),
            pltpu.VMEM((2, HALF, WIDE), bf16),
            pltpu.VMEM((LATENT, 2 * HALF), bf16),
            pltpu.VMEM((2, 2 * HALF, GROUP * SUFFIX), f32),
            pltpu.VMEM((2, 2 * HALF, GROUP * SUFFIX), bf16),
            pltpu.VMEM((heads, LATENT, SUFFIX), f32),
            pltpu.VMEM((heads, 8, SUFFIX), f32),
            pltpu.VMEM((heads, 8, SUFFIX), f32),
            pltpu.VMEM((SUFFIX, heads * VALUE_DIM), bf16),
            pltpu.SMEM((pool_count,), jnp.int32),
            dma((5,)),
            dma((2,)),
            dma((2,)),
            dma((tp_count - 1,)),
            dma((tp_count - 1,)),
            dma((7,)),
            dma((7,)),
            dma((2, 2, 2)),
            dma((2, 2, 2)),
            dma((2, 2)),
            dma((2, 2)),
        ],
        compiler_params=pltpu.CompilerParams(
            collective_id=0, has_side_effects=True, vmem_limit_bytes=60 * 1024 * 1024
        ),
        name="latent_attention",
    )(
        block_holder,
        block_slot,
        prefix_blocks,
        suffix_len,
        kv_gain.reshape(1, LATENT),
        jnp.asarray(frequency),
        tokens,
        down_weight.T,
        queries.transpose(1, 2, 0),
        value_weight,
        pool,
    )
    return pl.pallas_call(
        finish,
        out_shape=(
            jax.ShapeDtypeStruct(result.shape, bf16),
            jax.ShapeDtypeStruct(pool.shape, bf16),
        ),
        in_specs=[smem] * 3 + [anywhere] * 3,
        out_specs=(anywhere, anywhere),
        scratch_shapes=[
            pltpu.VMEM(result.shape, bf16),
            pltpu.VMEM(fresh.shape, bf16),
            pltpu.VMEM(pool.shape, bf16),
            dma((3,)),
        ],
        name="finish",
    )(block_holder, block_slot, prefix_blocks, result, fresh, pool)


def solution(mesh):
    in_specs = (
        P("pool", "tp"),
        P("tp", None),
        P(),
        P("pool", "tp", None),
        P("tp", None, None),
        P("pool", "tp", None),
        P(),
        P(),
        P(),
        P(),
    )
    out_specs = (P("pool", "tp"), P("pool", "tp", None))
    return jax.shard_map(
        functools.partial(on_device, mesh.shape["pool"], mesh.shape["tp"]),
        mesh=mesh,
        in_specs=in_specs,
        out_specs=out_specs,
        check_vma=False,
    )
```

```python
import functools
import math

import jax
import jax.numpy as jnp
import numpy as np
from jax import lax
from jax.experimental import pallas as pl
from jax.experimental.pallas import tpu as pltpu
from jax.sharding import PartitionSpec as P

LATENT = 512
VALUE_DIM = 128
BLOCK = 64
SUFFIX = 128
TABLE = 32
WIDTH = 576
WIDE = 640
ROPE = WIDTH - LATENT
HALF = 256
SCALE = 192.0 ** (-0.5) * math.log2(math.e)
HIDDEN = -1e30
EPSILON = 1e-06
ROWS = 1024
STRIP = 32
LOWEST = -3e38
MESH = pl.DeviceIdType.MESH


def kernel(
    pool_count,
    tp_count,
    holder,
    slot,
    prefix,
    length,
    gain,
    frequency,
    tokens_h,
    down_h,
    queries_h,
    value_h,
    pool_h,
    out_h,
    new_pool_h,
    tokens_v,
    down_v,
    queries_in,
    queries,
    value_v,
    pool_v,
    leaving,
    arrived_even,
    arrived_odd,
    partial_v,
    partial_in,
    fresh_in,
    keys,
    keys_t,
    bias,
    scores_a,
    scores_b,
    weights_a,
    weights_b,
    decay_a,
    decay_b,
    acc,
    high,
    norm,
    out_v,
    new_pool_v,
    index_v,
    index_s,
    entry_s,
    load_sem,
    index_sem,
    block_send,
    block_recv,
    sum_send,
    sum_recv,
    fresh_send,
    fresh_recv,
    near_send,
    near_recv,
    far_send,
    far_recv,
):
    me = lax.axis_index("pool")
    tp = lax.axis_index("tp")
    core, z, x = me % 2, (me // 2) % 4, me // 8
    ahead, behind = (tp + 1) % tp_count, (tp + tp_count - 1) % tp_count
    across = (tp + 2) % tp_count
    heads = queries_in.shape[0]
    slots = pool_v.shape[0]
    piece = pool_v.shape[1]
    groups = TABLE // 2
    arrived = (arrived_even, arrived_odd)
    scores, weights = (scores_a, scores_b), (weights_a, weights_b)
    decay = (decay_a, decay_b)

    def peer(step):
        to_core = (core + step % 2) % 2
        to_z = (z + (step // 2) % 4) % 4
        to_x = (x + step // 8) % 4
        return (to_x * 4 + to_z) * 2 + to_core

    loads = [
        pltpu.make_async_copy(pool_h, pool_v, load_sem.at[0]),
        pltpu.make_async_copy(tokens_h, tokens_v, load_sem.at[1]),
        pltpu.make_async_copy(down_h, down_v, load_sem.at[2]),
        pltpu.make_async_copy(queries_h, queries_in, load_sem.at[3]),
        pltpu.make_async_copy(value_h, value_v, load_sem.at[4]),
    ]
    for load in loads:
        load.start()

    barrier = pltpu.get_barrier_semaphore()

    @pl.loop(1, pool_count)
    def _(step):
        pl.semaphore_signal(barrier, inc=1, device_id=(peer(step), tp), device_id_type=MESH)

    for step in range(1, tp_count):
        pl.semaphore_signal(
            barrier, inc=1, device_id=(me, (tp + step) % tp_count), device_id_type=MESH
        )

    loads[0].wait()

    @pl.loop(0, pool_count)
    def _(request):
        at = jnp.int32(0)
        for k in range(groups - 1):
            at = jnp.where(holder[request, 2 * k] == me, 2 * k, at)
        entry_s[request] = at
        leaving[0, request] = pool_v[slot[request, at]]

    arrived[0][me] = pool_v[slot[me, entry_s[me]]]

    pl.semaphore_wait(barrier, pool_count - 1 + tp_count - 1)

    def send_blocks(parity):
        @pl.loop(1, pool_count)
        def _(step):
            request = peer(step)
            pltpu.make_async_remote_copy(
                src_ref=leaving.at[parity, request],
                dst_ref=arrived[parity].at[me],
                send_sem=block_send.at[parity],
                recv_sem=block_recv.at[parity],
                device_id=(request, tp),
                device_id_type=MESH,
            ).start()

    send_blocks(0)

    @pl.loop(0, pool_count)
    def _(request):
        leaving[1, request] = pool_v[slot[request, entry_s[request] + 1]]

    arrived[1][me] = pool_v[slot[me, entry_s[me] + 1]]

    loads[1].wait()
    loads[2].wait()
    partial = lax.dot_general(
        tokens_v[...], down_v[...], (((1,), (1,)), ((), ())), preferred_element_type=jnp.float32
    )
    for owner in range(tp_count):
        for b in range(2):
            partial_v[owner, b * piece : (b + 1) * piece, :] = partial[
                b * BLOCK + owner * piece : b * BLOCK + (owner + 1) * piece, :
            ]
    sums = []
    for step in range(1, tp_count):
        to = (tp + step) % tp_count
        copy = pltpu.make_async_remote_copy(
            src_ref=partial_v.at[to],
            dst_ref=partial_in.at[step - 1],
            send_sem=sum_send.at[step - 1],
            recv_sem=sum_recv.at[step - 1],
            device_id=(me, to),
            device_id_type=MESH,
        )
        copy.start()
        sums.append(copy)

    for copy in sums:
        copy.wait_recv()
    latent = partial_v[tp] + partial_in[0] + partial_in[1] + partial_in[2]
    content = latent[:, :LATENT]
    rotary = latent[:, LATENT:]
    inverse = lax.rsqrt(jnp.mean(content * content, axis=1, keepdims=True) + EPSILON)
    normed = content * inverse * gain[...]
    row = lax.broadcasted_iota(jnp.int32, (2 * piece, ROPE), 0)
    lane = lax.broadcasted_iota(jnp.int32, (2 * piece, ROPE), 1)
    token = (row // piece) * BLOCK + tp * piece + row % piece
    angles = (prefix[me] * BLOCK + token).astype(jnp.float32) * frequency[...]
    turned_by = jnp.concatenate([rotary[:, ROPE // 2 :], rotary[:, : ROPE // 2]], axis=1)
    sine = jnp.where(lane < ROPE // 2, -1.0, 1.0) * jnp.sin(angles)
    turned = rotary * jnp.cos(angles) + turned_by * sine
    row512 = lax.broadcasted_iota(jnp.int32, (2 * piece, LATENT), 0)
    token512 = (row512 // piece) * BLOCK + tp * piece + row512 % piece
    normed = jnp.where(token512 < length[me], normed, 0.0).astype(jnp.bfloat16)
    turned = jnp.where(token < length[me], turned, 0.0)
    fresh_at = 2 * ((core * 4 + z) * 4 + x)
    plain = jnp.zeros((piece, WIDE - WIDTH), jnp.float32)
    for b in range(2):
        rows = slice(b * piece, (b + 1) * piece)
        last = jnp.concatenate([turned[rows], plain], axis=1).astype(jnp.bfloat16)
        fresh_in[fresh_at + b, :, :LATENT] = normed[rows]
        fresh_in[fresh_at + b, :, LATENT:] = last[:, :ROPE]
        keys[b, (groups - 1) * piece : groups * piece, :LATENT] = normed[rows]
        keys[b, (groups - 1) * piece : groups * piece, LATENT:] = last

    def along_x(step):
        here = fresh_in.at[pl.ds(fresh_place(core, z, x), 2)]
        to = (((x + step) % 4) * 4 + z) * 2 + core
        return pltpu.make_async_remote_copy(
            src_ref=here,
            dst_ref=here,
            send_sem=fresh_send.at[step - 1],
            recv_sem=fresh_recv.at[step - 1],
            device_id=(to, tp),
            device_id_type=MESH,
        )

    def along_z(step):
        here = fresh_in.at[pl.ds(fresh_place(core, z, 0), 8)]
        to = (x * 4 + (z + step) % 4) * 2 + core
        return pltpu.make_async_remote_copy(
            src_ref=here,
            dst_ref=here,
            send_sem=fresh_send.at[step + 2],
            recv_sem=fresh_recv.at[step + 2],
            device_id=(to, tp),
            device_id_type=MESH,
        )

    def to_other_core():
        here = fresh_in.at[pl.ds(fresh_place(core, 0, 0), 32)]
        return pltpu.make_async_remote_copy(
            src_ref=here,
            dst_ref=here,
            send_sem=fresh_send.at[6],
            recv_sem=fresh_recv.at[6],
            device_id=((x * 4 + z) * 2 + 1 - core, tp),
            device_id_type=MESH,
        )

    for step in range(1, 4):
        along_x(step).start()

    lane_mark = lax.broadcasted_iota(jnp.int32, (piece, WIDE - WIDTH), 1)

    def gather_blocks(parity):
        others = arrived[parity].at[pl.ds(0, pool_count - 1)]
        pltpu.make_async_copy(others, others, block_recv.at[parity]).wait()
        if parity == 0:
            send_blocks(1)

        @pl.loop(0, groups - 1)
        def _(k):
            block = arrived[parity][holder[me, 2 * k + parity]]
            mark = jnp.where(2 * k + parity < prefix[me], 0.0, HIDDEN)
            marks = jnp.where(lane_mark == 0, mark, 0.0).astype(jnp.bfloat16)
            rows = pl.ds(pl.multiple_of(k * piece, piece), piece)
            keys[parity, rows, :LATENT] = block[:, :LATENT]
            keys[parity, rows, LATENT:] = jnp.concatenate([block[:, LATENT:], marks], axis=1)

        for part in range(2):
            for side in range(2):
                near_copy(parity, part, side).start()

    neighbours = (ahead, behind)
    third = HALF // 2

    def near_copy(parity, part, side):
        return pltpu.make_async_remote_copy(
            src_ref=keys.at[parity, pl.ds(part * third, third)],
            dst_ref=keys.at[2 * parity + part, pl.ds(HALF + side * third, third)],
            send_sem=near_send.at[parity, part, side],
            recv_sem=near_recv.at[parity, part, side],
            device_id=(me, neighbours[side]),
            device_id_type=MESH,
        )

    def far_copy(parity, side):
        return pltpu.make_async_remote_copy(
            src_ref=keys.at[2 * parity + side, pl.ds(HALF + side * third, third)],
            dst_ref=keys.at[2 + parity, pl.ds(side * third, third)],
            send_sem=far_send.at[parity, side],
            recv_sem=far_recv.at[parity, side],
            device_id=(me, neighbours[side]),
            device_id_type=MESH,
        )

    def take(parity, part):
        for side in range(2):
            near_copy(parity, part, side).wait_recv()
        far_copy(parity, part).start()

    def take_far(parity):
        for side in range(2):
            far_copy(parity, side).wait_recv()

    mark_lane = lax.broadcasted_iota(jnp.int32, (SUFFIX, WIDE - WIDTH), 1)
    one_mark = jnp.where(mark_lane == 0, 1.0, 0.0).astype(jnp.bfloat16)

    def turn(head):
        rows = pl.ds(pl.multiple_of(head * SUFFIX, SUFFIX), SUFFIX)
        turned_query = queries_in[head].T
        queries[rows, :LATENT] = turned_query[:, :LATENT]
        queries[rows, LATENT:] = jnp.concatenate([turned_query[:, LATENT:], one_mark], axis=1)

    loads[3].wait()
    early = heads * 5 // 8

    @pl.loop(0, early)
    def _(head):
        turn(head)

    gather_blocks(0)

    @pl.loop(early, heads)
    def _(head):
        turn(head)

    acc[...] = jnp.zeros_like(acc)
    norm[...] = jnp.zeros_like(norm)
    high[...] = jnp.full(high.shape, LOWEST, jnp.float32)

    lane = lax.broadcasted_iota(jnp.int32, (SUFFIX, 128), 1)
    row_token = lax.broadcasted_iota(jnp.int32, (SUFFIX, 128), 0)
    new_lane = lane - (128 - piece)

    def score(tile, place):
        rows = slice(tile * ROWS, (tile + 1) * ROWS)
        scores[place][...] = jnp.dot(
            queries[rows, :], keys_t[...], preferred_element_type=jnp.float32
        )

    def weigh(tile, place):
        for start in range(0, ROWS, STRIP):
            rows = slice(start, start + STRIP)
            all_rows = slice(tile * ROWS + start, tile * ROWS + start + STRIP)
            tokens_of = slice(start % SUFFIX, start % SUFFIX + STRIP)
            parts = [scores[place][rows, j * 128 : (j + 1) * 128] for j in range(4)]
            for j in range(1, 4):
                parts[j] = parts[j] + bias[j - 1, tokens_of, :]
            top = functools.reduce(jnp.maximum, parts)
            top = jnp.max(top, axis=1, keepdims=True) * SCALE
            old = high[all_rows, :]
            top = jnp.maximum(old, top)
            fade = jnp.exp2(old - top)
            raised = [jnp.exp2(part * SCALE - top) for part in parts]
            high[all_rows, :] = top
            decay[place][rows, :] = fade
            norm[all_rows, :] = norm[all_rows, :] * fade + functools.reduce(jnp.add, raised)
            for j in range(4):
                weights[place][rows, j * 128 : (j + 1) * 128] = raised[j].astype(jnp.bfloat16)

    def mix(tile, place, step):
        rows = slice(tile * ROWS, (tile + 1) * ROWS)
        mixed = jnp.dot(
            weights[place][...], keys[step, :, :LATENT], preferred_element_type=jnp.float32
        )
        for j in range(LATENT // 128):
            lanes = slice(j * 128, (j + 1) * 128)
            acc[rows, lanes] = acc[rows, lanes] * decay[place][...] + mixed[:, lanes]

    @pl.loop(0, 4)
    def _(step):
        @pl.when(step == 0)
        def _():
            take(0, 0)

        @pl.when(step == 1)
        def _():
            gather_blocks(1)
            take(0, 1)
            for hop in range(1, 4):
                along_x(hop).wait_recv()
            for hop in range(1, 4):
                along_z(hop).start()

        @pl.when(step == 2)
        def _():
            take(1, 0)
            take(1, 1)
            take_far(0)
            for hop in range(1, 4):
                along_z(hop).wait_recv()
            to_other_core().start()

        @pl.when(step == 3)
        def _():
            take_far(1)

        first_part = (step % 2) * BLOCK + jnp.where(step < 2, tp, across) * piece
        near_part = (step // 2) * BLOCK
        shown = (1 - step % 2) * -1000
        bases = (first_part, near_part + behind * piece + shown, near_part + ahead * piece + shown)
        for j, base in enumerate(bases):
            hide = (new_lane >= 0) & (base + new_lane > row_token)
            bias[j] = jnp.where(hide, HIDDEN, 0.0)
        keys_t[...] = keys[step].T

        tiles = queries.shape[0] // ROWS
        score(0, 0)
        for tile in range(tiles):
            if tile + 1 < tiles:
                score(tile + 1, (tile + 1) % 2)
            weigh(tile, tile % 2)
            mix(tile, tile % 2, step)

    loads[4].wait()
    live = lax.broadcasted_iota(jnp.int32, (SUFFIX, VALUE_DIM), 0) < length[me]

    @pl.loop(0, heads // 4)
    def _(quad):
        for inner in range(4):
            head = quad * 4 + inner
            rows = pl.ds(pl.multiple_of(head * SUFFIX, SUFFIX), SUFFIX)
            share = 1.0 / jnp.sum(norm[rows, :], axis=1, keepdims=True)
            mixed = (acc[rows, :] * share).astype(jnp.bfloat16)
            value = jnp.dot(mixed, value_v[head], preferred_element_type=jnp.float32)
            columns = pl.ds(pl.multiple_of(head * VALUE_DIM, VALUE_DIM), VALUE_DIM)
            out_v[:, columns] = jnp.where(live, value, 0.0).astype(jnp.bfloat16)

    store_out = pltpu.make_async_copy(out_v, out_h, load_sem.at[1])
    store_out.start()

    lane_slot = lax.broadcasted_iota(jnp.int32, (8, 128), 1)

    def mark_slot(request, index):
        for b in range(2):
            entry = prefix[request] + b
            here = holder[request, entry] == me
            target = jnp.where(here, slot[request, entry], -1)
            index = jnp.where(lane_slot == target, fresh_place(request % 2, (request // 2) % 4, request // 8) + b, index)
        return index

    index_v[...] = lax.fori_loop(0, pool_count, mark_slot, jnp.full((8, 128), -1, jnp.int32))
    to_scalars = pltpu.make_async_copy(index_v, index_s, index_sem)
    to_scalars.start()
    to_other_core().wait_recv()
    to_scalars.wait()

    @pl.loop(0, slots)
    def _(place):
        at = index_s[0, place]
        replaced = jnp.where(at >= 0, 1.0, 0.0)
        kept = pool_v[place]
        taken = fresh_in[jnp.maximum(at, 0)]
        new_pool_v[place] = jnp.where(replaced > 0.5, taken, kept)

    store_pool = pltpu.make_async_copy(new_pool_v, new_pool_h, load_sem.at[0])
    store_pool.start()


    for copy in sums:
        copy.wait_send()
    for parity in range(2):
        sent = arrived[parity].at[pl.ds(0, pool_count - 1)]
        pltpu.make_async_copy(sent, sent, block_send.at[parity]).wait()
        for side in range(2):
            for part in range(2):
                near_copy(parity, part, side).wait_send()
            far_copy(parity, side).wait_send()
    for step in range(1, 4):
        along_x(step).wait_send()
        along_z(step).wait_send()
    to_other_core().wait_send()
    store_pool.wait()
    store_out.wait()


def fresh_place(at_core, at_z, at_x):
    return 2 * ((at_core * 4 + at_z) * 4 + at_x)


def on_device(
    pool_count,
    tp_count,
    tokens,
    down_weight,
    kv_gain,
    queries,
    value_weight,
    pool,
    block_holder,
    block_slot,
    prefix_blocks,
    suffix_len,
):
    heads = queries.shape[1]
    piece = pool.shape[1]
    rows = SUFFIX * heads
    exponent = np.arange(ROPE // 2).astype(np.float32) * np.float32(2.0 / ROPE)
    inverse_frequency = np.power(np.float32(10000.0), -exponent).astype(np.float32)
    frequency = np.tile(inverse_frequency, 2)[None, :]
    bf16, f32 = jnp.bfloat16, jnp.float32
    smem = pl.BlockSpec(memory_space=pltpu.SMEM)
    vmem = pl.BlockSpec(memory_space=pltpu.VMEM)
    anywhere = pl.BlockSpec(memory_space=pl.ANY)
    dma = pltpu.SemaphoreType.DMA
    return pl.pallas_call(
        functools.partial(kernel, pool_count, tp_count),
        out_shape=(
            jax.ShapeDtypeStruct((SUFFIX, heads * VALUE_DIM), bf16),
            jax.ShapeDtypeStruct(pool.shape, bf16),
        ),
        in_specs=[smem] * 4 + [vmem] * 2 + [anywhere] * 5,
        out_specs=(anywhere, anywhere),
        scratch_shapes=[
            pltpu.VMEM(tokens.shape, bf16),
            pltpu.VMEM(down_weight.shape[::-1], bf16),
            pltpu.VMEM((heads, WIDTH, SUFFIX), bf16),
            pltpu.VMEM((rows, WIDE), bf16),
            pltpu.VMEM(value_weight.shape, bf16),
            pltpu.VMEM(pool.shape, bf16),
            pltpu.VMEM((2, pool_count, piece, WIDTH), bf16),
            pltpu.VMEM((pool_count, piece, WIDTH), bf16),
            pltpu.VMEM((pool_count, piece, WIDTH), bf16),
            pltpu.VMEM((tp_count, 2 * piece, WIDTH), f32),
            pltpu.VMEM((tp_count - 1, 2 * piece, WIDTH), f32),
            pltpu.VMEM((2 * pool_count, piece, WIDTH), bf16),
            pltpu.VMEM((4, 2 * HALF, WIDE), bf16),
            pltpu.VMEM((WIDE, 2 * HALF), bf16),
            pltpu.VMEM((3, SUFFIX, 128), f32),
            pltpu.VMEM((ROWS, 2 * HALF), f32),
            pltpu.VMEM((ROWS, 2 * HALF), f32),
            pltpu.VMEM((ROWS, 2 * HALF), bf16),
            pltpu.VMEM((ROWS, 2 * HALF), bf16),
            pltpu.VMEM((ROWS, 128), f32),
            pltpu.VMEM((ROWS, 128), f32),
            pltpu.VMEM((rows, LATENT), f32),
            pltpu.VMEM((rows, 128), f32),
            pltpu.VMEM((rows, 128), f32),
            pltpu.VMEM((SUFFIX, heads * VALUE_DIM), bf16),
            pltpu.VMEM(pool.shape, bf16),
            pltpu.VMEM((8, 128), jnp.int32),
            pltpu.SMEM((8, 128), jnp.int32),
            pltpu.SMEM((pool_count,), jnp.int32),
            dma((5,)),
            dma,
            dma((2,)),
            dma((2,)),
            dma((tp_count - 1,)),
            dma((tp_count - 1,)),
            dma((7,)),
            dma((7,)),
            dma((2, 2, 2)),
            dma((2, 2, 2)),
            dma((2, 2)),
            dma((2, 2)),
        ],
        compiler_params=pltpu.CompilerParams(
            collective_id=0, has_side_effects=True, vmem_limit_bytes=60 * 1024 * 1024
        ),
        name="latent_attention",
    )(
        block_holder,
        block_slot,
        prefix_blocks,
        suffix_len,
        kv_gain.reshape(1, LATENT),
        jnp.asarray(frequency),
        tokens,
        down_weight.T,
        queries.transpose(1, 2, 0),
        value_weight,
        pool,
    )


def solution(mesh):
    in_specs = (
        P("pool", "tp"),
        P("tp", None),
        P(),
        P("pool", "tp", None),
        P("tp", None, None),
        P("pool", "tp", None),
        P(),
        P(),
        P(),
        P(),
    )
    out_specs = (P("pool", "tp"), P("pool", "tp", None))
    return jax.shard_map(
        functools.partial(on_device, mesh.shape["pool"], mesh.shape["tp"]),
        mesh=mesh,
        in_specs=in_specs,
        out_specs=out_specs,
        check_vma=False,
    )
```

```python
import functools
import math

import jax
import jax.numpy as jnp
import numpy as np
from jax import lax
from jax.experimental import pallas as pl
from jax.experimental.pallas import tpu as pltpu
from jax.sharding import PartitionSpec as P

LATENT = 512
VALUE_DIM = 128
BLOCK = 64
SUFFIX = 128
TABLE = 32
WIDTH = 576
WIDE = 640
ROPE = WIDTH - LATENT
HALF = 256
SCALE = 192.0 ** (-0.5) * math.log2(math.e)
HIDDEN = -1e30
EPSILON = 1e-06
ROWS = 256
STRIP = 32
LOWEST = -3e38
MESH = pl.DeviceIdType.MESH


def kernel(
    pool_count,
    tp_count,
    holder,
    slot,
    prefix,
    length,
    gain,
    frequency,
    tokens_h,
    down_h,
    queries_h,
    value_h,
    pool_h,
    out_h,
    new_pool_h,
    tokens_v,
    down_v,
    queries_in,
    queries,
    value_v,
    pool_v,
    leaving,
    arrived_even,
    arrived_odd,
    partial_v,
    partial_in,
    fresh_in,
    keys,
    keys_t,
    bias,
    scores_a,
    scores_b,
    weights_a,
    weights_b,
    decay_a,
    decay_b,
    acc,
    high,
    norm,
    out_v,
    new_pool_v,
    index_v,
    index_s,
    entry_s,
    load_sem,
    index_sem,
    block_send,
    block_recv,
    sum_send,
    sum_recv,
    fresh_send,
    fresh_recv,
    near_send,
    near_recv,
    far_send,
    far_recv,
):
    me = lax.axis_index("pool")
    tp = lax.axis_index("tp")
    core, z, x = me % 2, (me // 2) % 4, me // 8
    ahead, behind = (tp + 1) % tp_count, (tp + tp_count - 1) % tp_count
    across = (tp + 2) % tp_count
    heads = queries_in.shape[0]
    slots = pool_v.shape[0]
    piece = pool_v.shape[1]
    groups = TABLE // 2
    arrived = (arrived_even, arrived_odd)
    scores, weights = (scores_a, scores_b), (weights_a, weights_b)
    decay = (decay_a, decay_b)

    def peer(step):
        to_core = (core + step % 2) % 2
        to_z = (z + (step // 2) % 4) % 4
        to_x = (x + step // 8) % 4
        return (to_x * 4 + to_z) * 2 + to_core

    loads = [
        pltpu.make_async_copy(pool_h, pool_v, load_sem.at[0]),
        pltpu.make_async_copy(tokens_h, tokens_v, load_sem.at[1]),
        pltpu.make_async_copy(down_h, down_v, load_sem.at[2]),
        pltpu.make_async_copy(queries_h, queries_in, load_sem.at[3]),
        pltpu.make_async_copy(value_h, value_v, load_sem.at[4]),
    ]
    for load in loads:
        load.start()

    barrier = pltpu.get_barrier_semaphore()

    @pl.loop(1, pool_count)
    def _(step):
        pl.semaphore_signal(barrier, inc=1, device_id=(peer(step), tp), device_id_type=MESH)

    for step in range(1, tp_count):
        pl.semaphore_signal(
            barrier, inc=1, device_id=(me, (tp + step) % tp_count), device_id_type=MESH
        )

    loads[0].wait()

    @pl.loop(0, pool_count)
    def _(request):
        at = jnp.int32(0)
        for k in range(groups - 1):
            at = jnp.where(holder[request, 2 * k] == me, 2 * k, at)
        entry_s[request] = at
        leaving[0, request] = pool_v[slot[request, at]]

    arrived[0][me] = pool_v[slot[me, entry_s[me]]]

    pl.semaphore_wait(barrier, pool_count - 1 + tp_count - 1)

    def send_blocks(parity):
        @pl.loop(1, pool_count)
        def _(step):
            request = peer(step)
            pltpu.make_async_remote_copy(
                src_ref=leaving.at[parity, request],
                dst_ref=arrived[parity].at[me],
                send_sem=block_send.at[parity],
                recv_sem=block_recv.at[parity],
                device_id=(request, tp),
                device_id_type=MESH,
            ).start()

    send_blocks(0)

    @pl.loop(0, pool_count)
    def _(request):
        leaving[1, request] = pool_v[slot[request, entry_s[request] + 1]]

    arrived[1][me] = pool_v[slot[me, entry_s[me] + 1]]

    loads[1].wait()
    loads[2].wait()
    partial = lax.dot_general(
        tokens_v[...], down_v[...], (((1,), (1,)), ((), ())), preferred_element_type=jnp.float32
    )
    for owner in range(tp_count):
        for b in range(2):
            partial_v[owner, b * piece : (b + 1) * piece, :] = partial[
                b * BLOCK + owner * piece : b * BLOCK + (owner + 1) * piece, :
            ]
    sums = []
    for step in range(1, tp_count):
        to = (tp + step) % tp_count
        copy = pltpu.make_async_remote_copy(
            src_ref=partial_v.at[to],
            dst_ref=partial_in.at[step - 1],
            send_sem=sum_send.at[step - 1],
            recv_sem=sum_recv.at[step - 1],
            device_id=(me, to),
            device_id_type=MESH,
        )
        copy.start()
        sums.append(copy)

    for copy in sums:
        copy.wait_recv()
    latent = partial_v[tp] + partial_in[0] + partial_in[1] + partial_in[2]
    content = latent[:, :LATENT]
    rotary = latent[:, LATENT:]
    inverse = lax.rsqrt(jnp.mean(content * content, axis=1, keepdims=True) + EPSILON)
    normed = content * inverse * gain[...]
    row = lax.broadcasted_iota(jnp.int32, (2 * piece, ROPE), 0)
    lane = lax.broadcasted_iota(jnp.int32, (2 * piece, ROPE), 1)
    token = (row // piece) * BLOCK + tp * piece + row % piece
    angles = (prefix[me] * BLOCK + token).astype(jnp.float32) * frequency[...]
    turned_by = jnp.concatenate([rotary[:, ROPE // 2 :], rotary[:, : ROPE // 2]], axis=1)
    sine = jnp.where(lane < ROPE // 2, -1.0, 1.0) * jnp.sin(angles)
    turned = rotary * jnp.cos(angles) + turned_by * sine
    row512 = lax.broadcasted_iota(jnp.int32, (2 * piece, LATENT), 0)
    token512 = (row512 // piece) * BLOCK + tp * piece + row512 % piece
    normed = jnp.where(token512 < length[me], normed, 0.0).astype(jnp.bfloat16)
    turned = jnp.where(token < length[me], turned, 0.0)
    fresh_at = 2 * ((core * 4 + z) * 4 + x)
    plain = jnp.zeros((piece, WIDE - WIDTH), jnp.float32)
    for b in range(2):
        rows = slice(b * piece, (b + 1) * piece)
        last = jnp.concatenate([turned[rows], plain], axis=1).astype(jnp.bfloat16)
        fresh_in[fresh_at + b, :, :LATENT] = normed[rows]
        fresh_in[fresh_at + b, :, LATENT:] = last[:, :ROPE]
        keys[b, (groups - 1) * piece : groups * piece, :LATENT] = normed[rows]
        keys[b, (groups - 1) * piece : groups * piece, LATENT:] = last

    def along_x(step):
        here = fresh_in.at[pl.ds(fresh_place(core, z, x), 2)]
        to = (((x + step) % 4) * 4 + z) * 2 + core
        return pltpu.make_async_remote_copy(
            src_ref=here,
            dst_ref=here,
            send_sem=fresh_send.at[step - 1],
            recv_sem=fresh_recv.at[step - 1],
            device_id=(to, tp),
            device_id_type=MESH,
        )

    def along_z(step):
        here = fresh_in.at[pl.ds(fresh_place(core, z, 0), 8)]
        to = (x * 4 + (z + step) % 4) * 2 + core
        return pltpu.make_async_remote_copy(
            src_ref=here,
            dst_ref=here,
            send_sem=fresh_send.at[step + 2],
            recv_sem=fresh_recv.at[step + 2],
            device_id=(to, tp),
            device_id_type=MESH,
        )

    def to_other_core():
        here = fresh_in.at[pl.ds(fresh_place(core, 0, 0), 32)]
        return pltpu.make_async_remote_copy(
            src_ref=here,
            dst_ref=here,
            send_sem=fresh_send.at[6],
            recv_sem=fresh_recv.at[6],
            device_id=((x * 4 + z) * 2 + 1 - core, tp),
            device_id_type=MESH,
        )

    for step in range(1, 4):
        along_x(step).start()

    lane_mark = lax.broadcasted_iota(jnp.int32, (piece, WIDE - WIDTH), 1)

    def gather_blocks(parity):
        others = arrived[parity].at[pl.ds(0, pool_count - 1)]
        pltpu.make_async_copy(others, others, block_recv.at[parity]).wait()
        if parity == 0:
            send_blocks(1)

        @pl.loop(0, groups - 1)
        def _(k):
            block = arrived[parity][holder[me, 2 * k + parity]]
            mark = jnp.where(2 * k + parity < prefix[me], 0.0, HIDDEN)
            marks = jnp.where(lane_mark == 0, mark, 0.0).astype(jnp.bfloat16)
            rows = pl.ds(pl.multiple_of(k * piece, piece), piece)
            keys[parity, rows, :LATENT] = block[:, :LATENT]
            keys[parity, rows, LATENT:] = jnp.concatenate([block[:, LATENT:], marks], axis=1)

        for part in range(2):
            for side in range(2):
                near_copy(parity, part, side).start()

    neighbours = (ahead, behind)
    third = HALF // 2

    def near_copy(parity, part, side):
        return pltpu.make_async_remote_copy(
            src_ref=keys.at[parity, pl.ds(part * third, third)],
            dst_ref=keys.at[2 * parity + part, pl.ds(HALF + side * third, third)],
            send_sem=near_send.at[parity, part, side],
            recv_sem=near_recv.at[parity, part, side],
            device_id=(me, neighbours[side]),
            device_id_type=MESH,
        )

    def far_copy(parity, side):
        return pltpu.make_async_remote_copy(
            src_ref=keys.at[2 * parity + side, pl.ds(HALF + side * third, third)],
            dst_ref=keys.at[2 + parity, pl.ds(side * third, third)],
            send_sem=far_send.at[parity, side],
            recv_sem=far_recv.at[parity, side],
            device_id=(me, neighbours[side]),
            device_id_type=MESH,
        )

    def take(parity, part):
        for side in range(2):
            near_copy(parity, part, side).wait_recv()
        far_copy(parity, part).start()

    def take_far(parity):
        for side in range(2):
            far_copy(parity, side).wait_recv()

    mark_lane = lax.broadcasted_iota(jnp.int32, (SUFFIX, WIDE - WIDTH), 1)
    one_mark = jnp.where(mark_lane == 0, 1.0, 0.0).astype(jnp.bfloat16)

    def turn(head):
        rows = pl.ds(pl.multiple_of(head * SUFFIX, SUFFIX), SUFFIX)
        turned_query = queries_in[head].T
        queries[rows, :LATENT] = turned_query[:, :LATENT]
        queries[rows, LATENT:] = jnp.concatenate([turned_query[:, LATENT:], one_mark], axis=1)

    lane_slot = lax.broadcasted_iota(jnp.int32, (8, 128), 1)

    def mark_slot(request, index):
        for b in range(2):
            entry = prefix[request] + b
            here = holder[request, entry] == me
            target = jnp.where(here, slot[request, entry], -1)
            index = jnp.where(lane_slot == target, fresh_place(request % 2, (request // 2) % 4, request // 8) + b, index)
        return index

    index_v[...] = lax.fori_loop(0, pool_count, mark_slot, jnp.full((8, 128), -1, jnp.int32))
    to_scalars = pltpu.make_async_copy(index_v, index_s, index_sem)
    to_scalars.start()

    loads[3].wait()
    early = heads * 5 // 8

    @pl.loop(0, early)
    def _(head):
        turn(head)

    gather_blocks(0)

    @pl.loop(early, heads)
    def _(head):
        turn(head)

    acc[...] = jnp.zeros_like(acc)
    norm[...] = jnp.zeros_like(norm)
    high[...] = jnp.full(high.shape, LOWEST, jnp.float32)

    lane = lax.broadcasted_iota(jnp.int32, (SUFFIX, 128), 1)
    row_token = lax.broadcasted_iota(jnp.int32, (SUFFIX, 128), 0)
    new_lane = lane - (128 - piece)

    def score(tile, place):
        rows = pl.ds(pl.multiple_of(tile * ROWS, ROWS), ROWS)
        scores[place][...] = jnp.dot(
            queries[rows, :], keys_t[...], preferred_element_type=jnp.float32
        )

    def weigh(tile, place):
        for start in range(0, ROWS, STRIP):
            rows = slice(start, start + STRIP)
            all_rows = pl.ds(pl.multiple_of(tile * ROWS + start, STRIP), STRIP)
            tokens_of = slice(start % SUFFIX, start % SUFFIX + STRIP)
            parts = [scores[place][rows, j * 128 : (j + 1) * 128] for j in range(4)]
            for j in range(1, 4):
                parts[j] = parts[j] + bias[j - 1, tokens_of, :]
            top = functools.reduce(jnp.maximum, parts)
            top = jnp.max(top, axis=1, keepdims=True) * SCALE
            old = high[all_rows, :]
            top = jnp.maximum(old, top)
            fade = jnp.exp2(old - top)
            raised = [jnp.exp2(part * SCALE - top) for part in parts]
            high[all_rows, :] = top
            decay[place][rows, :] = fade
            norm[all_rows, :] = norm[all_rows, :] * fade + functools.reduce(jnp.add, raised)
            for j in range(4):
                weights[place][rows, j * 128 : (j + 1) * 128] = raised[j].astype(jnp.bfloat16)

    def mix(tile, place, step):
        rows = pl.ds(pl.multiple_of(tile * ROWS, ROWS), ROWS)
        mixed = jnp.dot(
            weights[place][...], keys[step, :, :LATENT], preferred_element_type=jnp.float32
        )
        for j in range(LATENT // 128):
            lanes = slice(j * 128, (j + 1) * 128)
            acc[rows, lanes] = acc[rows, lanes] * decay[place][...] + mixed[:, lanes]

    @pl.loop(0, 4)
    def _(step):
        @pl.when(step == 0)
        def _():
            take(0, 0)

        @pl.when(step == 1)
        def _():
            gather_blocks(1)
            take(0, 1)
            for hop in range(1, 4):
                along_x(hop).wait_recv()
            for hop in range(1, 4):
                along_z(hop).start()

        @pl.when(step == 2)
        def _():
            take(1, 0)
            take(1, 1)
            take_far(0)
            for hop in range(1, 4):
                along_z(hop).wait_recv()
            to_other_core().start()

        @pl.when(step == 3)
        def _():
            take_far(1)

        first_part = (step % 2) * BLOCK + jnp.where(step < 2, tp, across) * piece
        near_part = (step // 2) * BLOCK
        shown = (1 - step % 2) * -1000
        bases = (first_part, near_part + behind * piece + shown, near_part + ahead * piece + shown)
        for j, base in enumerate(bases):
            hide = (new_lane >= 0) & (base + new_lane > row_token)
            bias[j] = jnp.where(hide, HIDDEN, 0.0)
        keys_t[...] = keys[step].T

        def two_tiles(tile, more):
            score(tile + 1, 1)
            weigh(tile, 0)
            mix(tile, 0, step)
            if more:
                score(tile + 2, 0)
            weigh(tile + 1, 1)
            mix(tile + 1, 1, step)

        tiles = queries.shape[0] // ROWS
        score(0, 0)

        @pl.loop(0, tiles // 2 - 1)
        def _(pair):
            two_tiles(2 * pair, True)

        two_tiles(tiles - 2, False)

    loads[4].wait()
    live = lax.broadcasted_iota(jnp.int32, (SUFFIX, VALUE_DIM), 0) < length[me]

    @pl.loop(0, heads // 4)
    def _(quad):
        for inner in range(4):
            head = quad * 4 + inner
            rows = pl.ds(pl.multiple_of(head * SUFFIX, SUFFIX), SUFFIX)
            share = 1.0 / jnp.sum(norm[rows, :], axis=1, keepdims=True)
            mixed = (acc[rows, :] * share).astype(jnp.bfloat16)
            value = jnp.dot(mixed, value_v[head], preferred_element_type=jnp.float32)
            columns = pl.ds(pl.multiple_of(head * VALUE_DIM, VALUE_DIM), VALUE_DIM)
            out_v[:, columns] = jnp.where(live, value, 0.0).astype(jnp.bfloat16)

    store_out = pltpu.make_async_copy(out_v, out_h, load_sem.at[1])
    store_out.start()

    to_other_core().wait_recv()
    to_scalars.wait()

    @pl.loop(0, slots)
    def _(place):
        at = index_s[0, place]
        replaced = jnp.where(at >= 0, 1.0, 0.0)
        kept = pool_v[place]
        taken = fresh_in[jnp.maximum(at, 0)]
        new_pool_v[place] = jnp.where(replaced > 0.5, taken, kept)

    store_pool = pltpu.make_async_copy(new_pool_v, new_pool_h, load_sem.at[0])
    store_pool.start()


    for copy in sums:
        copy.wait_send()
    for parity in range(2):
        sent = arrived[parity].at[pl.ds(0, pool_count - 1)]
        pltpu.make_async_copy(sent, sent, block_send.at[parity]).wait()
        for side in range(2):
            for part in range(2):
                near_copy(parity, part, side).wait_send()
            far_copy(parity, side).wait_send()
    for step in range(1, 4):
        along_x(step).wait_send()
        along_z(step).wait_send()
    to_other_core().wait_send()
    store_pool.wait()
    store_out.wait()


def fresh_place(at_core, at_z, at_x):
    return 2 * ((at_core * 4 + at_z) * 4 + at_x)


def on_device(
    pool_count,
    tp_count,
    tokens,
    down_weight,
    kv_gain,
    queries,
    value_weight,
    pool,
    block_holder,
    block_slot,
    prefix_blocks,
    suffix_len,
):
    heads = queries.shape[1]
    piece = pool.shape[1]
    rows = SUFFIX * heads
    exponent = np.arange(ROPE // 2).astype(np.float32) * np.float32(2.0 / ROPE)
    inverse_frequency = np.power(np.float32(10000.0), -exponent).astype(np.float32)
    frequency = np.tile(inverse_frequency, 2)[None, :]
    bf16, f32 = jnp.bfloat16, jnp.float32
    smem = pl.BlockSpec(memory_space=pltpu.SMEM)
    vmem = pl.BlockSpec(memory_space=pltpu.VMEM)
    anywhere = pl.BlockSpec(memory_space=pl.ANY)
    dma = pltpu.SemaphoreType.DMA
    return pl.pallas_call(
        functools.partial(kernel, pool_count, tp_count),
        out_shape=(
            jax.ShapeDtypeStruct((SUFFIX, heads * VALUE_DIM), bf16),
            jax.ShapeDtypeStruct(pool.shape, bf16),
        ),
        in_specs=[smem] * 4 + [vmem] * 2 + [anywhere] * 5,
        out_specs=(anywhere, anywhere),
        scratch_shapes=[
            pltpu.VMEM(tokens.shape, bf16),
            pltpu.VMEM(down_weight.shape[::-1], bf16),
            pltpu.VMEM((heads, WIDTH, SUFFIX), bf16),
            pltpu.VMEM((rows, WIDE), bf16),
            pltpu.VMEM(value_weight.shape, bf16),
            pltpu.VMEM(pool.shape, bf16),
            pltpu.VMEM((2, pool_count, piece, WIDTH), bf16),
            pltpu.VMEM((pool_count, piece, WIDTH), bf16),
            pltpu.VMEM((pool_count, piece, WIDTH), bf16),
            pltpu.VMEM((tp_count, 2 * piece, WIDTH), f32),
            pltpu.VMEM((tp_count - 1, 2 * piece, WIDTH), f32),
            pltpu.VMEM((2 * pool_count, piece, WIDTH), bf16),
            pltpu.VMEM((4, 2 * HALF, WIDE), bf16),
            pltpu.VMEM((WIDE, 2 * HALF), bf16),
            pltpu.VMEM((3, SUFFIX, 128), f32),
            pltpu.VMEM((ROWS, 2 * HALF), f32),
            pltpu.VMEM((ROWS, 2 * HALF), f32),
            pltpu.VMEM((ROWS, 2 * HALF), bf16),
            pltpu.VMEM((ROWS, 2 * HALF), bf16),
            pltpu.VMEM((ROWS, 128), f32),
            pltpu.VMEM((ROWS, 128), f32),
            pltpu.VMEM((rows, LATENT), f32),
            pltpu.VMEM((rows, 128), f32),
            pltpu.VMEM((rows, 128), f32),
            pltpu.VMEM((SUFFIX, heads * VALUE_DIM), bf16),
            pltpu.VMEM(pool.shape, bf16),
            pltpu.VMEM((8, 128), jnp.int32),
            pltpu.SMEM((8, 128), jnp.int32),
            pltpu.SMEM((pool_count,), jnp.int32),
            dma((5,)),
            dma,
            dma((2,)),
            dma((2,)),
            dma((tp_count - 1,)),
            dma((tp_count - 1,)),
            dma((7,)),
            dma((7,)),
            dma((2, 2, 2)),
            dma((2, 2, 2)),
            dma((2, 2)),
            dma((2, 2)),
        ],
        compiler_params=pltpu.CompilerParams(
            collective_id=0, has_side_effects=True, vmem_limit_bytes=60 * 1024 * 1024
        ),
        name="latent_attention",
    )(
        block_holder,
        block_slot,
        prefix_blocks,
        suffix_len,
        kv_gain.reshape(1, LATENT),
        jnp.asarray(frequency),
        tokens,
        down_weight.T,
        queries.transpose(1, 2, 0),
        value_weight,
        pool,
    )


def solution(mesh):
    in_specs = (
        P("pool", "tp"),
        P("tp", None),
        P(),
        P("pool", "tp", None),
        P("tp", None, None),
        P("pool", "tp", None),
        P(),
        P(),
        P(),
        P(),
    )
    out_specs = (P("pool", "tp"), P("pool", "tp", None))
    return jax.shard_map(
        functools.partial(on_device, mesh.shape["pool"], mesh.shape["tp"]),
        mesh=mesh,
        in_specs=in_specs,
        out_specs=out_specs,
        check_vma=False,
    )
```

```python
import functools
import math

import jax
import jax.numpy as jnp
import numpy as np
from jax import lax
from jax.experimental import pallas as pl
from jax.experimental.pallas import tpu as pltpu
from jax.sharding import PartitionSpec as P

LATENT = 512
VALUE_DIM = 128
BLOCK = 64
SUFFIX = 128
TABLE = 32
WIDTH = 576
WIDE = 640
ROPE = WIDTH - LATENT
HALF = 256
SCALE = 192.0 ** (-0.5) * math.log2(math.e)
HIDDEN = -1e30
EPSILON = 1e-06
ROWS = 1024
STRIP = 32
MESH = pl.DeviceIdType.MESH


def kernel(
    pool_count,
    tp_count,
    holder,
    slot,
    prefix,
    length,
    gain,
    frequency,
    tokens_h,
    down_h,
    queries_h,
    value_h,
    pool_h,
    out_h,
    new_pool_h,
    tokens_v,
    down_v,
    queries_in,
    queries,
    value_v,
    pool_v,
    leaving,
    arrived_even,
    arrived_odd,
    partial_v,
    partial_in,
    fresh_in,
    keys,
    keys_t,
    bias,
    scores_a,
    scores_b,
    weights_a,
    weights_b,
    decay_a,
    decay_b,
    acc,
    high,
    norm,
    out_v,
    new_pool_v,
    index_v,
    index_s,
    entry_s,
    load_sem,
    index_sem,
    block_send,
    block_recv,
    sum_send,
    sum_recv,
    fresh_send,
    fresh_recv,
    near_send,
    near_recv,
    far_send,
    far_recv,
):
    me = lax.axis_index("pool")
    tp = lax.axis_index("tp")
    core, z, x = me % 2, (me // 2) % 4, me // 8
    ahead, behind = (tp + 1) % tp_count, (tp + tp_count - 1) % tp_count
    across = (tp + 2) % tp_count
    heads = queries_in.shape[0]
    slots = pool_v.shape[0]
    piece = pool_v.shape[1]
    groups = TABLE // 2
    arrived = (arrived_even, arrived_odd)
    scores, weights = (scores_a, scores_b), (weights_a, weights_b)
    decay = (decay_a, decay_b)

    def peer(step):
        to_core = (core + step % 2) % 2
        to_z = (z + (step // 2) % 4) % 4
        to_x = (x + step // 8) % 4
        return (to_x * 4 + to_z) * 2 + to_core

    loads = [
        pltpu.make_async_copy(pool_h, pool_v, load_sem.at[0]),
        pltpu.make_async_copy(tokens_h, tokens_v, load_sem.at[1]),
        pltpu.make_async_copy(down_h, down_v, load_sem.at[2]),
        pltpu.make_async_copy(queries_h, queries_in, load_sem.at[3]),
        pltpu.make_async_copy(value_h, value_v, load_sem.at[4]),
    ]
    for load in loads:
        load.start()

    barrier = pltpu.get_barrier_semaphore()

    @pl.loop(1, pool_count)
    def _(step):
        pl.semaphore_signal(barrier, inc=1, device_id=(peer(step), tp), device_id_type=MESH)

    for step in range(1, tp_count):
        pl.semaphore_signal(
            barrier, inc=1, device_id=(me, (tp + step) % tp_count), device_id_type=MESH
        )

    loads[0].wait()

    @pl.loop(0, pool_count)
    def _(request):
        at = jnp.int32(0)
        for k in range(groups - 1):
            at = jnp.where(holder[request, 2 * k] == me, 2 * k, at)
        entry_s[request] = at
        leaving[0, request] = pool_v[slot[request, at]]

    arrived[0][me] = pool_v[slot[me, entry_s[me]]]

    pl.semaphore_wait(barrier, pool_count - 1 + tp_count - 1)

    def send_blocks(parity):
        @pl.loop(1, pool_count)
        def _(step):
            request = peer(step)
            pltpu.make_async_remote_copy(
                src_ref=leaving.at[parity, request],
                dst_ref=arrived[parity].at[me],
                send_sem=block_send.at[parity],
                recv_sem=block_recv.at[parity],
                device_id=(request, tp),
                device_id_type=MESH,
            ).start()

    send_blocks(0)

    @pl.loop(0, pool_count)
    def _(request):
        leaving[1, request] = pool_v[slot[request, entry_s[request] + 1]]

    arrived[1][me] = pool_v[slot[me, entry_s[me] + 1]]

    loads[1].wait()
    loads[2].wait()
    partial = lax.dot_general(
        tokens_v[...], down_v[...], (((1,), (1,)), ((), ())), preferred_element_type=jnp.float32
    )
    for owner in range(tp_count):
        for b in range(2):
            partial_v[owner, b * piece : (b + 1) * piece, :] = partial[
                b * BLOCK + owner * piece : b * BLOCK + (owner + 1) * piece, :
            ]
    sums = []
    for step in range(1, tp_count):
        to = (tp + step) % tp_count
        copy = pltpu.make_async_remote_copy(
            src_ref=partial_v.at[to],
            dst_ref=partial_in.at[step - 1],
            send_sem=sum_send.at[step - 1],
            recv_sem=sum_recv.at[step - 1],
            device_id=(me, to),
            device_id_type=MESH,
        )
        copy.start()
        sums.append(copy)

    for copy in sums:
        copy.wait_recv()
    latent = partial_v[tp] + partial_in[0] + partial_in[1] + partial_in[2]
    content = latent[:, :LATENT]
    rotary = latent[:, LATENT:]
    inverse = lax.rsqrt(jnp.mean(content * content, axis=1, keepdims=True) + EPSILON)
    normed = content * inverse * gain[...]
    row = lax.broadcasted_iota(jnp.int32, (2 * piece, ROPE), 0)
    lane = lax.broadcasted_iota(jnp.int32, (2 * piece, ROPE), 1)
    token = (row // piece) * BLOCK + tp * piece + row % piece
    angles = (prefix[me] * BLOCK + token).astype(jnp.float32) * frequency[...]
    turned_by = jnp.concatenate([rotary[:, ROPE // 2 :], rotary[:, : ROPE // 2]], axis=1)
    sine = jnp.where(lane < ROPE // 2, -1.0, 1.0) * jnp.sin(angles)
    turned = rotary * jnp.cos(angles) + turned_by * sine
    row512 = lax.broadcasted_iota(jnp.int32, (2 * piece, LATENT), 0)
    token512 = (row512 // piece) * BLOCK + tp * piece + row512 % piece
    normed = jnp.where(token512 < length[me], normed, 0.0).astype(jnp.bfloat16)
    turned = jnp.where(token < length[me], turned, 0.0)
    fresh_at = 2 * ((core * 4 + z) * 4 + x)
    plain = jnp.zeros((piece, WIDE - WIDTH), jnp.float32)
    for b in range(2):
        rows = slice(b * piece, (b + 1) * piece)
        last = jnp.concatenate([turned[rows], plain], axis=1).astype(jnp.bfloat16)
        fresh_in[fresh_at + b, :, :LATENT] = normed[rows]
        fresh_in[fresh_at + b, :, LATENT:] = last[:, :ROPE]
        keys[b, (groups - 1) * piece : groups * piece, :LATENT] = normed[rows]
        keys[b, (groups - 1) * piece : groups * piece, LATENT:] = last

    def along_x(step):
        here = fresh_in.at[pl.ds(fresh_place(core, z, x), 2)]
        to = (((x + step) % 4) * 4 + z) * 2 + core
        return pltpu.make_async_remote_copy(
            src_ref=here,
            dst_ref=here,
            send_sem=fresh_send.at[step - 1],
            recv_sem=fresh_recv.at[step - 1],
            device_id=(to, tp),
            device_id_type=MESH,
        )

    def along_z(step):
        here = fresh_in.at[pl.ds(fresh_place(core, z, 0), 8)]
        to = (x * 4 + (z + step) % 4) * 2 + core
        return pltpu.make_async_remote_copy(
            src_ref=here,
            dst_ref=here,
            send_sem=fresh_send.at[step + 2],
            recv_sem=fresh_recv.at[step + 2],
            device_id=(to, tp),
            device_id_type=MESH,
        )

    def to_other_core():
        here = fresh_in.at[pl.ds(fresh_place(core, 0, 0), 32)]
        return pltpu.make_async_remote_copy(
            src_ref=here,
            dst_ref=here,
            send_sem=fresh_send.at[6],
            recv_sem=fresh_recv.at[6],
            device_id=((x * 4 + z) * 2 + 1 - core, tp),
            device_id_type=MESH,
        )

    for step in range(1, 4):
        along_x(step).start()

    lane_mark = lax.broadcasted_iota(jnp.int32, (piece, WIDE - WIDTH), 1)

    def gather_blocks(parity):
        others = arrived[parity].at[pl.ds(0, pool_count - 1)]
        pltpu.make_async_copy(others, others, block_recv.at[parity]).wait()
        if parity == 0:
            send_blocks(1)

        @pl.loop(0, groups - 1)
        def _(k):
            block = arrived[parity][holder[me, 2 * k + parity]]
            mark = jnp.where(2 * k + parity < prefix[me], 0.0, HIDDEN)
            marks = jnp.where(lane_mark == 0, mark, 0.0).astype(jnp.bfloat16)
            rows = pl.ds(pl.multiple_of(k * piece, piece), piece)
            keys[parity, rows, :LATENT] = block[:, :LATENT]
            keys[parity, rows, LATENT:] = jnp.concatenate([block[:, LATENT:], marks], axis=1)

        for part in range(2):
            for side in range(2):
                near_copy(parity, part, side).start()

    neighbours = (ahead, behind)
    third = HALF // 2

    def near_copy(parity, part, side):
        return pltpu.make_async_remote_copy(
            src_ref=keys.at[parity, pl.ds(part * third, third)],
            dst_ref=keys.at[2 * parity + part, pl.ds(HALF + side * third, third)],
            send_sem=near_send.at[parity, part, side],
            recv_sem=near_recv.at[parity, part, side],
            device_id=(me, neighbours[side]),
            device_id_type=MESH,
        )

    def far_copy(parity, side):
        return pltpu.make_async_remote_copy(
            src_ref=keys.at[2 * parity + side, pl.ds(HALF + side * third, third)],
            dst_ref=keys.at[2 + parity, pl.ds(side * third, third)],
            send_sem=far_send.at[parity, side],
            recv_sem=far_recv.at[parity, side],
            device_id=(me, neighbours[side]),
            device_id_type=MESH,
        )

    def take(parity, part):
        for side in range(2):
            near_copy(parity, part, side).wait_recv()
        far_copy(parity, part).start()

    def take_far(parity):
        for side in range(2):
            far_copy(parity, side).wait_recv()

    mark_lane = lax.broadcasted_iota(jnp.int32, (SUFFIX, WIDE - WIDTH), 1)
    one_mark = jnp.where(mark_lane == 0, 1.0, 0.0).astype(jnp.bfloat16)

    def turn(head):
        rows = pl.ds(pl.multiple_of(head * SUFFIX, SUFFIX), SUFFIX)
        turned_query = queries_in[head].T
        queries[rows, :LATENT] = turned_query[:, :LATENT]
        queries[rows, LATENT:] = jnp.concatenate([turned_query[:, LATENT:], one_mark], axis=1)

    lane_slot = lax.broadcasted_iota(jnp.int32, (8, 128), 1)

    def mark_slot(request, index):
        for b in range(2):
            entry = prefix[request] + b
            here = holder[request, entry] == me
            target = jnp.where(here, slot[request, entry], -1)
            index = jnp.where(lane_slot == target, fresh_place(request % 2, (request // 2) % 4, request // 8) + b, index)
        return index

    index_v[...] = lax.fori_loop(0, pool_count, mark_slot, jnp.full((8, 128), -1, jnp.int32))
    to_scalars = pltpu.make_async_copy(index_v, index_s, index_sem)
    to_scalars.start()

    loads[3].wait()
    early = heads * 5 // 8

    @pl.loop(0, early)
    def _(head):
        turn(head)

    gather_blocks(0)

    @pl.loop(early, heads)
    def _(head):
        turn(head)

    def before_near_even():
        take(0, 0)

    def before_own_odd():
        gather_blocks(1)
        take(0, 1)
        for hop in range(1, 4):
            along_x(hop).wait_recv()
        for hop in range(1, 4):
            along_z(hop).start()

    def before_far_even():
        take(1, 0)
        take(1, 1)
        take_far(0)
        for hop in range(1, 4):
            along_z(hop).wait_recv()
        to_other_core().start()

    def before_far_odd():
        take_far(1)
        loads[4].wait()

    def first_new(parity, owner):
        return parity * BLOCK + owner * piece

    steps = (
        (lambda: None, 0, 0, HALF, {1: first_new(0, tp)}),
        (before_near_even, 0, HALF, HALF, {}),
        (
            before_own_odd,
            1,
            0,
            2 * HALF,
            {1: first_new(1, tp), 2: first_new(0, behind), 3: first_new(0, ahead)},
        ),
        (before_far_even, 2, 0, 2 * HALF, {1: first_new(0, across)}),
        (
            before_far_odd,
            3,
            0,
            2 * HALF,
            {1: first_new(1, across), 2: first_new(1, behind), 3: first_new(1, ahead)},
        ),
    )

    lane = lax.broadcasted_iota(jnp.int32, (SUFFIX, 128), 1)
    row_token = lax.broadcasted_iota(jnp.int32, (SUFFIX, 128), 0)
    new_lane = lane - (128 - piece)
    masks = []
    for step in steps:
        places = {}
        for tile, base in step[4].items():
            number = sum(len(m) for m in masks) + len(places)
            hide = (new_lane >= 0) & (base + new_lane > row_token)
            bias[number] = jnp.where(hide, HIDDEN, 0.0)
            places[tile] = number
        masks.append(places)
    live = lax.broadcasted_iota(jnp.int32, (SUFFIX, VALUE_DIM), 0) < length[me]
    tiles = queries.shape[0] // ROWS

    def prepare(step):
        before, number, start, count, _ = steps[step]
        before()
        keys_t[step % 2, :, :count] = keys[number, start : start + count].T

    def score(step, tile, place):
        count = steps[step][3]
        rows = slice(tile * ROWS, (tile + 1) * ROWS)
        scores[place][:, :count] = jnp.dot(
            queries[rows, :], keys_t[step % 2, :, :count], preferred_element_type=jnp.float32
        )

    def weigh(step, tile, place):
        for start in range(0, ROWS, STRIP):
            rows = slice(start, start + STRIP)
            all_rows = slice(tile * ROWS + start, tile * ROWS + start + STRIP)
            tokens_of = slice(start % SUFFIX, start % SUFFIX + STRIP)
            columns = [slice(j * 128, (j + 1) * 128) for j in range(steps[step][3] // 128)]
            parts = [scores[place][rows, lanes] for lanes in columns]
            for j, number in masks[step].items():
                parts[j] = parts[j] + bias[number, tokens_of, :]
            top = functools.reduce(jnp.maximum, parts)
            top = jnp.max(top, axis=1, keepdims=True) * SCALE
            if step == 0:
                top = jnp.broadcast_to(top, (STRIP, 128))
            else:
                old = high[all_rows, :]
                top = jnp.maximum(old, top)
                fade = jnp.exp2(old - top)
                decay[place][rows, :] = fade
            raised = [jnp.exp2(part * SCALE - top) for part in parts]
            total = functools.reduce(jnp.add, raised)
            if step > 0:
                total = total + norm[all_rows, :] * fade
            high[all_rows, :] = top
            norm[all_rows, :] = total
            for lanes, part in zip(columns, raised):
                weights[place][rows, lanes] = part.astype(jnp.bfloat16)

    def mix(step, tile, place):
        _, number, start, count, _ = steps[step]
        rows = slice(tile * ROWS, (tile + 1) * ROWS)
        mixed = jnp.dot(
            weights[place][:, :count],
            keys[number, start : start + count, :LATENT],
            preferred_element_type=jnp.float32,
        )
        for j in range(LATENT // 128):
            lanes = slice(j * 128, (j + 1) * 128)
            part = mixed[:, lanes]
            if step > 0:
                part = part + acc[rows, lanes] * decay[place][...]
            acc[rows, lanes] = part

    def project(tile):
        for inner in range(ROWS // SUFFIX):
            head = tile * (ROWS // SUFFIX) + inner
            rows = slice(head * SUFFIX, (head + 1) * SUFFIX)
            share = 1.0 / jnp.sum(norm[rows, :], axis=1, keepdims=True)
            mixed = (acc[rows, :] * share).astype(jnp.bfloat16)
            value = jnp.dot(mixed, value_v[head], preferred_element_type=jnp.float32)
            columns = slice(head * VALUE_DIM, (head + 1) * VALUE_DIM)
            out_v[:, columns] = jnp.where(live, value, 0.0).astype(jnp.bfloat16)

    work = [(step, tile) for step in range(len(steps)) for tile in range(tiles)]
    prepare(0)
    score(0, 0, 0)
    for at, (step, tile) in enumerate(work):
        if at + 1 < len(work):
            after_step, after_tile = work[at + 1]
            if after_step != step:
                prepare(after_step)
            score(after_step, after_tile, (at + 1) % 2)
        weigh(step, tile, at % 2)
        mix(step, tile, at % 2)
        if step == len(steps) - 1:
            project(tile)

    store_out = pltpu.make_async_copy(out_v, out_h, load_sem.at[1])
    store_out.start()

    to_other_core().wait_recv()
    to_scalars.wait()

    @pl.loop(0, slots)
    def _(place):
        at = index_s[0, place]
        replaced = jnp.where(at >= 0, 1.0, 0.0)
        kept = pool_v[place]
        taken = fresh_in[jnp.maximum(at, 0)]
        new_pool_v[place] = jnp.where(replaced > 0.5, taken, kept)

    store_pool = pltpu.make_async_copy(new_pool_v, new_pool_h, load_sem.at[0])
    store_pool.start()


    for copy in sums:
        copy.wait_send()
    for parity in range(2):
        sent = arrived[parity].at[pl.ds(0, pool_count - 1)]
        pltpu.make_async_copy(sent, sent, block_send.at[parity]).wait()
        for side in range(2):
            for part in range(2):
                near_copy(parity, part, side).wait_send()
            far_copy(parity, side).wait_send()
    for step in range(1, 4):
        along_x(step).wait_send()
        along_z(step).wait_send()
    to_other_core().wait_send()
    store_pool.wait()
    store_out.wait()


def fresh_place(at_core, at_z, at_x):
    return 2 * ((at_core * 4 + at_z) * 4 + at_x)


def on_device(
    pool_count,
    tp_count,
    tokens,
    down_weight,
    kv_gain,
    queries,
    value_weight,
    pool,
    block_holder,
    block_slot,
    prefix_blocks,
    suffix_len,
):
    heads = queries.shape[1]
    piece = pool.shape[1]
    rows = SUFFIX * heads
    exponent = np.arange(ROPE // 2).astype(np.float32) * np.float32(2.0 / ROPE)
    inverse_frequency = np.power(np.float32(10000.0), -exponent).astype(np.float32)
    frequency = np.tile(inverse_frequency, 2)[None, :]
    bf16, f32 = jnp.bfloat16, jnp.float32
    smem = pl.BlockSpec(memory_space=pltpu.SMEM)
    vmem = pl.BlockSpec(memory_space=pltpu.VMEM)
    anywhere = pl.BlockSpec(memory_space=pl.ANY)
    dma = pltpu.SemaphoreType.DMA
    return pl.pallas_call(
        functools.partial(kernel, pool_count, tp_count),
        out_shape=(
            jax.ShapeDtypeStruct((SUFFIX, heads * VALUE_DIM), bf16),
            jax.ShapeDtypeStruct(pool.shape, bf16),
        ),
        in_specs=[smem] * 4 + [vmem] * 2 + [anywhere] * 5,
        out_specs=(anywhere, anywhere),
        scratch_shapes=[
            pltpu.VMEM(tokens.shape, bf16),
            pltpu.VMEM(down_weight.shape[::-1], bf16),
            pltpu.VMEM((heads, WIDTH, SUFFIX), bf16),
            pltpu.VMEM((rows, WIDE), bf16),
            pltpu.VMEM(value_weight.shape, bf16),
            pltpu.VMEM(pool.shape, bf16),
            pltpu.VMEM((2, pool_count, piece, WIDTH), bf16),
            pltpu.VMEM((pool_count, piece, WIDTH), bf16),
            pltpu.VMEM((pool_count, piece, WIDTH), bf16),
            pltpu.VMEM((tp_count, 2 * piece, WIDTH), f32),
            pltpu.VMEM((tp_count - 1, 2 * piece, WIDTH), f32),
            pltpu.VMEM((2 * pool_count, piece, WIDTH), bf16),
            pltpu.VMEM((4, 2 * HALF, WIDE), bf16),
            pltpu.VMEM((2, WIDE, 2 * HALF), bf16),
            pltpu.VMEM((8, SUFFIX, 128), f32),
            pltpu.VMEM((ROWS, 2 * HALF), f32),
            pltpu.VMEM((ROWS, 2 * HALF), f32),
            pltpu.VMEM((ROWS, 2 * HALF), bf16),
            pltpu.VMEM((ROWS, 2 * HALF), bf16),
            pltpu.VMEM((ROWS, 128), f32),
            pltpu.VMEM((ROWS, 128), f32),
            pltpu.VMEM((rows, LATENT), f32),
            pltpu.VMEM((rows, 128), f32),
            pltpu.VMEM((rows, 128), f32),
            pltpu.VMEM((SUFFIX, heads * VALUE_DIM), bf16),
            pltpu.VMEM(pool.shape, bf16),
            pltpu.VMEM((8, 128), jnp.int32),
            pltpu.SMEM((8, 128), jnp.int32),
            pltpu.SMEM((pool_count,), jnp.int32),
            dma((5,)),
            dma,
            dma((2,)),
            dma((2,)),
            dma((tp_count - 1,)),
            dma((tp_count - 1,)),
            dma((7,)),
            dma((7,)),
            dma((2, 2, 2)),
            dma((2, 2, 2)),
            dma((2, 2)),
            dma((2, 2)),
        ],
        compiler_params=pltpu.CompilerParams(
            collective_id=0, has_side_effects=True, vmem_limit_bytes=60 * 1024 * 1024
        ),
        name="latent_attention",
    )(
        block_holder,
        block_slot,
        prefix_blocks,
        suffix_len,
        kv_gain.reshape(1, LATENT),
        jnp.asarray(frequency),
        tokens,
        down_weight.T,
        queries.transpose(1, 2, 0),
        value_weight,
        pool,
    )


def solution(mesh):
    in_specs = (
        P("pool", "tp"),
        P("tp", None),
        P(),
        P("pool", "tp", None),
        P("tp", None, None),
        P("pool", "tp", None),
        P(),
        P(),
        P(),
        P(),
    )
    out_specs = (P("pool", "tp"), P("pool", "tp", None))
    return jax.shard_map(
        functools.partial(on_device, mesh.shape["pool"], mesh.shape["tp"]),
        mesh=mesh,
        in_specs=in_specs,
        out_specs=out_specs,
        check_vma=False,
    )
```

```python
import functools
import math

import jax
import jax.numpy as jnp
import numpy as np
from jax import lax
from jax.experimental import pallas as pl
from jax.experimental.pallas import tpu as pltpu
from jax.sharding import PartitionSpec as P

LATENT = 512
VALUE_DIM = 128
BLOCK = 64
SUFFIX = 128
TABLE = 32
WIDTH = 576
WIDE = 640
ROPE = WIDTH - LATENT
HALF = 256
SCALE = 192.0 ** (-0.5) * math.log2(math.e)
HIDDEN = -1e30
EPSILON = 1e-06
ROWS = 1024
STRIP = 32
MESH = pl.DeviceIdType.MESH


def kernel(
    pool_count,
    tp_count,
    holder,
    slot,
    prefix,
    length,
    gain,
    frequency,
    tokens_h,
    down_h,
    queries_h,
    value_h,
    pool_h,
    out_h,
    new_pool_h,
    tokens_v,
    down_v,
    queries_in,
    queries,
    value_v,
    pool_v,
    leaving,
    arrived_even,
    arrived_odd,
    partial_v,
    partial_in,
    fresh_in,
    keys,
    keys_t,
    bias,
    scores_a,
    scores_b,
    weights_a,
    weights_b,
    decay_a,
    decay_b,
    acc,
    high,
    norm,
    out_v,
    new_pool_v,
    index_v,
    index_s,
    entry_s,
    load_sem,
    index_sem,
    block_send,
    block_recv,
    sum_send,
    sum_recv,
    fresh_send,
    fresh_recv,
    near_send,
    near_recv,
    far_send,
    far_recv,
):
    me = lax.axis_index("pool")
    tp = lax.axis_index("tp")
    core, z, x = me % 2, (me // 2) % 4, me // 8
    ahead, behind = (tp + 1) % tp_count, (tp + tp_count - 1) % tp_count
    across = (tp + 2) % tp_count
    heads = queries_in.shape[0]
    slots = pool_v.shape[0]
    piece = pool_v.shape[1]
    groups = TABLE // 2
    arrived = (arrived_even, arrived_odd)
    scores, weights = (scores_a, scores_b), (weights_a, weights_b)
    decay = (decay_a, decay_b)

    def peer(step):
        to_core = (core + step % 2) % 2
        to_z = (z + (step // 2) % 4) % 4
        to_x = (x + step // 8) % 4
        return (to_x * 4 + to_z) * 2 + to_core

    loads = [
        pltpu.make_async_copy(pool_h, pool_v, load_sem.at[0]),
        pltpu.make_async_copy(tokens_h, tokens_v, load_sem.at[1]),
        pltpu.make_async_copy(down_h, down_v, load_sem.at[2]),
        pltpu.make_async_copy(queries_h, queries_in, load_sem.at[3]),
        pltpu.make_async_copy(value_h, value_v, load_sem.at[4]),
    ]
    for load in loads:
        load.start()

    barrier = pltpu.get_barrier_semaphore()

    @pl.loop(1, pool_count)
    def _(step):
        pl.semaphore_signal(barrier, inc=1, device_id=(peer(step), tp), device_id_type=MESH)

    for step in range(1, tp_count):
        pl.semaphore_signal(
            barrier, inc=1, device_id=(me, (tp + step) % tp_count), device_id_type=MESH
        )

    loads[0].wait()

    @pl.loop(0, pool_count)
    def _(request):
        at = jnp.int32(0)
        for k in range(groups - 1):
            at = jnp.where(holder[request, 2 * k] == me, 2 * k, at)
        entry_s[request] = at
        leaving[0, request] = pool_v[slot[request, at]]

    arrived[0][me] = pool_v[slot[me, entry_s[me]]]

    pl.semaphore_wait(barrier, pool_count - 1 + tp_count - 1)

    def send_blocks(parity):
        @pl.loop(1, pool_count)
        def _(step):
            request = peer(step)
            pltpu.make_async_remote_copy(
                src_ref=leaving.at[parity, request],
                dst_ref=arrived[parity].at[me],
                send_sem=block_send.at[parity],
                recv_sem=block_recv.at[parity],
                device_id=(request, tp),
                device_id_type=MESH,
            ).start()

    def blocks_sent(parity):
        sent = leaving.at[parity, pl.ds(0, pool_count - 1)]
        return pltpu.make_async_copy(sent, sent, block_send.at[parity])

    send_blocks(0)

    @pl.loop(0, pool_count)
    def _(request):
        leaving[1, request] = pool_v[slot[request, entry_s[request] + 1]]

    arrived[1][me] = pool_v[slot[me, entry_s[me] + 1]]

    loads[1].wait()
    loads[2].wait()
    partial = lax.dot_general(
        tokens_v[...], down_v[...], (((1,), (1,)), ((), ())), preferred_element_type=jnp.float32
    )
    for owner in range(tp_count):
        for b in range(2):
            partial_v[owner, b * piece : (b + 1) * piece, :] = partial[
                b * BLOCK + owner * piece : b * BLOCK + (owner + 1) * piece, :
            ]
    sums = []
    for step in range(1, tp_count):
        to = (tp + step) % tp_count
        copy = pltpu.make_async_remote_copy(
            src_ref=partial_v.at[to],
            dst_ref=partial_in.at[step - 1],
            send_sem=sum_send.at[step - 1],
            recv_sem=sum_recv.at[step - 1],
            device_id=(me, to),
            device_id_type=MESH,
        )
        copy.start()
        sums.append(copy)

    for copy in sums:
        copy.wait_recv()
    latent = partial_v[tp] + partial_in[0] + partial_in[1] + partial_in[2]
    content = latent[:, :LATENT]
    rotary = latent[:, LATENT:]
    inverse = lax.rsqrt(jnp.mean(content * content, axis=1, keepdims=True) + EPSILON)
    normed = content * inverse * gain[...]
    row = lax.broadcasted_iota(jnp.int32, (2 * piece, ROPE), 0)
    lane = lax.broadcasted_iota(jnp.int32, (2 * piece, ROPE), 1)
    token = (row // piece) * BLOCK + tp * piece + row % piece
    angles = (prefix[me] * BLOCK + token).astype(jnp.float32) * frequency[...]
    turned_by = jnp.concatenate([rotary[:, ROPE // 2 :], rotary[:, : ROPE // 2]], axis=1)
    sine = jnp.where(lane < ROPE // 2, -1.0, 1.0) * jnp.sin(angles)
    turned = rotary * jnp.cos(angles) + turned_by * sine
    row512 = lax.broadcasted_iota(jnp.int32, (2 * piece, LATENT), 0)
    token512 = (row512 // piece) * BLOCK + tp * piece + row512 % piece
    normed = jnp.where(token512 < length[me], normed, 0.0).astype(jnp.bfloat16)
    turned = jnp.where(token < length[me], turned, 0.0)
    fresh_at = 2 * ((core * 4 + z) * 4 + x)
    plain = jnp.zeros((piece, WIDE - WIDTH), jnp.float32)
    for b in range(2):
        rows = slice(b * piece, (b + 1) * piece)
        last = jnp.concatenate([turned[rows], plain], axis=1).astype(jnp.bfloat16)
        fresh_in[fresh_at + b, :, :LATENT] = normed[rows]
        fresh_in[fresh_at + b, :, LATENT:] = last[:, :ROPE]
        keys[b, (groups - 1) * piece : groups * piece, :LATENT] = normed[rows]
        keys[b, (groups - 1) * piece : groups * piece, LATENT:] = last

    def along_x(step):
        here = fresh_in.at[pl.ds(fresh_place(core, z, x), 2)]
        to = (((x + step) % 4) * 4 + z) * 2 + core
        return pltpu.make_async_remote_copy(
            src_ref=here,
            dst_ref=here,
            send_sem=fresh_send.at[step - 1],
            recv_sem=fresh_recv.at[step - 1],
            device_id=(to, tp),
            device_id_type=MESH,
        )

    def along_z(step):
        here = fresh_in.at[pl.ds(fresh_place(core, z, 0), 8)]
        to = (x * 4 + (z + step) % 4) * 2 + core
        return pltpu.make_async_remote_copy(
            src_ref=here,
            dst_ref=here,
            send_sem=fresh_send.at[step + 2],
            recv_sem=fresh_recv.at[step + 2],
            device_id=(to, tp),
            device_id_type=MESH,
        )

    def to_other_core():
        here = fresh_in.at[pl.ds(fresh_place(core, 0, 0), 32)]
        return pltpu.make_async_remote_copy(
            src_ref=here,
            dst_ref=here,
            send_sem=fresh_send.at[6],
            recv_sem=fresh_recv.at[6],
            device_id=((x * 4 + z) * 2 + 1 - core, tp),
            device_id_type=MESH,
        )

    for step in range(1, 4):
        along_x(step).start()

    lane_mark = lax.broadcasted_iota(jnp.int32, (piece, WIDE - WIDTH), 1)

    def gather_blocks(parity):
        others = arrived[parity].at[pl.ds(0, pool_count - 1)]
        pltpu.make_async_copy(others, others, block_recv.at[parity]).wait()

        @pl.loop(0, groups - 1)
        def _(k):
            block = arrived[parity][holder[me, 2 * k + parity]]
            mark = jnp.where(2 * k + parity < prefix[me], 0.0, HIDDEN)
            marks = jnp.where(lane_mark == 0, mark, 0.0).astype(jnp.bfloat16)
            rows = pl.ds(pl.multiple_of(k * piece, piece), piece)
            keys[parity, rows, :LATENT] = block[:, :LATENT]
            keys[parity, rows, LATENT:] = jnp.concatenate([block[:, LATENT:], marks], axis=1)

        for part in range(2):
            for side in range(2):
                near_copy(parity, part, side).start()

    neighbours = (ahead, behind)
    third = HALF // 2

    def near_copy(parity, part, side):
        return pltpu.make_async_remote_copy(
            src_ref=keys.at[parity, pl.ds(part * third, third)],
            dst_ref=keys.at[2 * parity + part, pl.ds(HALF + side * third, third)],
            send_sem=near_send.at[parity, part, side],
            recv_sem=near_recv.at[parity, part, side],
            device_id=(me, neighbours[side]),
            device_id_type=MESH,
        )

    def far_copy(parity, side):
        return pltpu.make_async_remote_copy(
            src_ref=keys.at[2 * parity + side, pl.ds(HALF + side * third, third)],
            dst_ref=keys.at[2 + parity, pl.ds(side * third, third)],
            send_sem=far_send.at[parity, side],
            recv_sem=far_recv.at[parity, side],
            device_id=(me, neighbours[side]),
            device_id_type=MESH,
        )

    def take(parity, part):
        for side in range(2):
            near_copy(parity, part, side).wait_recv()
        far_copy(parity, part).start()

    def take_far(parity):
        for side in range(2):
            far_copy(parity, side).wait_recv()

    mark_lane = lax.broadcasted_iota(jnp.int32, (SUFFIX, WIDE - WIDTH), 1)
    one_mark = jnp.where(mark_lane == 0, 1.0, 0.0).astype(jnp.bfloat16)

    def turn(head):
        rows = pl.ds(pl.multiple_of(head * SUFFIX, SUFFIX), SUFFIX)
        turned_query = queries_in[head].T
        queries[rows, :LATENT] = turned_query[:, :LATENT]
        queries[rows, LATENT:] = jnp.concatenate([turned_query[:, LATENT:], one_mark], axis=1)

    lane_slot = lax.broadcasted_iota(jnp.int32, (8, 128), 1)

    def mark_slot(request, index):
        for b in range(2):
            entry = prefix[request] + b
            here = holder[request, entry] == me
            target = jnp.where(here, slot[request, entry], -1)
            index = jnp.where(lane_slot == target, fresh_place(request % 2, (request // 2) % 4, request // 8) + b, index)
        return index

    index_v[...] = lax.fori_loop(0, pool_count, mark_slot, jnp.full((8, 128), -1, jnp.int32))
    to_scalars = pltpu.make_async_copy(index_v, index_s, index_sem)
    to_scalars.start()

    loads[3].wait()
    tiles = queries.shape[0] // ROWS
    tile_heads = ROWS // SUFFIX

    @pl.loop(0, tile_heads)
    def _(head):
        turn(head)

    blocks_sent(0).wait()
    send_blocks(1)

    @pl.loop(tile_heads, 2 * tile_heads)
    def _(head):
        turn(head)

    gather_blocks(0)

    def before_near_even():
        take(0, 0)

    def before_own_odd():
        gather_blocks(1)
        take(0, 1)
        for hop in range(1, 4):
            along_x(hop).wait_recv()
        for hop in range(1, 4):
            along_z(hop).start()

    def before_far_even():
        take(1, 0)
        take(1, 1)
        take_far(0)
        for hop in range(1, 4):
            along_z(hop).wait_recv()
        to_other_core().start()

    def before_far_odd():
        take_far(1)
        loads[4].wait()

    def first_new(parity, owner):
        return parity * BLOCK + owner * piece

    steps = (
        (lambda: None, 0, 0, HALF, {1: first_new(0, tp)}),
        (before_near_even, 0, HALF, HALF, {}),
        (
            before_own_odd,
            1,
            0,
            2 * HALF,
            {1: first_new(1, tp), 2: first_new(0, behind), 3: first_new(0, ahead)},
        ),
        (before_far_even, 2, 0, 2 * HALF, {1: first_new(0, across)}),
        (
            before_far_odd,
            3,
            0,
            2 * HALF,
            {1: first_new(1, across), 2: first_new(1, behind), 3: first_new(1, ahead)},
        ),
    )

    lane = lax.broadcasted_iota(jnp.int32, (SUFFIX, 128), 1)
    row_token = lax.broadcasted_iota(jnp.int32, (SUFFIX, 128), 0)
    new_lane = lane - (128 - piece)
    masks = []
    for step in steps:
        places = {}
        for tile, base in step[4].items():
            number = sum(len(m) for m in masks) + len(places)
            hide = (new_lane >= 0) & (base + new_lane > row_token)
            bias[number] = jnp.where(hide, HIDDEN, 0.0)
            places[tile] = number
        masks.append(places)
    live = lax.broadcasted_iota(jnp.int32, (SUFFIX, VALUE_DIM), 0) < length[me]
    def prepare(step):
        before, number, start, count, _ = steps[step]
        before()
        keys_t[step % 2, :, :count] = keys[number, start : start + count].T

    def score(step, tile, place):
        count = steps[step][3]
        rows = slice(tile * ROWS, (tile + 1) * ROWS)
        scores[place][:, :count] = jnp.dot(
            queries[rows, :], keys_t[step % 2, :, :count], preferred_element_type=jnp.float32
        )

    def weigh(step, tile, place):
        for start in range(0, ROWS, STRIP):
            rows = slice(start, start + STRIP)
            all_rows = slice(tile * ROWS + start, tile * ROWS + start + STRIP)
            tokens_of = slice(start % SUFFIX, start % SUFFIX + STRIP)
            columns = [slice(j * 128, (j + 1) * 128) for j in range(steps[step][3] // 128)]
            parts = [scores[place][rows, lanes] for lanes in columns]
            for j, number in masks[step].items():
                parts[j] = parts[j] + bias[number, tokens_of, :]
            top = functools.reduce(jnp.maximum, parts)
            top = jnp.max(top, axis=1, keepdims=True) * SCALE
            if step == 0:
                top = jnp.broadcast_to(top, (STRIP, 128))
            else:
                old = high[all_rows, :]
                top = jnp.maximum(old, top)
                fade = jnp.exp2(old - top)
                decay[place][rows, :] = fade
            raised = [jnp.exp2(part * SCALE - top) for part in parts]
            total = functools.reduce(jnp.add, raised)
            if step > 0:
                total = total + norm[all_rows, :] * fade
            high[all_rows, :] = top
            norm[all_rows, :] = total
            for lanes, part in zip(columns, raised):
                weights[place][rows, lanes] = part.astype(jnp.bfloat16)

    def mix(step, tile, place):
        _, number, start, count, _ = steps[step]
        rows = slice(tile * ROWS, (tile + 1) * ROWS)
        mixed = jnp.dot(
            weights[place][:, :count],
            keys[number, start : start + count, :LATENT],
            preferred_element_type=jnp.float32,
        )
        for j in range(LATENT // 128):
            lanes = slice(j * 128, (j + 1) * 128)
            part = mixed[:, lanes]
            if step > 0:
                part = part + acc[rows, lanes] * decay[place][...]
            acc[rows, lanes] = part

    def project(tile):
        for inner in range(tile_heads):
            head = tile * tile_heads + inner
            rows = slice(head * SUFFIX, (head + 1) * SUFFIX)
            share = 1.0 / jnp.sum(norm[rows, :], axis=1, keepdims=True)
            mixed = (acc[rows, :] * share).astype(jnp.bfloat16)
            value = jnp.dot(mixed, value_v[head], preferred_element_type=jnp.float32)
            columns = slice(head * VALUE_DIM, (head + 1) * VALUE_DIM)
            out_v[:, columns] = jnp.where(live, value, 0.0).astype(jnp.bfloat16)

    work = [(step, tile) for step in range(len(steps)) for tile in range(tiles)]
    prepare(0)
    score(0, 0, 0)
    for at, (step, tile) in enumerate(work):
        if at + 1 < len(work):
            after_step, after_tile = work[at + 1]
            if after_step != step:
                prepare(after_step)
            score(after_step, after_tile, (at + 1) % 2)
        if step == 0 and tile + 2 < tiles:
            for head in range((tile + 2) * tile_heads, (tile + 3) * tile_heads):
                turn(head)
        weigh(step, tile, at % 2)
        mix(step, tile, at % 2)
        if step == len(steps) - 1:
            project(tile)

    store_out = pltpu.make_async_copy(out_v, out_h, load_sem.at[1])
    store_out.start()

    to_other_core().wait_recv()
    to_scalars.wait()

    @pl.loop(0, slots)
    def _(place):
        at = index_s[0, place]
        replaced = jnp.where(at >= 0, 1.0, 0.0)
        kept = pool_v[place]
        taken = fresh_in[jnp.maximum(at, 0)]
        new_pool_v[place] = jnp.where(replaced > 0.5, taken, kept)

    store_pool = pltpu.make_async_copy(new_pool_v, new_pool_h, load_sem.at[0])
    store_pool.start()


    for copy in sums:
        copy.wait_send()
    blocks_sent(1).wait()
    for parity in range(2):
        for side in range(2):
            for part in range(2):
                near_copy(parity, part, side).wait_send()
            far_copy(parity, side).wait_send()
    for step in range(1, 4):
        along_x(step).wait_send()
        along_z(step).wait_send()
    to_other_core().wait_send()
    store_pool.wait()
    store_out.wait()


def fresh_place(at_core, at_z, at_x):
    return 2 * ((at_core * 4 + at_z) * 4 + at_x)


def on_device(
    pool_count,
    tp_count,
    tokens,
    down_weight,
    kv_gain,
    queries,
    value_weight,
    pool,
    block_holder,
    block_slot,
    prefix_blocks,
    suffix_len,
):
    heads = queries.shape[1]
    piece = pool.shape[1]
    rows = SUFFIX * heads
    exponent = np.arange(ROPE // 2).astype(np.float32) * np.float32(2.0 / ROPE)
    inverse_frequency = np.power(np.float32(10000.0), -exponent).astype(np.float32)
    frequency = np.tile(inverse_frequency, 2)[None, :]
    bf16, f32 = jnp.bfloat16, jnp.float32
    smem = pl.BlockSpec(memory_space=pltpu.SMEM)
    vmem = pl.BlockSpec(memory_space=pltpu.VMEM)
    anywhere = pl.BlockSpec(memory_space=pl.ANY)
    dma = pltpu.SemaphoreType.DMA
    return pl.pallas_call(
        functools.partial(kernel, pool_count, tp_count),
        out_shape=(
            jax.ShapeDtypeStruct((SUFFIX, heads * VALUE_DIM), bf16),
            jax.ShapeDtypeStruct(pool.shape, bf16),
        ),
        in_specs=[smem] * 4 + [vmem] * 2 + [anywhere] * 5,
        out_specs=(anywhere, anywhere),
        scratch_shapes=[
            pltpu.VMEM(tokens.shape, bf16),
            pltpu.VMEM(down_weight.shape[::-1], bf16),
            pltpu.VMEM((heads, WIDTH, SUFFIX), bf16),
            pltpu.VMEM((rows, WIDE), bf16),
            pltpu.VMEM(value_weight.shape, bf16),
            pltpu.VMEM(pool.shape, bf16),
            pltpu.VMEM((2, pool_count, piece, WIDTH), bf16),
            pltpu.VMEM((pool_count, piece, WIDTH), bf16),
            pltpu.VMEM((pool_count, piece, WIDTH), bf16),
            pltpu.VMEM((tp_count, 2 * piece, WIDTH), f32),
            pltpu.VMEM((tp_count - 1, 2 * piece, WIDTH), f32),
            pltpu.VMEM((2 * pool_count, piece, WIDTH), bf16),
            pltpu.VMEM((4, 2 * HALF, WIDE), bf16),
            pltpu.VMEM((2, WIDE, 2 * HALF), bf16),
            pltpu.VMEM((8, SUFFIX, 128), f32),
            pltpu.VMEM((ROWS, 2 * HALF), f32),
            pltpu.VMEM((ROWS, 2 * HALF), f32),
            pltpu.VMEM((ROWS, 2 * HALF), bf16),
            pltpu.VMEM((ROWS, 2 * HALF), bf16),
            pltpu.VMEM((ROWS, 128), f32),
            pltpu.VMEM((ROWS, 128), f32),
            pltpu.VMEM((rows, LATENT), f32),
            pltpu.VMEM((rows, 128), f32),
            pltpu.VMEM((rows, 128), f32),
            pltpu.VMEM((SUFFIX, heads * VALUE_DIM), bf16),
            pltpu.VMEM(pool.shape, bf16),
            pltpu.VMEM((8, 128), jnp.int32),
            pltpu.SMEM((8, 128), jnp.int32),
            pltpu.SMEM((pool_count,), jnp.int32),
            dma((5,)),
            dma,
            dma((2,)),
            dma((2,)),
            dma((tp_count - 1,)),
            dma((tp_count - 1,)),
            dma((7,)),
            dma((7,)),
            dma((2, 2, 2)),
            dma((2, 2, 2)),
            dma((2, 2)),
            dma((2, 2)),
        ],
        compiler_params=pltpu.CompilerParams(
            collective_id=0, has_side_effects=True, vmem_limit_bytes=60 * 1024 * 1024
        ),
        name="latent_attention",
    )(
        block_holder,
        block_slot,
        prefix_blocks,
        suffix_len,
        kv_gain.reshape(1, LATENT),
        jnp.asarray(frequency),
        tokens,
        down_weight.T,
        queries.transpose(1, 2, 0),
        value_weight,
        pool,
    )


def solution(mesh):
    in_specs = (
        P("pool", "tp"),
        P("tp", None),
        P(),
        P("pool", "tp", None),
        P("tp", None, None),
        P("pool", "tp", None),
        P(),
        P(),
        P(),
        P(),
    )
    out_specs = (P("pool", "tp"), P("pool", "tp", None))
    return jax.shard_map(
        functools.partial(on_device, mesh.shape["pool"], mesh.shape["tp"]),
        mesh=mesh,
        in_specs=in_specs,
        out_specs=out_specs,
        check_vma=False,
    )
```

```python
import functools
import math

import jax
import jax.numpy as jnp
import numpy as np
from jax import lax
from jax.experimental import pallas as pl
from jax.experimental.pallas import tpu as pltpu
from jax.sharding import PartitionSpec as P

LATENT = 512
VALUE_DIM = 128
BLOCK = 64
SUFFIX = 128
TABLE = 32
WIDTH = 576
WIDE = 640
ROPE = WIDTH - LATENT
HALF = 256
SCALE = 192.0 ** (-0.5) * math.log2(math.e)
HIDDEN = -1e30
EPSILON = 1e-06
ROWS = 1024
STRIP = 32
MESH = pl.DeviceIdType.MESH


def kernel(
    pool_count,
    tp_count,
    holder,
    slot,
    prefix,
    length,
    gain,
    frequency,
    tokens_h,
    down_h,
    queries_h,
    value_h,
    pool_h,
    out_h,
    new_pool_h,
    tokens_v,
    down_v,
    queries_in,
    queries,
    value_v,
    pool_v,
    leaving,
    arrived_even,
    arrived_odd,
    partial_v,
    partial_in,
    fresh_in,
    keys,
    keys_t,
    bias,
    scores_a,
    scores_b,
    weights_a,
    weights_b,
    decay_a,
    decay_b,
    acc,
    high,
    norm,
    out_v,
    new_pool_v,
    index_v,
    index_s,
    entry_s,
    load_sem,
    index_sem,
    block_send,
    block_recv,
    sum_send,
    sum_recv,
    fresh_send,
    fresh_recv,
    near_send,
    near_recv,
    far_send,
    far_recv,
):
    me = lax.axis_index("pool")
    tp = lax.axis_index("tp")
    core, z, x = me % 2, (me // 2) % 4, me // 8
    ahead, behind = (tp + 1) % tp_count, (tp + tp_count - 1) % tp_count
    across = (tp + 2) % tp_count
    heads = queries_in.shape[0]
    slots = pool_v.shape[0]
    piece = pool_v.shape[1]
    groups = TABLE // 2
    arrived = (arrived_even, arrived_odd)
    scores, weights = (scores_a, scores_b), (weights_a, weights_b)
    decay = (decay_a, decay_b)

    def peer(step):
        to_core = (core + step % 2) % 2
        to_z = (z + (step // 2) % 4) % 4
        to_x = (x + step // 8) % 4
        return (to_x * 4 + to_z) * 2 + to_core

    loads = [
        pltpu.make_async_copy(pool_h, pool_v, load_sem.at[0]),
        pltpu.make_async_copy(tokens_h, tokens_v, load_sem.at[1]),
        pltpu.make_async_copy(down_h, down_v, load_sem.at[2]),
        pltpu.make_async_copy(queries_h, queries_in, load_sem.at[3]),
        pltpu.make_async_copy(value_h, value_v, load_sem.at[4]),
    ]
    for load in loads:
        load.start()

    barrier = pltpu.get_barrier_semaphore()

    @pl.loop(1, pool_count)
    def _(step):
        pl.semaphore_signal(barrier, inc=1, device_id=(peer(step), tp), device_id_type=MESH)

    for step in range(1, tp_count):
        pl.semaphore_signal(
            barrier, inc=1, device_id=(me, (tp + step) % tp_count), device_id_type=MESH
        )

    loads[0].wait()

    @pl.loop(0, pool_count)
    def _(request):
        at = jnp.int32(0)
        for k in range(groups - 1):
            at = jnp.where(holder[request, 2 * k] == me, 2 * k, at)
        entry_s[request] = at
        leaving[0, request] = pool_v[slot[request, at]]

    arrived[0][me] = pool_v[slot[me, entry_s[me]]]

    pl.semaphore_wait(barrier, pool_count - 1 + tp_count - 1)

    def send_blocks(parity):
        @pl.loop(1, pool_count)
        def _(step):
            request = peer(step)
            pltpu.make_async_remote_copy(
                src_ref=leaving.at[parity, request],
                dst_ref=arrived[parity].at[me],
                send_sem=block_send.at[parity],
                recv_sem=block_recv.at[parity],
                device_id=(request, tp),
                device_id_type=MESH,
            ).start()

    def blocks_sent(parity):
        sent = leaving.at[parity, pl.ds(0, pool_count - 1)]
        return pltpu.make_async_copy(sent, sent, block_send.at[parity])

    send_blocks(0)

    @pl.loop(0, pool_count)
    def _(request):
        leaving[1, request] = pool_v[slot[request, entry_s[request] + 1]]

    arrived[1][me] = pool_v[slot[me, entry_s[me] + 1]]

    loads[1].wait()
    loads[2].wait()
    partial = lax.dot_general(
        tokens_v[...], down_v[...], (((1,), (1,)), ((), ())), preferred_element_type=jnp.float32
    )
    for owner in range(tp_count):
        for b in range(2):
            partial_v[owner, b * piece : (b + 1) * piece, :] = partial[
                b * BLOCK + owner * piece : b * BLOCK + (owner + 1) * piece, :
            ]
    sums = []
    for step in range(1, tp_count):
        to = (tp + step) % tp_count
        copy = pltpu.make_async_remote_copy(
            src_ref=partial_v.at[to],
            dst_ref=partial_in.at[step - 1],
            send_sem=sum_send.at[step - 1],
            recv_sem=sum_recv.at[step - 1],
            device_id=(me, to),
            device_id_type=MESH,
        )
        copy.start()
        sums.append(copy)

    for copy in sums:
        copy.wait_recv()
    latent = partial_v[tp] + partial_in[0] + partial_in[1] + partial_in[2]
    content = latent[:, :LATENT]
    rotary = latent[:, LATENT:]
    inverse = lax.rsqrt(jnp.mean(content * content, axis=1, keepdims=True) + EPSILON)
    normed = content * inverse * gain[...]
    row = lax.broadcasted_iota(jnp.int32, (2 * piece, ROPE), 0)
    lane = lax.broadcasted_iota(jnp.int32, (2 * piece, ROPE), 1)
    token = (row // piece) * BLOCK + tp * piece + row % piece
    angles = (prefix[me] * BLOCK + token).astype(jnp.float32) * frequency[...]
    turned_by = jnp.concatenate([rotary[:, ROPE // 2 :], rotary[:, : ROPE // 2]], axis=1)
    sine = jnp.where(lane < ROPE // 2, -1.0, 1.0) * jnp.sin(angles)
    turned = rotary * jnp.cos(angles) + turned_by * sine
    row512 = lax.broadcasted_iota(jnp.int32, (2 * piece, LATENT), 0)
    token512 = (row512 // piece) * BLOCK + tp * piece + row512 % piece
    normed = jnp.where(token512 < length[me], normed, 0.0).astype(jnp.bfloat16)
    turned = jnp.where(token < length[me], turned, 0.0)
    fresh_at = 2 * ((core * 4 + z) * 4 + x)
    plain = jnp.zeros((piece, WIDE - WIDTH), jnp.float32)
    for b in range(2):
        rows = slice(b * piece, (b + 1) * piece)
        last = jnp.concatenate([turned[rows], plain], axis=1).astype(jnp.bfloat16)
        fresh_in[fresh_at + b, :, :LATENT] = normed[rows]
        fresh_in[fresh_at + b, :, LATENT:] = last[:, :ROPE]
        keys[b, (groups - 1) * piece : groups * piece, :LATENT] = normed[rows]
        keys[b, (groups - 1) * piece : groups * piece, LATENT:] = last

    def along_x(step):
        here = fresh_in.at[pl.ds(fresh_place(core, z, x), 2)]
        to = (((x + step) % 4) * 4 + z) * 2 + core
        return pltpu.make_async_remote_copy(
            src_ref=here,
            dst_ref=here,
            send_sem=fresh_send.at[step - 1],
            recv_sem=fresh_recv.at[step - 1],
            device_id=(to, tp),
            device_id_type=MESH,
        )

    def along_z(step):
        here = fresh_in.at[pl.ds(fresh_place(core, z, 0), 8)]
        to = (x * 4 + (z + step) % 4) * 2 + core
        return pltpu.make_async_remote_copy(
            src_ref=here,
            dst_ref=here,
            send_sem=fresh_send.at[step + 2],
            recv_sem=fresh_recv.at[step + 2],
            device_id=(to, tp),
            device_id_type=MESH,
        )

    def to_other_core():
        here = fresh_in.at[pl.ds(fresh_place(core, 0, 0), 32)]
        return pltpu.make_async_remote_copy(
            src_ref=here,
            dst_ref=here,
            send_sem=fresh_send.at[6],
            recv_sem=fresh_recv.at[6],
            device_id=((x * 4 + z) * 2 + 1 - core, tp),
            device_id_type=MESH,
        )

    for step in range(1, 4):
        along_x(step).start()

    lane_mark = lax.broadcasted_iota(jnp.int32, (piece, WIDE - WIDTH), 1)

    def gather_blocks(parity):
        others = arrived[parity].at[pl.ds(0, pool_count - 1)]
        pltpu.make_async_copy(others, others, block_recv.at[parity]).wait()

        @pl.loop(0, groups - 1)
        def _(k):
            block = arrived[parity][holder[me, 2 * k + parity]]
            mark = jnp.where(2 * k + parity < prefix[me], 0.0, HIDDEN)
            marks = jnp.where(lane_mark == 0, mark, 0.0).astype(jnp.bfloat16)
            rows = pl.ds(pl.multiple_of(k * piece, piece), piece)
            keys[parity, rows, :LATENT] = block[:, :LATENT]
            keys[parity, rows, LATENT:] = jnp.concatenate([block[:, LATENT:], marks], axis=1)

        for part in range(2):
            for side in range(2):
                near_copy(parity, part, side).start()

    neighbours = (ahead, behind)
    third = HALF // 2

    def near_copy(parity, part, side):
        return pltpu.make_async_remote_copy(
            src_ref=keys.at[parity, pl.ds(part * third, third)],
            dst_ref=keys.at[2 * parity + part, pl.ds(HALF + side * third, third)],
            send_sem=near_send.at[parity, part, side],
            recv_sem=near_recv.at[parity, part, side],
            device_id=(me, neighbours[side]),
            device_id_type=MESH,
        )

    def far_copy(parity, side):
        return pltpu.make_async_remote_copy(
            src_ref=keys.at[2 * parity + side, pl.ds(HALF + side * third, third)],
            dst_ref=keys.at[2 + parity, pl.ds(side * third, third)],
            send_sem=far_send.at[parity, side],
            recv_sem=far_recv.at[parity, side],
            device_id=(me, neighbours[side]),
            device_id_type=MESH,
        )

    def take(parity, part):
        for side in range(2):
            near_copy(parity, part, side).wait_recv()
        far_copy(parity, part).start()

    def take_far(parity):
        for side in range(2):
            far_copy(parity, side).wait_recv()

    mark_lane = lax.broadcasted_iota(jnp.int32, (SUFFIX, WIDE - WIDTH), 1)
    one_mark = jnp.where(mark_lane == 0, 1.0, 0.0).astype(jnp.bfloat16)

    def turn(head):
        rows = pl.ds(pl.multiple_of(head * SUFFIX, SUFFIX), SUFFIX)
        turned_query = queries_in[head].T
        queries[rows, :LATENT] = turned_query[:, :LATENT]
        queries[rows, LATENT:] = jnp.concatenate([turned_query[:, LATENT:], one_mark], axis=1)

    lane_slot = lax.broadcasted_iota(jnp.int32, (8, 128), 1)

    def mark_slot(request, index):
        for b in range(2):
            entry = prefix[request] + b
            here = holder[request, entry] == me
            target = jnp.where(here, slot[request, entry], -1)
            index = jnp.where(lane_slot == target, fresh_place(request % 2, (request // 2) % 4, request // 8) + b, index)
        return index

    index_v[...] = lax.fori_loop(0, pool_count, mark_slot, jnp.full((8, 128), -1, jnp.int32))
    to_scalars = pltpu.make_async_copy(index_v, index_s, index_sem)
    to_scalars.start()

    loads[3].wait()
    tiles = queries.shape[0] // ROWS
    tile_heads = ROWS // SUFFIX

    @pl.loop(0, tile_heads)
    def _(head):
        turn(head)

    blocks_sent(0).wait()
    send_blocks(1)

    @pl.loop(tile_heads, 2 * tile_heads)
    def _(head):
        turn(head)

    gather_blocks(0)

    def before_near_even():
        take(0, 0)

    def before_own_odd():
        gather_blocks(1)
        take(0, 1)
        for hop in range(1, 4):
            along_x(hop).wait_recv()
        for hop in range(1, 4):
            along_z(hop).start()

    def before_far_even():
        take(1, 0)
        take(1, 1)
        take_far(0)
        for hop in range(1, 4):
            along_z(hop).wait_recv()
        to_other_core().start()

    store_pool = pltpu.make_async_copy(new_pool_v, new_pool_h, load_sem.at[0])

    def before_far_odd():
        to_other_core().wait_recv()
        to_scalars.wait()

        @pl.loop(0, slots // 4)
        def _(quad):
            for inner in range(4):
                place = quad * 4 + inner
                at = index_s[0, place]
                replaced = jnp.where(at >= 0, 1.0, 0.0)
                kept = pool_v[place]
                taken = fresh_in[jnp.maximum(at, 0)]
                new_pool_v[place] = jnp.where(replaced > 0.5, taken, kept)

        store_pool.start()
        take_far(1)
        loads[4].wait()

    def first_new(parity, owner):
        return parity * BLOCK + owner * piece

    steps = (
        (lambda: None, 0, 0, HALF, {1: first_new(0, tp)}),
        (before_near_even, 0, HALF, HALF, {}),
        (
            before_own_odd,
            1,
            0,
            2 * HALF,
            {1: first_new(1, tp), 2: first_new(0, behind), 3: first_new(0, ahead)},
        ),
        (before_far_even, 2, 0, 2 * HALF, {1: first_new(0, across)}),
        (
            before_far_odd,
            3,
            0,
            2 * HALF,
            {1: first_new(1, across), 2: first_new(1, behind), 3: first_new(1, ahead)},
        ),
    )

    lane = lax.broadcasted_iota(jnp.int32, (SUFFIX, 128), 1)
    row_token = lax.broadcasted_iota(jnp.int32, (SUFFIX, 128), 0)
    new_lane = lane - (128 - piece)
    masks = []
    for step in steps:
        places = {}
        for tile, base in step[4].items():
            number = sum(len(m) for m in masks) + len(places)
            hide = (new_lane >= 0) & (base + new_lane > row_token)
            bias[number] = jnp.where(hide, HIDDEN, 0.0)
            places[tile] = number
        masks.append(places)
    live = lax.broadcasted_iota(jnp.int32, (SUFFIX, VALUE_DIM), 0) < length[me]
    def prepare(step):
        before, number, start, count, _ = steps[step]
        before()
        keys_t[step % 2, :, :count] = keys[number, start : start + count].T

    def score(step, tile, place):
        count = steps[step][3]
        rows = slice(tile * ROWS, (tile + 1) * ROWS)
        scores[place][:, :count] = jnp.dot(
            queries[rows, :], keys_t[step % 2, :, :count], preferred_element_type=jnp.float32
        )

    def weigh(step, tile, place):
        for start in range(0, ROWS, STRIP):
            rows = slice(start, start + STRIP)
            all_rows = slice(tile * ROWS + start, tile * ROWS + start + STRIP)
            tokens_of = slice(start % SUFFIX, start % SUFFIX + STRIP)
            columns = [slice(j * 128, (j + 1) * 128) for j in range(steps[step][3] // 128)]
            parts = [scores[place][rows, lanes] for lanes in columns]
            for j, number in masks[step].items():
                parts[j] = parts[j] + bias[number, tokens_of, :]
            top = functools.reduce(jnp.maximum, parts)
            top = jnp.max(top, axis=1, keepdims=True) * SCALE
            if step == 0:
                top = jnp.broadcast_to(top, (STRIP, 128))
            else:
                old = high[all_rows, :]
                top = jnp.maximum(old, top)
                fade = jnp.exp2(old - top)
                decay[place][rows, :] = fade
            raised = [jnp.exp2(part * SCALE - top) for part in parts]
            total = functools.reduce(jnp.add, raised)
            if step > 0:
                total = total + norm[all_rows, :] * fade
            high[all_rows, :] = top
            norm[all_rows, :] = total
            for lanes, part in zip(columns, raised):
                weights[place][rows, lanes] = part.astype(jnp.bfloat16)

    def mix(step, tile, place):
        _, number, start, count, _ = steps[step]
        rows = slice(tile * ROWS, (tile + 1) * ROWS)
        mixed = jnp.dot(
            weights[place][:, :count],
            keys[number, start : start + count, :LATENT],
            preferred_element_type=jnp.float32,
        )
        for j in range(LATENT // 128):
            lanes = slice(j * 128, (j + 1) * 128)
            part = mixed[:, lanes]
            if step > 0:
                part = part + acc[rows, lanes] * decay[place][...]
            acc[rows, lanes] = part

    def project(tile):
        for inner in range(tile_heads):
            head = tile * tile_heads + inner
            rows = slice(head * SUFFIX, (head + 1) * SUFFIX)
            share = 1.0 / jnp.sum(norm[rows, :], axis=1, keepdims=True)
            mixed = (acc[rows, :] * share).astype(jnp.bfloat16)
            value = jnp.dot(mixed, value_v[head], preferred_element_type=jnp.float32)
            columns = slice(head * VALUE_DIM, (head + 1) * VALUE_DIM)
            out_v[:, columns] = jnp.where(live, value, 0.0).astype(jnp.bfloat16)

    work = [(step, tile) for step in range(len(steps)) for tile in range(tiles)]
    prepare(0)
    score(0, 0, 0)
    for at, (step, tile) in enumerate(work):
        if at + 1 < len(work):
            after_step, after_tile = work[at + 1]
            if after_step != step:
                prepare(after_step)
            score(after_step, after_tile, (at + 1) % 2)
        if step == 0 and tile + 2 < tiles:
            for head in range((tile + 2) * tile_heads, (tile + 3) * tile_heads):
                turn(head)
        weigh(step, tile, at % 2)
        mix(step, tile, at % 2)
        if step == len(steps) - 1:
            project(tile)

    store_out = pltpu.make_async_copy(out_v, out_h, load_sem.at[1])
    store_out.start()

    for copy in sums:
        copy.wait_send()
    blocks_sent(1).wait()
    for parity in range(2):
        for side in range(2):
            for part in range(2):
                near_copy(parity, part, side).wait_send()
            far_copy(parity, side).wait_send()
    for step in range(1, 4):
        along_x(step).wait_send()
        along_z(step).wait_send()
    to_other_core().wait_send()
    store_pool.wait()
    store_out.wait()


def fresh_place(at_core, at_z, at_x):
    return 2 * ((at_core * 4 + at_z) * 4 + at_x)


def on_device(
    pool_count,
    tp_count,
    tokens,
    down_weight,
    kv_gain,
    queries,
    value_weight,
    pool,
    block_holder,
    block_slot,
    prefix_blocks,
    suffix_len,
):
    heads = queries.shape[1]
    piece = pool.shape[1]
    rows = SUFFIX * heads
    exponent = np.arange(ROPE // 2).astype(np.float32) * np.float32(2.0 / ROPE)
    inverse_frequency = np.power(np.float32(10000.0), -exponent).astype(np.float32)
    frequency = np.tile(inverse_frequency, 2)[None, :]
    bf16, f32 = jnp.bfloat16, jnp.float32
    smem = pl.BlockSpec(memory_space=pltpu.SMEM)
    vmem = pl.BlockSpec(memory_space=pltpu.VMEM)
    anywhere = pl.BlockSpec(memory_space=pl.ANY)
    dma = pltpu.SemaphoreType.DMA
    return pl.pallas_call(
        functools.partial(kernel, pool_count, tp_count),
        out_shape=(
            jax.ShapeDtypeStruct((SUFFIX, heads * VALUE_DIM), bf16),
            jax.ShapeDtypeStruct(pool.shape, bf16),
        ),
        in_specs=[smem] * 4 + [vmem] * 2 + [anywhere] * 5,
        out_specs=(anywhere, anywhere),
        scratch_shapes=[
            pltpu.VMEM(tokens.shape, bf16),
            pltpu.VMEM(down_weight.shape[::-1], bf16),
            pltpu.VMEM((heads, WIDTH, SUFFIX), bf16),
            pltpu.VMEM((rows, WIDE), bf16),
            pltpu.VMEM(value_weight.shape, bf16),
            pltpu.VMEM(pool.shape, bf16),
            pltpu.VMEM((2, pool_count, piece, WIDTH), bf16),
            pltpu.VMEM((pool_count, piece, WIDTH), bf16),
            pltpu.VMEM((pool_count, piece, WIDTH), bf16),
            pltpu.VMEM((tp_count, 2 * piece, WIDTH), f32),
            pltpu.VMEM((tp_count - 1, 2 * piece, WIDTH), f32),
            pltpu.VMEM((2 * pool_count, piece, WIDTH), bf16),
            pltpu.VMEM((4, 2 * HALF, WIDE), bf16),
            pltpu.VMEM((2, WIDE, 2 * HALF), bf16),
            pltpu.VMEM((8, SUFFIX, 128), f32),
            pltpu.VMEM((ROWS, 2 * HALF), f32),
            pltpu.VMEM((ROWS, 2 * HALF), f32),
            pltpu.VMEM((ROWS, 2 * HALF), bf16),
            pltpu.VMEM((ROWS, 2 * HALF), bf16),
            pltpu.VMEM((ROWS, 128), f32),
            pltpu.VMEM((ROWS, 128), f32),
            pltpu.VMEM((rows, LATENT), f32),
            pltpu.VMEM((rows, 128), f32),
            pltpu.VMEM((rows, 128), f32),
            pltpu.VMEM((SUFFIX, heads * VALUE_DIM), bf16),
            pltpu.VMEM(pool.shape, bf16),
            pltpu.VMEM((8, 128), jnp.int32),
            pltpu.SMEM((8, 128), jnp.int32),
            pltpu.SMEM((pool_count,), jnp.int32),
            dma((5,)),
            dma,
            dma((2,)),
            dma((2,)),
            dma((tp_count - 1,)),
            dma((tp_count - 1,)),
            dma((7,)),
            dma((7,)),
            dma((2, 2, 2)),
            dma((2, 2, 2)),
            dma((2, 2)),
            dma((2, 2)),
        ],
        compiler_params=pltpu.CompilerParams(
            collective_id=0, has_side_effects=True, vmem_limit_bytes=60 * 1024 * 1024
        ),
        name="latent_attention",
    )(
        block_holder,
        block_slot,
        prefix_blocks,
        suffix_len,
        kv_gain.reshape(1, LATENT),
        jnp.asarray(frequency),
        tokens,
        down_weight.T,
        queries.transpose(1, 2, 0),
        value_weight,
        pool,
    )


def solution(mesh):
    in_specs = (
        P("pool", "tp"),
        P("tp", None),
        P(),
        P("pool", "tp", None),
        P("tp", None, None),
        P("pool", "tp", None),
        P(),
        P(),
        P(),
        P(),
    )
    out_specs = (P("pool", "tp"), P("pool", "tp", None))
    return jax.shard_map(
        functools.partial(on_device, mesh.shape["pool"], mesh.shape["tp"]),
        mesh=mesh,
        in_specs=in_specs,
        out_specs=out_specs,
        check_vma=False,
    )
```
